512 devices in a mesh: sect: 4 (over z_hi), tok: 4 (over z_lo), vocab: 32 (over y, x, core).
Axes of the slice: x: 4, y: 4, z: 16 (z_hi: 4, z_lo: 4; z = z_hi * 4 + z_lo), core: 2. Of those that a mesh axis runs over, the one named last changes fastest.
Arguments:
- hidden: bfloat16 [2048, 4096], P('sect', ('tok', 'vocab')), may hold values from -256 to 256
- head_weight: bfloat16 [4096, 65536], P('tok', 'vocab'), may hold values from -1 to 1
- teacher_logits: bfloat16 [2048, 65536], P(('sect', 'tok', 'vocab')), may hold values from -16 to 390
- pairing: int32 [4, 4], replicated, may hold values from 0 to 3, as said below
Outputs:
- grad_hidden: float32 [2048, 4096], P('sect', ('tok', 'vocab'))
- divergence: float32 [2048], P(('sect', 'tok'))
The draws below stay inside these ranges and needn't reach their ends.
Inputs may be any that keep to these rules, and one draw needn't show every extreme that they name: `pairing`: every row is a permutation of the sections.
All inputs are finite; a program needn't handle non-finite values.
Results may differ from the reference program's by a relative error of at most 0.0027.
Values may be sent and summed in bfloat16 or wider, within the bound.
No kernel may reach another device: no remote copies, remote signals or barrier semaphores. Data moves between devices by JAX's collectives and lax.ppermute only.
A program may use at most 64 MiB of HBM per device.

```python
import math
import jax
import jax.numpy as jnp
from jax import lax

D = 4096
TOK_DEV = 128
VOCAB = 65536
TOKENS = 2048
N_SECT = 4
N_TOK = 4
N_VOCAB = 32


def column_block(key, index):
    return jnp.clip(jax.random.normal(jax.random.fold_in(key, index), (D, 16), jnp.float32), -7.0, 7.0)


def draw_head_weight(key, part):
    blocks = jax.vmap(lambda index: column_block(key, index))(jnp.arange(VOCAB // 16))
    key = jax.random.fold_in(key, 5)
    return (blocks.transpose(1, 0, 2).reshape(D, VOCAB) / math.sqrt(D)).astype(jnp.bfloat16)


def draw_hidden(key, part):
    key = jax.random.fold_in(key, 7)
    key_vals = jax.random.fold_in(key, 0)
    values = jnp.clip(jax.random.normal(key_vals, (TOKENS, D), jnp.float32), -5.0, 5.0) * 3.0
    return values.astype(jnp.bfloat16)


def draw_teacher_logits(key, part):
    key = jax.random.fold_in(key, 13)
    key_vals = jax.random.fold_in(key, 0)
    values = jnp.clip(jax.random.normal(key_vals, (TOKENS, VOCAB), jnp.float32), -5.0, 5.0) * 3.0
    return values.astype(jnp.bfloat16)


def draw_pairing(key, part):
    key = jax.random.fold_in(key, 17)
    scores = jax.random.randint(key, (N_SECT, N_SECT), 0, 65536) * N_SECT + jnp.arange(N_SECT, dtype=jnp.int32)[None, :]
    return jnp.argsort(scores, axis=1, stable=True).astype(jnp.int32)


def setup_inputs(seed: int = 0) -> dict:
    arg_keys = jax.random.split(jax.random.key(seed), 5)
    hidden = draw_hidden(jax.random.fold_in(arg_keys[4], 71), 0)
    head_weight = draw_head_weight(jax.random.fold_in(arg_keys[4], 71), 0)
    teacher_logits = draw_teacher_logits(jax.random.fold_in(arg_keys[4], 71), 0)
    pairing = draw_pairing(jax.random.fold_in(arg_keys[4], 71), 0)
    return dict(hidden=hidden, head_weight=head_weight, teacher_logits=teacher_logits, pairing=pairing)


loss_scale = 16.0


def student_order(teacher_logits, pairing):
    piece_rows = TOK_DEV // (N_VOCAB * N_SECT)
    table = teacher_logits.reshape(N_SECT, N_TOK, N_VOCAB, N_SECT, piece_rows, VOCAB)
    inverse = jnp.argsort(pairing, axis=1).astype(jnp.int32)
    picked = jnp.stack([jnp.take(table[section], inverse[section], axis=2) for section in range(N_SECT)])
    return picked.transpose(3, 1, 0, 4, 2, 5).reshape(TOKENS, VOCAB)


def distill_rows(hidden_rows, teacher_rows, head_weight):
    logits = jnp.dot(hidden_rows, head_weight, preferred_element_type=jnp.float32)
    teacher_vals = teacher_rows.astype(jnp.float32)
    top_student = jnp.max(logits, axis=1, keepdims=True)
    exp_student = jnp.exp(logits - top_student)
    total_student = jnp.sum(exp_student, axis=1, keepdims=True)
    top_teacher = jnp.max(teacher_vals, axis=1, keepdims=True)
    exp_teacher = jnp.exp(teacher_vals - top_teacher)
    total_teacher = jnp.sum(exp_teacher, axis=1, keepdims=True)
    cross = jnp.sum(exp_teacher * (teacher_vals - logits), axis=1, keepdims=True)
    diverge = cross / total_teacher - top_teacher - jnp.log(total_teacher) + top_student + jnp.log(total_student)
    grad_logits = (loss_scale * (exp_student / total_student - exp_teacher / total_teacher)).astype(jnp.bfloat16)
    grad_rows = lax.dot_general(grad_logits, head_weight, (((1,), (1,)), ((), ())), preferred_element_type=jnp.float32)
    return grad_rows, diverge[:, 0]


def reference(hidden, head_weight, teacher_logits, pairing):
    aligned = student_order(teacher_logits, pairing)
    block_count = N_SECT * N_TOK
    hidden_blocks = hidden.reshape(block_count, TOK_DEV, D)
    teacher_blocks = aligned.reshape(block_count, TOK_DEV, VOCAB)
    grads, diverge = lax.map(lambda both: distill_rows(both[0], both[1], head_weight), (hidden_blocks, teacher_blocks))
    return grads.reshape(TOKENS, D), diverge.reshape(TOKENS)
```

```python
import jax
import jax.numpy as jnp
from jax import lax
from jax.sharding import PartitionSpec as P

loss_scale = 16.0


def along_z(value, steps, planes):
    return lax.ppermute(
        value, ("sect", "tok"), [(i, (i + steps) % planes) for i in range(planes)]
    )


def along_sect(value, steps, sections):
    return lax.ppermute(value, "sect", [(i, (i + steps) % sections) for i in range(sections)])


def edge_offset(token_section, sections):
    return jnp.where(token_section < sections // 2, -2, 2)


def window_offsets(token_section, sections):
    return [edge_offset(token_section, sections), -1, 0, 1]


def row_block(plane, sections, toks):
    plane = (plane + sections * toks) % (sections * toks)
    return (plane % toks) * sections + plane // toks


def shards(hidden, head_weight, teacher_logits, pairing):
    sections = lax.axis_size("sect")
    toks = lax.axis_size("tok")
    vocabs = lax.axis_size("vocab")
    planes = sections * toks
    width = head_weight.shape[1]
    feats = hidden.shape[1]
    rows = hidden.shape[0]
    unit = rows // planes
    own = sections * unit
    half = own // 2
    section = lax.axis_index("sect")
    tok = lax.axis_index("tok")

    blocks = []
    for k in range(sections):
        plane = ((section + k) % sections) * toks + tok
        blocks += [row_block(plane + off, sections, toks) for off in window_offsets(section, sections)]
    source = jnp.repeat(jnp.stack(blocks), unit) * unit + jnp.tile(
        jnp.arange(unit, dtype=jnp.int32), sections * 4
    )
    pick = (jnp.arange(rows, dtype=jnp.int32)[:, None] == source[None, :]).astype(jnp.bfloat16)
    picked = lax.dot_general(
        hidden, pick, (((0,), (0,)), ((), ())), preferred_element_type=jnp.float32
    ).astype(jnp.bfloat16)
    parts = picked.reshape(feats, sections, own)
    arrived = [parts[:, 0]] + [along_sect(parts[:, k], k, sections) for k in range(1, sections)]
    by_section = jnp.zeros((sections, feats, 4, unit), jnp.bfloat16)
    for k in range(sections):
        by_section = lax.dynamic_update_slice(
            by_section,
            arrived[k].reshape(1, feats, 4, unit),
            ((section - k + sections) % sections, 0, 0, 0),
        )
    by_section = by_section.transpose(1, 2, 0, 3)
    edges = by_section[:, 0].reshape(feats, own)
    window = jnp.concatenate(
        [edges[:, :half], by_section[:, 1:].reshape(feats, 3 * own), edges[:, half:]], axis=1
    )
    spread = lax.all_to_all(
        jnp.broadcast_to(window[None], (vocabs, feats, rows)),
        "vocab",
        split_axis=0,
        concat_axis=0,
        tiled=True,
    ).reshape(vocabs * feats, rows)

    partial = lax.dot_general(
        spread, head_weight, (((0,), (0,)), ((), ())), preferred_element_type=jnp.float32
    )
    below = half
    mine = below + own
    above = mine + own
    last = above + own
    far_down = along_z(partial[:below], -1, planes)
    far_up = along_z(partial[last:], 1, planes)
    down_b = along_z(partial[below + half : mine], -1, planes)
    up_a = along_z(partial[above : above + half], 1, planes)
    down_a = along_z(partial[below : below + half] + far_down, -1, planes)
    up_b = along_z(partial[above + half : last] + far_up, 1, planes)
    logits = (
        partial[mine:above]
        + jnp.concatenate([down_a, down_b], axis=0)
        + jnp.concatenate([up_a, up_b], axis=0)
    )

    pairs_row = lax.dynamic_slice_in_dim(pairing, section, 1, 0)[0]
    select = (pairs_row[None, :] == jnp.arange(sections, dtype=jnp.int32)[:, None]).astype(
        jnp.bfloat16
    )
    ordered = jnp.dot(select, teacher_logits, preferred_element_type=jnp.float32).astype(
        jnp.bfloat16
    )
    teacher = lax.all_to_all(
        ordered.reshape(sections, vocabs, width).transpose(1, 0, 2),
        "vocab",
        split_axis=0,
        concat_axis=0,
        tiled=True,
    )
    teacher = teacher.transpose(1, 0, 2).reshape(own, width).astype(jnp.float32)

    top_s = jnp.max(logits, axis=1)
    top_t = jnp.max(teacher, axis=1)
    exp_t = jnp.exp(teacher - top_t[:, None])
    sum_s = jnp.sum(jnp.exp(logits - top_s[:, None]), axis=1)
    sum_t = jnp.sum(exp_t, axis=1)
    cross = jnp.sum(exp_t * (teacher - logits), axis=1)
    zero = jnp.zeros_like(cross)
    stats = jnp.stack([top_s, top_t, sum_s, sum_t, cross, zero, zero, zero])
    stats = lax.all_to_all(
        jnp.broadcast_to(stats[None], (vocabs,) + stats.shape),
        "vocab",
        split_axis=0,
        concat_axis=0,
        tiled=True,
    )
    top_student = jnp.max(stats[:, 0], axis=0)
    top_teacher = jnp.max(stats[:, 1], axis=0)
    scale_s = jnp.exp(stats[:, 0] - top_student[None])
    scale_t = jnp.exp(stats[:, 1] - top_teacher[None])
    total_student = jnp.sum(stats[:, 2] * scale_s, axis=0)
    total_teacher = jnp.sum(stats[:, 3] * scale_t, axis=0)
    cross = jnp.sum(stats[:, 4] * scale_t, axis=0)
    diverge = (
        cross / total_teacher
        - top_teacher
        - jnp.log(total_teacher)
        + top_student
        + jnp.log(total_student)
    )
    grad_logits = (
        loss_scale
        * (
            jnp.exp(logits - top_student[:, None]) / total_student[:, None]
            - jnp.exp(teacher - top_teacher[:, None]) / total_teacher[:, None]
        )
    ).astype(jnp.bfloat16)

    near_below = along_z(grad_logits, 1, planes)
    near_above = along_z(grad_logits, -1, planes)
    far_below = along_z(grad_logits[:half], 2, planes)
    far_above = along_z(grad_logits[half:], -2, planes)
    window_grad = jnp.concatenate(
        [far_below, near_below, grad_logits, near_above, far_above], axis=0
    )
    own_grad = lax.dot_general(
        head_weight, window_grad, (((1,), (1,)), ((), ())), preferred_element_type=jnp.float32
    )
    summed = jnp.sum(
        lax.all_to_all(
            own_grad.reshape(vocabs, feats, rows),
            "vocab",
            split_axis=0,
            concat_axis=0,
            tiled=True,
        ),
        axis=0,
    )

    edges = jnp.concatenate([summed[:, :below], summed[:, last:]], axis=1)
    returned = jnp.concatenate([edges, summed[:, below:last]], axis=1)
    returned = returned.reshape(feats, 4, sections, unit).transpose(2, 0, 1, 3)
    returned = returned.reshape(sections, feats, own)
    extra = jnp.pad(diverge.reshape(sections, 1, unit), ((0, 0), (0, 7), (0, own - unit)))
    returned = jnp.concatenate([returned, extra], axis=1)
    got = []
    for k in range(sections):
        piece = lax.dynamic_index_in_dim(returned, (section + k) % sections, 0, keepdims=False)
        got.append(piece if k == 0 else along_sect(piece, k, sections))
    grads = jnp.zeros((planes, unit, feats), jnp.float32)
    div = jnp.zeros((sections, unit), jnp.float32)
    for k in range(sections):
        sender = (section - k + sections) % sections
        piece = got[k][:feats].reshape(feats, 4, unit).transpose(1, 2, 0)
        for place, off in enumerate(window_offsets(section, sections)):
            grads = lax.dynamic_update_slice(
                grads,
                piece[place : place + 1],
                (row_block(sender * toks + tok + off, sections, toks), 0, 0),
            )
        div = lax.dynamic_update_slice(div, got[k][feats : feats + 1, :unit], (sender, 0))
    return grads.reshape(rows, feats), div.reshape(own)


def solution(mesh):
    placed = (
        P("sect", ("tok", "vocab")),
        P("tok", "vocab"),
        P(("sect", "tok", "vocab"), None),
        P(),
    )
    return jax.shard_map(
        shards,
        mesh=mesh,
        in_specs=placed,
        out_specs=(P("sect", ("tok", "vocab")), P(("sect", "tok"))),
        check_vma=False,
    )
```

```python
import functools

import jax
import jax.numpy as jnp
from jax import lax
from jax.experimental import pallas as pl
from jax.experimental.pallas import tpu as pltpu
from jax.sharding import PartitionSpec as P

loss_scale = 16.0
VMEM_BYTES = 40 * 1024 * 1024


def along_z(value, steps, planes):
    return lax.ppermute(
        value, ("sect", "tok"), [(i, (i + steps) % planes) for i in range(planes)]
    )


def across_vocab(value):
    return lax.all_to_all(value, "vocab", split_axis=0, concat_axis=0, tiled=True)


def window_offsets(token_section, sections):
    return [jnp.where(token_section < sections // 2, -2, 2), -1, 0, 1]


def row_block(plane, sections, toks):
    plane = lax.rem(plane + sections * toks, sections * toks)
    return lax.rem(plane, toks) * sections + lax.div(plane, toks)


def params(**more):
    return pltpu.CompilerParams(vmem_limit_bytes=VMEM_BYTES, **more)


def logits_kernel(first, x_ref, w_ref, *refs):
    *outs, flipped = refs

    @pl.when(pl.program_id(0) == 0)
    def _():
        flipped[...] = x_ref[:, first:].T

    result = jnp.dot(flipped[...], w_ref[...], preferred_element_type=jnp.float32)
    start = 0
    for out in outs:
        out[...] = result[start : start + out.shape[0]]
        start += out.shape[0]


def partial_logits(spread, head_weight, first, last, sizes):
    feats, width = head_weight.shape
    tile = 512
    count = last - first
    return pl.pallas_call(
        functools.partial(logits_kernel, first),
        grid=(width // tile,),
        in_specs=[
            pl.BlockSpec((feats, last), lambda i: (0, 0)),
            pl.BlockSpec((feats, tile), lambda i: (0, i)),
        ],
        out_specs=[pl.BlockSpec((size, tile), lambda i: (0, i)) for size in sizes],
        out_shape=[jax.ShapeDtypeStruct((size, width), jnp.float32) for size in sizes],
        scratch_shapes=[pltpu.VMEM((count, feats), jnp.bfloat16)],
        compiler_params=params(),
        cost_estimate=pl.CostEstimate(
            flops=2 * count * feats * width,
            bytes_accessed=feats * width * 2 + count * width * 4,
            transcendentals=0,
        ),
    )(spread, head_weight)


def stats_kernel(own_ref, lo_a, lo_b, hi_a, hi_b, teacher_ref, logits_ref, stats_ref):
    half = lo_a.shape[0]
    logits_ref[:half] = own_ref[:half] + lo_a[...] + lo_b[...]
    logits_ref[half:] = own_ref[half:] + hi_a[...] + hi_b[...]
    logits = logits_ref[...]
    teacher = teacher_ref[...].astype(jnp.float32)
    top_s = jnp.max(logits, axis=1, keepdims=True)
    top_t = jnp.max(teacher, axis=1, keepdims=True)
    sum_s = jnp.sum(jnp.exp(logits - top_s), axis=1, keepdims=True)
    exp_t = jnp.exp(teacher - top_t)
    sum_t = jnp.sum(exp_t, axis=1, keepdims=True)
    cross = jnp.sum(exp_t * (teacher - logits), axis=1, keepdims=True)
    own = logits.shape[0]
    lane = lax.broadcasted_iota(jnp.int32, (own, 128), 1)
    packed = jnp.zeros((own, 128), jnp.float32)
    for place, column in enumerate((top_s, top_t, sum_s, sum_t, cross)):
        packed = jnp.where(lane == place, column, packed)
    rows = packed.T[:8]
    for k in range(stats_ref.shape[0]):
        stats_ref[k] = rows


def grads_kernel(logits_ref, teacher_ref, stats_ref, grad_ref, low_ref, high_ref, div_ref):
    stats = stats_ref[...]
    top = jnp.max(stats, axis=0)
    scale = jnp.exp(stats[:, :2] - top[None, :2])
    top_s, top_t = top[0:1], top[1:2]
    total_s = jnp.sum(stats[:, 2] * scale[:, 0], axis=0, keepdims=True)
    total_t = jnp.sum(stats[:, 3] * scale[:, 1], axis=0, keepdims=True)
    cross = jnp.sum(stats[:, 4] * scale[:, 1], axis=0, keepdims=True)
    div_ref[...] = cross / total_t - top_t - jnp.log(total_t) + top_s + jnp.log(total_s)
    own = logits_ref.shape[0]
    row = lax.broadcasted_iota(jnp.int32, (128, own), 0)
    packed = jnp.zeros((128, own), jnp.float32)
    for place, values in enumerate((top_s, top_t, loss_scale / total_s, loss_scale / total_t)):
        packed = jnp.where(row == place, values, packed)
    columns = packed.T
    grad = (
        jnp.exp(logits_ref[...] - columns[:, 0:1]) * columns[:, 2:3]
        - jnp.exp(teacher_ref[...].astype(jnp.float32) - columns[:, 1:2]) * columns[:, 3:4]
    ).astype(jnp.bfloat16)
    grad_ref[...] = grad
    low_ref[...] = grad[: own // 2]
    high_ref[...] = grad[own // 2 :]


def hidden_kernel(w_ref, near_below, near_above, far_below, far_above, own_ref, out_ref, window):
    half = far_below.shape[0]

    @pl.when(pl.program_id(0) == 0)
    def _():
        window[:half] = far_below[...]
        window[half : 2 * half] = far_above[...]
        window[2 * half : 3 * half] = near_below[half:]
        window[3 * half : 4 * half] = near_above[:half]
        window[4 * half : 5 * half] = near_below[:half]
        window[5 * half : 6 * half] = near_above[half:]
        window[6 * half :] = own_ref[...]

    out_ref[...] = lax.dot_general(
        w_ref[...], window[...], (((1,), (1,)), ((), ())), preferred_element_type=jnp.float32
    )


def hidden_grads(head_weight, pieces):
    feats, width = head_weight.shape
    rows = sum(piece.shape[0] for piece in pieces)
    tile = 256
    return pl.pallas_call(
        hidden_kernel,
        grid=(feats // tile,),
        in_specs=[pl.BlockSpec((tile, width), lambda i: (i, 0))]
        + [pl.BlockSpec(piece.shape, lambda i: (0, 0)) for piece in pieces],
        out_specs=pl.BlockSpec((tile, rows), lambda i: (i, 0)),
        out_shape=jax.ShapeDtypeStruct((feats, rows), jnp.float32),
        scratch_shapes=[pltpu.VMEM((rows, width), jnp.bfloat16)],
        compiler_params=params(),
        cost_estimate=pl.CostEstimate(
            flops=2 * rows * feats * width,
            bytes_accessed=feats * width * 2 + rows * width * 2 + rows * feats * 4,
            transcendentals=0,
        ),
    )(head_weight, *pieces)


def shards(hidden, head_weight, teacher_logits, pairing):
    sections = lax.axis_size("sect")
    toks = lax.axis_size("tok")
    vocabs = lax.axis_size("vocab")
    planes = sections * toks
    width = head_weight.shape[1]
    feats = hidden.shape[1]
    rows = hidden.shape[0]
    unit = rows // planes
    own = sections * unit
    half = own // 2
    section = lax.axis_index("sect")
    tok = lax.axis_index("tok")

    blocks = []
    for k in range(sections):
        plane = k * toks + tok
        blocks += [row_block(plane + off, sections, toks) for off in window_offsets(section, sections)]
    source = jnp.repeat(jnp.stack(blocks), unit) * unit + jnp.tile(
        jnp.arange(unit, dtype=jnp.int32), sections * 4
    )
    pick = (jnp.arange(rows, dtype=jnp.int32)[:, None] == source[None, :]).astype(jnp.bfloat16)
    picked = lax.dot_general(
        hidden, pick, (((0,), (0,)), ((), ())), preferred_element_type=jnp.float32
    ).astype(jnp.bfloat16)
    by_section = lax.all_to_all(
        picked.reshape(feats, sections, own).transpose(1, 0, 2),
        "sect",
        split_axis=0,
        concat_axis=0,
        tiled=True,
    ).reshape(sections, feats, 4, unit)
    by_section = by_section.transpose(1, 2, 0, 3).reshape(feats, 4, own)
    edges, below, mine, above = (by_section[:, place] for place in range(4))
    window = jnp.concatenate(
        [edges, below[:, half:], above[:, :half], below[:, :half], above[:, half:], mine], axis=1
    )
    spread = across_vocab(jnp.broadcast_to(window[None], (vocabs, feats, rows)))
    spread = spread.reshape(vocabs * feats, rows)

    edge_down, edge_up = partial_logits(spread, head_weight, 0, own, [half, half])
    far_down = along_z(edge_down, -1, planes)
    far_up = along_z(edge_up, 1, planes)
    near_down, near_up, next_down, next_up, kept = partial_logits(
        spread, head_weight, own, rows, [half, half, half, half, own]
    )
    down_b = along_z(near_down, -1, planes)
    up_a = along_z(near_up, 1, planes)
    next_down, next_up = lax.optimization_barrier((next_down + far_down, next_up + far_up))
    down_a = along_z(next_down, -1, planes)
    up_b = along_z(next_up, 1, planes)

    pairs_row = lax.dynamic_slice_in_dim(pairing, section, 1, 0)[0]
    select = (pairs_row[None, :] == jnp.arange(sections, dtype=jnp.int32)[:, None]).astype(
        jnp.bfloat16
    )
    ordered = jnp.dot(select, teacher_logits, preferred_element_type=jnp.float32).astype(
        jnp.bfloat16
    )
    ordered = ordered.reshape(sections, vocabs, width).transpose(1, 0, 2)
    ordered, kept = lax.optimization_barrier((ordered, kept))
    teacher = across_vocab(ordered).transpose(1, 0, 2).reshape(own, width)

    logits, stats = pl.pallas_call(
        stats_kernel,
        out_shape=[
            jax.ShapeDtypeStruct((own, width), jnp.float32),
            jax.ShapeDtypeStruct((vocabs, 8, own), jnp.float32),
        ],
        compiler_params=params(),
    )(kept, down_a, up_a, down_b, up_b, teacher)
    stats = across_vocab(stats)
    grad_logits, low, high, diverge = pl.pallas_call(
        grads_kernel,
        out_shape=[
            jax.ShapeDtypeStruct((own, width), jnp.bfloat16),
            jax.ShapeDtypeStruct((half, width), jnp.bfloat16),
            jax.ShapeDtypeStruct((half, width), jnp.bfloat16),
            jax.ShapeDtypeStruct((1, own), jnp.float32),
        ],
        compiler_params=params(),
    )(logits, teacher, stats)

    near_below = along_z(grad_logits, 1, planes)
    near_above = along_z(grad_logits, -1, planes)
    far_below = along_z(low, 2, planes)
    far_above = along_z(high, -2, planes)
    own_grad = hidden_grads(
        head_weight, [near_below, near_above, far_below, far_above, grad_logits]
    )
    summed = jnp.sum(across_vocab(own_grad.reshape(vocabs, feats, rows)), axis=0)

    pieces = [summed[:, place * half : (place + 1) * half] for place in range(8)]
    returned = jnp.concatenate(
        pieces[:2] + [pieces[4], pieces[2], pieces[6], pieces[7], pieces[3], pieces[5]], axis=1
    )
    returned = returned.reshape(feats, 4, sections, unit).transpose(2, 0, 1, 3)
    returned = returned.reshape(sections, feats, own)
    extra = jnp.pad(diverge.reshape(sections, 1, unit), ((0, 0), (0, 7), (0, own - unit)))
    got = lax.all_to_all(
        jnp.concatenate([returned, extra], axis=1), "sect", split_axis=0, concat_axis=0, tiled=True
    )
    places = got[:, :feats].reshape(sections, feats, 4, unit).transpose(0, 2, 3, 1)
    grads = jnp.zeros((planes, unit, feats), jnp.float32)
    for sender in range(sections):
        for place, off in enumerate(window_offsets(section, sections)):
            grads = lax.dynamic_update_slice(
                grads,
                places[sender, place][None],
                (row_block(sender * toks + tok + off, sections, toks), 0, 0),
            )
    return grads.reshape(rows, feats), got[:, feats, :unit].reshape(own)


def solution(mesh):
    placed = (
        P("sect", ("tok", "vocab")),
        P("tok", "vocab"),
        P(("sect", "tok", "vocab"), None),
        P(),
    )
    return jax.shard_map(
        shards,
        mesh=mesh,
        in_specs=placed,
        out_specs=(P("sect", ("tok", "vocab")), P(("sect", "tok"))),
        check_vma=False,
    )
```

```python
import functools

import jax
import jax.numpy as jnp
from jax import lax
from jax.experimental import pallas as pl
from jax.experimental.pallas import tpu as pltpu
from jax.sharding import PartitionSpec as P

loss_scale = 16.0
VMEM_BYTES = 24 * 1024 * 1024
SMEM = pl.BlockSpec(memory_space=pltpu.SMEM)
VMEM = pl.BlockSpec(memory_space=pltpu.VMEM)


def along_z(value, steps, planes):
    return lax.ppermute(
        value, ("sect", "tok"), [(i, (i + steps) % planes) for i in range(planes)]
    )


def exchange(value, axis, **groups):
    return lax.all_to_all(value, axis, split_axis=0, concat_axis=0, tiled=True, **groups)


def params():
    return pltpu.CompilerParams(vmem_limit_bytes=VMEM_BYTES)


def cost(flops, bytes_accessed):
    return pl.CostEstimate(flops=flops, bytes_accessed=bytes_accessed, transcendentals=0)


def window_block(section, tok, token_section, piece, sections, toks):
    planes = sections * toks
    near = jnp.int32(piece - 2)
    far = jnp.where(token_section < sections // 2, -2, 2)
    plane = lax.rem(section * toks + tok + (far if piece == 0 else near) + planes, planes)
    return lax.rem(plane, toks) * sections + lax.div(plane, toks)


def window_order(sections):
    low = list(range(sections // 2))
    high = list(range(sections // 2, sections))
    order = [(0, s) for s in low + high]
    order += [(1, s) for s in high] + [(3, s) for s in low]
    order += [(1, s) for s in low] + [(3, s) for s in high]
    return order + [(2, s) for s in low + high]


def pick_kernel(place_ref, hidden_ref, picked_ref, *, toks):
    sections, _, own = picked_ref.shape
    rows = hidden_ref.shape[1]
    unit = own // 4
    section, tok = place_ref[0], place_ref[1]
    lane = lax.broadcasted_iota(jnp.int32, (rows, own), 1)
    row = lax.broadcasted_iota(jnp.int32, (rows, own), 0)
    for k in range(sections):
        source = lane
        for piece in range(4):
            block = window_block(jnp.int32(k), tok, section, piece, sections, toks)
            source = jnp.where(
                (lane >= piece * unit) & (lane < (piece + 1) * unit),
                (block - piece) * unit + lane,
                source,
            )
        pick = jnp.where(row == source, 1.0, 0.0).astype(jnp.bfloat16)
        picked_ref[k] = jnp.dot(
            hidden_ref[...], pick, preferred_element_type=jnp.float32
        ).astype(jnp.bfloat16)


def arrange_kernel(got_ref, spread_ref):
    sections, _, own = got_ref.shape
    rows = spread_ref.shape[2]
    unit = own // 4
    lane = lax.broadcasted_iota(jnp.int32, (own, rows), 1)
    row = lax.broadcasted_iota(jnp.int32, (own, rows), 0)
    total = None
    for s in range(sections):
        source = jnp.full((own, rows), -1, jnp.int32)
        for place, (piece, token_section) in enumerate(window_order(sections)):
            if token_section == s:
                source = jnp.where(
                    (lane >= place * unit) & (lane < (place + 1) * unit),
                    lane + (piece - place) * unit,
                    source,
                )
        move = jnp.where(row == source, 1.0, 0.0).astype(jnp.bfloat16)
        part = jnp.dot(got_ref[s], move, preferred_element_type=jnp.float32)
        total = part if total is None else total + part
    window = total.astype(jnp.bfloat16)
    for k in range(spread_ref.shape[0]):
        spread_ref[k] = window


def logits_kernel(first, x_ref, w_ref, *refs):
    *outs, flipped = refs

    @pl.when(pl.program_id(0) == 0)
    def _():
        flipped[...] = x_ref[:, first:].T

    result = jnp.dot(flipped[...], w_ref[...], preferred_element_type=jnp.float32)
    start = 0
    for out in outs:
        out[...] = result[start : start + out.shape[0]]
        start += out.shape[0]


def partial_logits(spread, head_weight, first, sizes):
    feats, width = head_weight.shape
    tile = 512
    count = sum(sizes)
    return pl.pallas_call(
        functools.partial(logits_kernel, first),
        grid=(width // tile,),
        in_specs=[
            pl.BlockSpec((feats, first + count), lambda i: (0, 0)),
            pl.BlockSpec((feats, tile), lambda i: (0, i)),
        ],
        out_specs=[pl.BlockSpec((size, tile), lambda i: (0, i)) for size in sizes],
        out_shape=[jax.ShapeDtypeStruct((size, width), jnp.float32) for size in sizes],
        scratch_shapes=[pltpu.VMEM((count, feats), jnp.bfloat16)],
        compiler_params=params(),
        cost_estimate=cost(
            2 * count * feats * width, feats * width * 2 + count * (feats * 2 + width * 4)
        ),
    )(spread, head_weight)


def order_kernel(place_ref, pairing_ref, teacher_ref, after_ref, ordered_ref):
    vocabs, sections, width = ordered_ref.shape
    section = place_ref[0]
    paired = [pairing_ref[section, k] for k in range(sections)]
    for v in range(vocabs):
        rows = teacher_ref[:, v * width : (v + 1) * width].astype(jnp.float32)
        row = lax.broadcasted_iota(jnp.int32, (sections, width), 0)
        out = jnp.zeros((sections, width), jnp.float32)
        for k in range(sections):
            out = jnp.where(row == paired[k], rows[k : k + 1], out)
        ordered_ref[v] = out.astype(jnp.bfloat16)


def add_kernel(down_ref, far_down_ref, up_ref, far_up_ref, down_out, up_out):
    down_out[...] = down_ref[...] + far_down_ref[...]
    up_out[...] = up_ref[...] + far_up_ref[...]


def stats_kernel(own_ref, lo_a, lo_b, hi_a, hi_b, teacher_ref, logits_ref, stats_ref):
    half = lo_a.shape[0]
    logits_ref[:half] = own_ref[:half] + lo_a[...] + lo_b[...]
    logits_ref[half:] = own_ref[half:] + hi_a[...] + hi_b[...]
    logits = logits_ref[...]
    teacher = teacher_ref[...].astype(jnp.float32)
    top_s = jnp.max(logits, axis=1, keepdims=True)
    top_t = jnp.max(teacher, axis=1, keepdims=True)
    sum_s = jnp.sum(jnp.exp(logits - top_s), axis=1, keepdims=True)
    exp_t = jnp.exp(teacher - top_t)
    sum_t = jnp.sum(exp_t, axis=1, keepdims=True)
    cross = jnp.sum(exp_t * (teacher - logits), axis=1, keepdims=True)
    own = logits.shape[0]
    lane = lax.broadcasted_iota(jnp.int32, (own, 128), 1)
    packed = jnp.zeros((own, 128), jnp.float32)
    for place, column in enumerate((top_s, top_t, sum_s, sum_t, cross)):
        packed = jnp.where(lane == place, column, packed)
    rows = packed.T[:8]
    for k in range(stats_ref.shape[0]):
        stats_ref[k] = rows


def grads_kernel(logits_ref, teacher_ref, stats_ref, low_ref, high_ref, div_ref):
    stats = stats_ref[...]
    top = jnp.max(stats, axis=0)
    scale = jnp.exp(stats[:, :2] - top[None, :2])
    top_s, top_t = top[0:1], top[1:2]
    total_s = jnp.sum(stats[:, 2] * scale[:, 0], axis=0, keepdims=True)
    total_t = jnp.sum(stats[:, 3] * scale[:, 1], axis=0, keepdims=True)
    cross = jnp.sum(stats[:, 4] * scale[:, 1], axis=0, keepdims=True)
    div_ref[...] = cross / total_t - top_t - jnp.log(total_t) + top_s + jnp.log(total_s)
    own = logits_ref.shape[0]
    half = own // 2
    row = lax.broadcasted_iota(jnp.int32, (128, own), 0)
    packed = jnp.zeros((128, own), jnp.float32)
    for place, values in enumerate((top_s, top_t, loss_scale / total_s, loss_scale / total_t)):
        packed = jnp.where(row == place, values, packed)
    columns = packed.T
    grad = (
        jnp.exp(logits_ref[...] - columns[:, 0:1]) * columns[:, 2:3]
        - jnp.exp(teacher_ref[...].astype(jnp.float32) - columns[:, 1:2]) * columns[:, 3:4]
    ).astype(jnp.bfloat16)
    low_ref[...] = grad[:half]
    high_ref[...] = grad[half:]


def hidden_kernel(place_ref, w_ref, *refs):
    *pieces, keep_ref, send_ref, window = refs

    @pl.when(pl.program_id(0) == 0)
    def _():
        start = 0
        for piece in pieces:
            window[start : start + piece.shape[0]] = piece[...]
            start += piece.shape[0]

    pairs, feats, rows = keep_ref.shape
    result = lax.dot_general(
        w_ref[...], window[...], (((1,), (1,)), ((), ())), preferred_element_type=jnp.float32
    ).reshape(pairs, 2, feats, rows)
    core = lax.rem(place_ref[2], 2)

    @pl.when(core == 0)
    def _():
        keep_ref[...] = result[:, 0]
        send_ref[...] = result[:, 1]

    @pl.when(core != 0)
    def _():
        keep_ref[...] = result[:, 1]
        send_ref[...] = result[:, 0]


def hidden_grads(place, head_weight, pieces, pairs):
    feats, width = head_weight.shape
    rows = sum(piece.shape[0] for piece in pieces)
    steps = 2
    shape = jax.ShapeDtypeStruct((pairs, feats // (2 * pairs), rows), jnp.float32)
    block = pl.BlockSpec((pairs // steps,) + shape.shape[1:], lambda i: (i, 0, 0))
    return pl.pallas_call(
        hidden_kernel,
        grid=(steps,),
        in_specs=[SMEM, pl.BlockSpec((feats // steps, width), lambda i: (i, 0))]
        + [pl.BlockSpec(piece.shape, lambda i: (0, 0)) for piece in pieces],
        out_specs=[block, block],
        out_shape=[shape, shape],
        scratch_shapes=[pltpu.VMEM((rows, width), jnp.bfloat16)],
        compiler_params=params(),
        cost_estimate=cost(
            2 * rows * feats * width, feats * width * 2 + rows * width * 2 + rows * feats * 4
        ),
    )(place, head_weight, *pieces)


def regroup_kernel(place_ref, parts_ref, div_ref, out_ref):
    sections, height, own = out_ref.shape
    _, feats, _ = parts_ref.shape
    unit = own // 4
    summed = jnp.sum(parts_ref[...], axis=0)
    lane = lax.broadcasted_iota(jnp.int32, (feats, own), 1)
    order = window_order(sections)
    for s in range(sections):
        out = jnp.zeros((feats, own), jnp.float32)
        for piece in range(4):
            start = order.index((piece, s)) * unit
            whole = start // own * own
            turned = pltpu.roll(
                summed[:, whole : whole + own], (piece * unit - start + whole) % own, 1
            )
            out = jnp.where((lane >= piece * unit) & (lane < (piece + 1) * unit), turned, out)
        out_ref[s, :feats] = out
    section = place_ref[0]
    values = jnp.broadcast_to(div_ref[...], (height - feats, own))
    small = lane[: height - feats]
    for s in range(sections):
        out = jnp.zeros_like(values)
        for mine in range(sections):
            turned = pltpu.roll(values, (mine - s) * unit % own, 1)
            inside = (small >= mine * unit) & (small < (mine + 1) * unit)
            out = jnp.where(inside & (section == mine), turned, out)
        out_ref[s, feats:] = out


def return_kernel(place_ref, got_ref, grads_ref, div_ref, ordered, *, toks):
    sections, _, own = got_ref.shape
    unit = own // 4
    feats = grads_ref.shape[0]
    for sender in range(sections):
        turned = got_ref[sender, :feats, :].T
        for piece in range(4):
            block = window_block(
                jnp.int32(sender), place_ref[1], place_ref[0], piece, sections, toks
            )
            ordered[pl.ds(pl.multiple_of(block * unit, unit), unit), :] = turned[
                piece * unit : (piece + 1) * unit
            ]
    grads_ref[...] = ordered[...].T
    div_ref[...] = jnp.sum(got_ref[:, feats : feats + 1, :], axis=0)


def shards(hidden, head_weight, teacher_logits, pairing):
    sections = lax.axis_size("sect")
    toks = lax.axis_size("tok")
    vocabs = lax.axis_size("vocab")
    planes = sections * toks
    width = head_weight.shape[1]
    rows, feats = hidden.shape
    own = rows // toks
    half = own // 2
    place = jnp.stack([lax.axis_index(name) for name in ("sect", "tok", "vocab")])

    picked = pl.pallas_call(
        functools.partial(pick_kernel, toks=toks),
        in_specs=[SMEM, VMEM],
        out_specs=VMEM,
        out_shape=jax.ShapeDtypeStruct((sections, feats, own), jnp.bfloat16),
        compiler_params=params(),
    )(place, hidden.T)
    spread = pl.pallas_call(
        arrange_kernel,
        in_specs=[VMEM],
        out_specs=VMEM,
        out_shape=jax.ShapeDtypeStruct((vocabs, feats, rows), jnp.bfloat16),
        compiler_params=params(),
        cost_estimate=cost(2 * feats * own * sections * rows, vocabs * feats * rows * 2),
    )(exchange(picked, "sect"))
    spread = exchange(spread, "vocab").reshape(vocabs * feats, rows)

    edge_down, edge_up = partial_logits(spread, head_weight, 0, [half, half])
    far_down = along_z(edge_down, -1, planes)
    far_up = along_z(edge_up, 1, planes)
    near_down, near_up, next_down, next_up, kept = partial_logits(
        spread, head_weight, own, [half, half, half, half, own]
    )
    down_b = along_z(near_down, -1, planes)
    up_a = along_z(near_up, 1, planes)
    next_down, next_up = pl.pallas_call(
        add_kernel,
        out_shape=[jax.ShapeDtypeStruct(next_down.shape, jnp.float32)] * 2,
        compiler_params=params(),
    )(next_down, far_down, next_up, far_up)
    down_a = along_z(next_down, -1, planes)
    up_b = along_z(next_up, 1, planes)

    ordered = pl.pallas_call(
        order_kernel,
        in_specs=[SMEM, SMEM, VMEM, pl.BlockSpec(memory_space=pl.ANY)],
        out_specs=VMEM,
        out_shape=jax.ShapeDtypeStruct((vocabs, sections, width), jnp.bfloat16),
        compiler_params=params(),
    )(place, pairing, teacher_logits, kept)
    teacher = exchange(ordered, "vocab").transpose(1, 0, 2).reshape(own, width)

    logits, stats = pl.pallas_call(
        stats_kernel,
        out_shape=[
            jax.ShapeDtypeStruct((own, width), jnp.float32),
            jax.ShapeDtypeStruct((vocabs, 8, own), jnp.float32),
        ],
        compiler_params=params(),
    )(kept, down_a, up_a, down_b, up_b, teacher)
    low, high, diverge = pl.pallas_call(
        grads_kernel,
        out_shape=[
            jax.ShapeDtypeStruct((half, width), jnp.bfloat16),
            jax.ShapeDtypeStruct((half, width), jnp.bfloat16),
            jax.ShapeDtypeStruct((1, own), jnp.float32),
        ],
        compiler_params=params(),
    )(logits, teacher, exchange(stats, "vocab"))

    below_low = along_z(low, 1, planes)
    above_high = along_z(high, -1, planes)
    below_high = along_z(high, 1, planes)
    above_low = along_z(low, -1, planes)
    far_below = along_z(below_low, 1, planes)
    far_above = along_z(above_high, -1, planes)
    keep, send = hidden_grads(
        place,
        head_weight,
        [far_below, far_above, below_high, above_low, below_low, above_high, low, high],
        vocabs // 2,
    )
    other = lax.ppermute(send, "vocab", [(i, i ^ 1) for i in range(vocabs)])
    groups = [list(range(core, vocabs, 2)) for core in range(2)]
    parts = exchange(keep + other, "vocab", axis_index_groups=groups)

    regrouped = pl.pallas_call(
        regroup_kernel,
        in_specs=[SMEM, VMEM, VMEM],
        out_specs=VMEM,
        out_shape=jax.ShapeDtypeStruct((sections, feats + 8, own), jnp.float32),
        compiler_params=params(),
    )(place, parts, diverge)
    grads, div = pl.pallas_call(
        functools.partial(return_kernel, toks=toks),
        in_specs=[SMEM, VMEM],
        out_specs=[VMEM, VMEM],
        out_shape=[
            jax.ShapeDtypeStruct((feats, rows), jnp.float32),
            jax.ShapeDtypeStruct((1, own), jnp.float32),
        ],
        scratch_shapes=[pltpu.VMEM((rows, feats), jnp.float32)],
        compiler_params=params(),
    )(place, exchange(regrouped, "sect"))
    return grads.T, div.reshape(own)


def solution(mesh):
    placed = (
        P("sect", ("tok", "vocab")),
        P("tok", "vocab"),
        P(("sect", "tok", "vocab"), None),
        P(),
    )
    return jax.shard_map(
        shards,
        mesh=mesh,
        in_specs=placed,
        out_specs=(P("sect", ("tok", "vocab")), P(("sect", "tok"))),
        check_vma=False,
    )
```

```python
import functools

import jax
import jax.numpy as jnp
from jax import lax
from jax.experimental import pallas as pl
from jax.experimental.pallas import tpu as pltpu
from jax.sharding import PartitionSpec as P

loss_scale = 16.0
VMEM_BYTES = 24 * 1024 * 1024
SMEM = pl.BlockSpec(memory_space=pltpu.SMEM)
VMEM = pl.BlockSpec(memory_space=pltpu.VMEM)
ANYWHERE = pl.BlockSpec(memory_space=pl.ANY)


def along_z(value, steps, planes):
    return lax.ppermute(
        value, ("sect", "tok"), [(i, (i + steps) % planes) for i in range(planes)]
    )


def exchange(value, axis, **groups):
    return lax.all_to_all(value, axis, split_axis=0, concat_axis=0, tiled=True, **groups)


def params():
    return pltpu.CompilerParams(vmem_limit_bytes=VMEM_BYTES)


def cost(flops, bytes_accessed):
    return pl.CostEstimate(flops=flops, bytes_accessed=bytes_accessed, transcendentals=0)


def remainder(value, count):
    return value & (count - 1) if count & (count - 1) == 0 else lax.rem(value, count)


def quotient(value, count):
    if count & (count - 1) == 0:
        return lax.shift_right_logical(value, jnp.int32(count.bit_length() - 1))
    return lax.div(value, count)


def window_block(section, tok, token_section, piece, sections, toks):
    planes = sections * toks
    near = jnp.int32(piece - 2)
    far = jnp.where(token_section < sections // 2, -2, 2)
    plane = remainder(section * toks + tok + (far if piece == 0 else near) + planes, planes)
    return remainder(plane, toks) * sections + quotient(plane, toks)


def window_order(sections):
    low = list(range(sections // 2))
    high = list(range(sections // 2, sections))
    order = [(0, s) for s in low + high]
    order += [(1, s) for s in high] + [(3, s) for s in low]
    order += [(1, s) for s in low] + [(3, s) for s in high]
    return order + [(2, s) for s in low + high]


def pick_kernel(place_ref, hidden_ref, picked_ref, *, toks):
    sections, _, own = picked_ref.shape
    rows = hidden_ref.shape[1]
    unit = own // 4
    section, tok = place_ref[0], place_ref[1]
    lane = lax.broadcasted_iota(jnp.int32, (rows, own), 1)
    row = lax.broadcasted_iota(jnp.int32, (rows, own), 0)
    for k in range(sections):
        source = lane
        for piece in range(4):
            block = window_block(jnp.int32(k), tok, section, piece, sections, toks)
            source = jnp.where(
                (lane >= piece * unit) & (lane < (piece + 1) * unit),
                (block - piece) * unit + lane,
                source,
            )
        pick = jnp.where(row == source, 1.0, 0.0).astype(jnp.bfloat16)
        picked_ref[k] = jnp.dot(
            hidden_ref[...], pick, preferred_element_type=jnp.float32
        ).astype(jnp.bfloat16)


def arrange_kernel(got_ref, spread_ref):
    sections, _, own = got_ref.shape
    rows = spread_ref.shape[2]
    unit = own // 4
    lane = lax.broadcasted_iota(jnp.int32, (own, rows), 1)
    row = lax.broadcasted_iota(jnp.int32, (own, rows), 0)
    total = None
    for s in range(sections):
        source = jnp.full((own, rows), -1, jnp.int32)
        for place, (piece, token_section) in enumerate(window_order(sections)):
            if token_section == s:
                source = jnp.where(
                    (lane >= place * unit) & (lane < (place + 1) * unit),
                    lane + (piece - place) * unit,
                    source,
                )
        move = jnp.where(row == source, 1.0, 0.0).astype(jnp.bfloat16)
        part = jnp.dot(got_ref[s], move, preferred_element_type=jnp.float32)
        total = part if total is None else total + part
    window = total.astype(jnp.bfloat16)
    for k in range(spread_ref.shape[0]):
        spread_ref[k] = window


def logits_kernel(first, place_ref, mine_ref, other_ref, w_ref, *refs):
    *outs, both, flipped = refs

    @pl.when(pl.program_id(0) == 0)
    def _():
        core = remainder(place_ref[2], 2)

        @pl.when(core == 0)
        def _():
            both[:, 0] = mine_ref[:, :, first:]
            both[:, 1] = other_ref[:, :, first:]

        @pl.when(core != 0)
        def _():
            both[:, 0] = other_ref[:, :, first:]
            both[:, 1] = mine_ref[:, :, first:]

        flipped[...] = both[...].reshape(w_ref.shape[0], flipped.shape[0]).T

    result = jnp.dot(flipped[...], w_ref[...], preferred_element_type=jnp.float32)
    start = 0
    for out in outs:
        out[...] = result[start : start + out.shape[0]]
        start += out.shape[0]


def partial_logits(place, mine, other, head_weight, first, sizes):
    feats, width = head_weight.shape
    tile = 512
    count = sum(sizes)
    pairs, unit, _ = mine.shape
    half = pl.BlockSpec((pairs, unit, first + count), lambda i: (0, 0, 0))
    return pl.pallas_call(
        functools.partial(logits_kernel, first),
        grid=(width // tile,),
        in_specs=[SMEM, half, half, pl.BlockSpec((feats, tile), lambda i: (0, i))],
        out_specs=[pl.BlockSpec((size, tile), lambda i: (0, i)) for size in sizes],
        out_shape=[jax.ShapeDtypeStruct((size, width), jnp.float32) for size in sizes],
        scratch_shapes=[
            pltpu.VMEM((pairs, 2, unit, count), jnp.bfloat16),
            pltpu.VMEM((count, feats), jnp.bfloat16),
        ],
        compiler_params=params(),
        cost_estimate=cost(
            2 * count * feats * width, feats * width * 2 + count * (feats * 2 + width * 4)
        ),
    )(place, mine, other, head_weight)


def order_kernel(place_ref, pairing_ref, teacher_ref, after_ref, ordered_ref):
    vocabs, sections, width = ordered_ref.shape
    section = place_ref[0]
    paired = [pairing_ref[section, k] for k in range(sections)]
    for v in range(vocabs):
        rows = teacher_ref[:, v * width : (v + 1) * width].astype(jnp.float32)
        row = lax.broadcasted_iota(jnp.int32, (sections, width), 0)
        out = jnp.zeros((sections, width), jnp.float32)
        for k in range(sections):
            out = jnp.where(row == paired[k], rows[k : k + 1], out)
        ordered_ref[v] = out.astype(jnp.bfloat16)


def add_kernel(mine_ref, far_ref, after_ref, out_ref):
    out_ref[...] = mine_ref[...] + far_ref[...]


def stats_kernel(own_ref, lo_a, lo_b, hi_a, hi_b, teacher_ref, logits_ref, stats_ref):
    half = lo_a.shape[0]
    logits_ref[:half] = own_ref[:half] + lo_a[...] + lo_b[...]
    logits_ref[half:] = own_ref[half:] + hi_a[...] + hi_b[...]
    logits = logits_ref[...]
    teacher = teacher_ref[...].astype(jnp.float32)
    top_s = jnp.max(logits, axis=1, keepdims=True)
    top_t = jnp.max(teacher, axis=1, keepdims=True)
    sum_s = jnp.sum(jnp.exp(logits - top_s), axis=1, keepdims=True)
    exp_t = jnp.exp(teacher - top_t)
    sum_t = jnp.sum(exp_t, axis=1, keepdims=True)
    cross = jnp.sum(exp_t * (teacher - logits), axis=1, keepdims=True)
    own = logits.shape[0]
    lane = lax.broadcasted_iota(jnp.int32, (own, 128), 1)
    packed = jnp.zeros((own, 128), jnp.float32)
    for place, column in enumerate((top_s, top_t, sum_s, sum_t, cross)):
        packed = jnp.where(lane == place, column, packed)
    rows = packed.T[:8]
    for k in range(stats_ref.shape[0]):
        stats_ref[k] = rows


def grads_kernel(logits_ref, teacher_ref, stats_ref, low_ref, high_ref, div_ref):
    stats = stats_ref[...]
    top = jnp.max(stats, axis=0)
    scale = jnp.exp(stats[:, :2] - top[None, :2])
    top_s, top_t = top[0:1], top[1:2]
    total_s = jnp.sum(stats[:, 2] * scale[:, 0], axis=0, keepdims=True)
    total_t = jnp.sum(stats[:, 3] * scale[:, 1], axis=0, keepdims=True)
    cross = jnp.sum(stats[:, 4] * scale[:, 1], axis=0, keepdims=True)
    div_ref[...] = cross / total_t - top_t - jnp.log(total_t) + top_s + jnp.log(total_s)
    own = logits_ref.shape[0]
    half = own // 2
    row = lax.broadcasted_iota(jnp.int32, (128, own), 0)
    packed = jnp.zeros((128, own), jnp.float32)
    for place, values in enumerate((top_s, top_t, loss_scale / total_s, loss_scale / total_t)):
        packed = jnp.where(row == place, values, packed)
    columns = packed.T
    grad = (
        jnp.exp(logits_ref[...] - columns[:, 0:1]) * columns[:, 2:3]
        - jnp.exp(teacher_ref[...].astype(jnp.float32) - columns[:, 1:2]) * columns[:, 3:4]
    ).astype(jnp.bfloat16)
    low_ref[...] = grad[:half]
    high_ref[...] = grad[half:]


def hidden_kernel(place_ref, w_ref, *refs):
    *pieces, keep_ref, send_ref, window = refs

    @pl.when(pl.program_id(0) == 0)
    def _():
        start = 0
        for piece in pieces:
            window[start : start + piece.shape[0]] = piece[...]
            start += piece.shape[0]

    pairs, feats, rows = keep_ref.shape
    result = lax.dot_general(
        w_ref[...], window[...], (((1,), (1,)), ((), ())), preferred_element_type=jnp.float32
    ).reshape(pairs, 2, feats, rows)
    core = remainder(place_ref[2], 2)

    @pl.when(core == 0)
    def _():
        keep_ref[...] = result[:, 0]
        send_ref[...] = result[:, 1]

    @pl.when(core != 0)
    def _():
        keep_ref[...] = result[:, 1]
        send_ref[...] = result[:, 0]


def hidden_grads(place, head_weight, pieces, pairs):
    feats, width = head_weight.shape
    rows = sum(piece.shape[0] for piece in pieces)
    steps = 2
    shape = jax.ShapeDtypeStruct((pairs, feats // (2 * pairs), rows), jnp.float32)
    block = pl.BlockSpec((pairs // steps,) + shape.shape[1:], lambda i: (i, 0, 0))
    return pl.pallas_call(
        hidden_kernel,
        grid=(steps,),
        in_specs=[SMEM, pl.BlockSpec((feats // steps, width), lambda i: (i, 0))]
        + [pl.BlockSpec(piece.shape, lambda i: (0, 0)) for piece in pieces],
        out_specs=[block, block],
        out_shape=[shape, shape],
        scratch_shapes=[pltpu.VMEM((rows, width), jnp.bfloat16)],
        compiler_params=params(),
        cost_estimate=cost(
            2 * rows * feats * width, feats * width * 2 + rows * width * 2 + rows * feats * 4
        ),
    )(place, head_weight, *pieces)


def regroup_kernel(place_ref, parts_ref, div_ref, out_ref):
    sections, height, own = out_ref.shape
    _, feats, _ = parts_ref.shape
    unit = own // 4
    summed = jnp.sum(parts_ref[...], axis=0)
    lane = lax.broadcasted_iota(jnp.int32, (feats, own), 1)
    order = window_order(sections)
    for s in range(sections):
        out = jnp.zeros((feats, own), jnp.float32)
        for piece in range(4):
            start = order.index((piece, s)) * unit
            whole = start // own * own
            turned = pltpu.roll(
                summed[:, whole : whole + own], (piece * unit - start + whole) % own, 1
            )
            out = jnp.where((lane >= piece * unit) & (lane < (piece + 1) * unit), turned, out)
        out_ref[s, :feats] = out
    section = place_ref[0]
    values = jnp.broadcast_to(div_ref[...], (height - feats, own))
    small = lane[: height - feats]
    for s in range(sections):
        out = jnp.zeros_like(values)
        for mine in range(sections):
            turned = pltpu.roll(values, (mine - s) * unit % own, 1)
            inside = (small >= mine * unit) & (small < (mine + 1) * unit)
            out = jnp.where(inside & (section == mine), turned, out)
        out_ref[s, feats:] = out


def return_kernel(place_ref, got_ref, grads_ref, div_ref, *, toks):
    sections, _, own = got_ref.shape
    unit = own // 4
    feats, rows = grads_ref.shape
    lane = lax.broadcasted_iota(jnp.int32, (feats, own), 1)
    outs = [jnp.zeros((feats, own), jnp.float32) for _ in range(rows // own)]
    for sender in range(sections):
        values = got_ref[sender, :feats]
        for piece in range(4):
            block = window_block(
                jnp.int32(sender), place_ref[1], place_ref[0], piece, sections, toks
            )
            begin = remainder(block, 4) * unit
            turned = pltpu.roll(values, remainder(begin - piece * unit + own, own), 1)
            first = lane - quotient(block, 4) * own - begin
            for index in range(len(outs)):
                inside = (first >= -index * own) & (first < unit - index * own)
                outs[index] = jnp.where(inside, turned, outs[index])
    for index, out in enumerate(outs):
        grads_ref[:, index * own : (index + 1) * own] = out
    div_ref[...] = jnp.sum(got_ref[:, feats : feats + 1, :], axis=0)


def shards(hidden, head_weight, teacher_logits, pairing):
    sections = lax.axis_size("sect")
    toks = lax.axis_size("tok")
    vocabs = lax.axis_size("vocab")
    planes = sections * toks
    width = head_weight.shape[1]
    rows, feats = hidden.shape
    own = rows // toks
    half = own // 2
    place = jnp.stack([lax.axis_index(name) for name in ("sect", "tok", "vocab")])

    picked = pl.pallas_call(
        functools.partial(pick_kernel, toks=toks),
        in_specs=[SMEM, VMEM],
        out_specs=VMEM,
        out_shape=jax.ShapeDtypeStruct((sections, feats, own), jnp.bfloat16),
        compiler_params=params(),
    )(place, hidden.T)
    spread = pl.pallas_call(
        arrange_kernel,
        in_specs=[VMEM],
        out_specs=VMEM,
        out_shape=jax.ShapeDtypeStruct((vocabs // 2, feats, rows), jnp.bfloat16),
        compiler_params=params(),
        cost_estimate=cost(20 * 10**9, 64 * 10**6),
    )(exchange(picked, "sect"))
    groups = [list(range(core, vocabs, 2)) for core in range(2)]
    other_core = [(i, i ^ 1) for i in range(vocabs)]
    mine = exchange(spread, "vocab", axis_index_groups=groups)
    other = lax.ppermute(mine, "vocab", other_core)

    edge_down, edge_up = partial_logits(
        place, mine, other, head_weight, 0, [half, half]
    )
    far_down = along_z(edge_down, -1, planes)
    far_up = along_z(edge_up, 1, planes)
    near_down, near_up, next_down, next_up, kept = partial_logits(
        place, mine, other, head_weight, own, [half, half, half, half, own]
    )
    down_b = along_z(near_down, -1, planes)
    up_a = along_z(near_up, 1, planes)

    ordered = pl.pallas_call(
        order_kernel,
        in_specs=[SMEM, SMEM, VMEM, ANYWHERE],
        out_specs=VMEM,
        out_shape=jax.ShapeDtypeStruct((vocabs, sections, width), jnp.bfloat16),
        compiler_params=params(),
    )(place, pairing, teacher_logits, kept)

    add = pl.pallas_call(
        add_kernel,
        in_specs=[VMEM, VMEM, ANYWHERE],
        out_specs=VMEM,
        out_shape=jax.ShapeDtypeStruct(next_down.shape, jnp.float32),
        compiler_params=params(),
    )
    down_a = along_z(add(next_down, far_down, ordered), -1, planes)
    up_b = along_z(add(next_up, far_up, ordered), 1, planes)
    teacher = exchange(ordered, "vocab").transpose(1, 0, 2).reshape(own, width)

    logits, stats = pl.pallas_call(
        stats_kernel,
        out_shape=[
            jax.ShapeDtypeStruct((own, width), jnp.float32),
            jax.ShapeDtypeStruct((vocabs, 8, own), jnp.float32),
        ],
        compiler_params=params(),
    )(kept, down_a, up_a, down_b, up_b, teacher)
    low, high, diverge = pl.pallas_call(
        grads_kernel,
        out_shape=[
            jax.ShapeDtypeStruct((half, width), jnp.bfloat16),
            jax.ShapeDtypeStruct((half, width), jnp.bfloat16),
            jax.ShapeDtypeStruct((1, own), jnp.float32),
        ],
        compiler_params=params(),
    )(logits, teacher, exchange(stats, "vocab"))

    below_low = along_z(low, 1, planes)
    above_high = along_z(high, -1, planes)
    below_high = along_z(high, 1, planes)
    above_low = along_z(low, -1, planes)
    far_below = along_z(below_low, 1, planes)
    far_above = along_z(above_high, -1, planes)
    keep, send = hidden_grads(
        place,
        head_weight,
        [far_below, far_above, below_high, above_low, below_low, above_high, low, high],
        vocabs // 2,
    )
    other = lax.ppermute(send, "vocab", other_core)
    parts = exchange(keep + other, "vocab", axis_index_groups=groups)

    regrouped = pl.pallas_call(
        regroup_kernel,
        in_specs=[SMEM, VMEM, VMEM],
        out_specs=VMEM,
        out_shape=jax.ShapeDtypeStruct((sections, feats + 8, own), jnp.float32),
        compiler_params=params(),
    )(place, parts, diverge)
    grads, div = pl.pallas_call(
        functools.partial(return_kernel, toks=toks),
        in_specs=[SMEM, VMEM],
        out_specs=[VMEM, VMEM],
        out_shape=[
            jax.ShapeDtypeStruct((feats, rows), jnp.float32),
            jax.ShapeDtypeStruct((1, own), jnp.float32),
        ],
        compiler_params=params(),
    )(place, exchange(regrouped, "sect"))
    return grads.T, div.reshape(own)


def solution(mesh):
    placed = (
        P("sect", ("tok", "vocab")),
        P("tok", "vocab"),
        P(("sect", "tok", "vocab"), None),
        P(),
    )
    return jax.shard_map(
        shards,
        mesh=mesh,
        in_specs=placed,
        out_specs=(P("sect", ("tok", "vocab")), P(("sect", "tok"))),
        check_vma=False,
    )
```

```python
import functools

import jax
import jax.numpy as jnp
from jax import lax
from jax.experimental import pallas as pl
from jax.experimental.pallas import tpu as pltpu
from jax.sharding import PartitionSpec as P

loss_scale = 16.0
VMEM_BYTES = 24 * 1024 * 1024
SMEM = pl.BlockSpec(memory_space=pltpu.SMEM)
VMEM = pl.BlockSpec(memory_space=pltpu.VMEM)
ANYWHERE = pl.BlockSpec(memory_space=pl.ANY)


def along_z(value, steps, planes):
    return lax.ppermute(
        value, ("sect", "tok"), [(i, (i + steps) % planes) for i in range(planes)]
    )


def exchange(value, axis, **groups):
    return lax.all_to_all(value, axis, split_axis=0, concat_axis=0, tiled=True, **groups)


def params():
    return pltpu.CompilerParams(vmem_limit_bytes=VMEM_BYTES)


def cost(flops, bytes_accessed):
    return pl.CostEstimate(flops=flops, bytes_accessed=bytes_accessed, transcendentals=0)


def remainder(value, count):
    return value & (count - 1) if count & (count - 1) == 0 else lax.rem(value, count)


def quotient(value, count):
    if count & (count - 1) == 0:
        return lax.shift_right_logical(value, jnp.int32(count.bit_length() - 1))
    return lax.div(value, count)


def window_block(section, tok, token_section, piece, sections, toks):
    planes = sections * toks
    near = jnp.int32(piece - 2)
    far = jnp.where(token_section < sections // 2, -2, 2)
    plane = remainder(section * toks + tok + (far if piece == 0 else near) + planes, planes)
    return remainder(plane, toks) * sections + quotient(plane, toks)


def window_order(sections):
    low = list(range(sections // 2))
    high = list(range(sections // 2, sections))
    order = [(0, s) for s in low + high]
    order += [(1, s) for s in high] + [(3, s) for s in low]
    order += [(1, s) for s in low] + [(3, s) for s in high]
    return order + [(2, s) for s in low + high]


def pick_kernel(place_ref, hidden_ref, picked_ref, *, toks):
    sections, _, own = picked_ref.shape
    rows = hidden_ref.shape[1]
    unit = own // 4
    section, tok = place_ref[0], place_ref[1]
    lane = lax.broadcasted_iota(jnp.int32, (rows, own), 1)
    row = lax.broadcasted_iota(jnp.int32, (rows, own), 0)
    for k in range(sections):
        source = lane
        for piece in range(4):
            block = window_block(jnp.int32(k), tok, section, piece, sections, toks)
            source = jnp.where(
                (lane >= piece * unit) & (lane < (piece + 1) * unit),
                (block - piece) * unit + lane,
                source,
            )
        pick = jnp.where(row == source, 1.0, 0.0).astype(jnp.bfloat16)
        picked_ref[k] = jnp.dot(
            hidden_ref[...], pick, preferred_element_type=jnp.float32
        ).astype(jnp.bfloat16)


def arrange_kernel(got_ref, spread_ref):
    sections, _, own = got_ref.shape
    rows = spread_ref.shape[2]
    unit = own // 4
    lane = lax.broadcasted_iota(jnp.int32, (own, rows), 1)
    row = lax.broadcasted_iota(jnp.int32, (own, rows), 0)
    total = None
    for s in range(sections):
        source = jnp.full((own, rows), -1, jnp.int32)
        for place, (piece, token_section) in enumerate(window_order(sections)):
            if token_section == s:
                source = jnp.where(
                    (lane >= place * unit) & (lane < (place + 1) * unit),
                    lane + (piece - place) * unit,
                    source,
                )
        move = jnp.where(row == source, 1.0, 0.0).astype(jnp.bfloat16)
        part = jnp.dot(got_ref[s], move, preferred_element_type=jnp.float32)
        total = part if total is None else total + part
    window = total.astype(jnp.bfloat16)
    for k in range(spread_ref.shape[0]):
        spread_ref[k] = window


def logits_kernel(first, place_ref, mine_ref, other_ref, w_ref, *refs):
    *outs, both, flipped = refs

    @pl.when(pl.program_id(0) == 0)
    def _():
        core = remainder(place_ref[2], 2)

        @pl.when(core == 0)
        def _():
            both[:, 0] = mine_ref[:, :, first : first + both.shape[3]]
            both[:, 1] = other_ref[:, :, first : first + both.shape[3]]

        @pl.when(core != 0)
        def _():
            both[:, 0] = other_ref[:, :, first : first + both.shape[3]]
            both[:, 1] = mine_ref[:, :, first : first + both.shape[3]]

        flipped[...] = both[...].reshape(w_ref.shape[0], flipped.shape[0]).T

    result = jnp.dot(flipped[...], w_ref[...], preferred_element_type=jnp.float32)
    start = 0
    for out in outs:
        out[...] = result[start : start + out.shape[0]]
        start += out.shape[0]


def partial_logits(place, mine, other, head_weight, first, sizes):
    feats, width = head_weight.shape
    tile = 512
    count = sum(sizes)
    pairs, unit, _ = mine.shape
    return pl.pallas_call(
        functools.partial(logits_kernel, first),
        grid=(width // tile,),
        in_specs=[SMEM, VMEM, VMEM, pl.BlockSpec((feats, tile), lambda i: (0, i))],
        out_specs=[pl.BlockSpec((size, tile), lambda i: (0, i)) for size in sizes],
        out_shape=[jax.ShapeDtypeStruct((size, width), jnp.float32) for size in sizes],
        scratch_shapes=[
            pltpu.VMEM((pairs, 2, unit, count), jnp.bfloat16),
            pltpu.VMEM((count, feats), jnp.bfloat16),
        ],
        compiler_params=params(),
        cost_estimate=cost(
            2 * count * feats * width, feats * width * 2 + count * (feats * 2 + width * 4)
        ),
    )(place, mine, other, head_weight)


def order_kernel(place_ref, pairing_ref, teacher_ref, after_ref, ordered_ref):
    vocabs, sections, width = ordered_ref.shape
    section = place_ref[0]
    paired = [pairing_ref[section, k] for k in range(sections)]
    for v in range(vocabs):
        rows = teacher_ref[:, v * width : (v + 1) * width].astype(jnp.float32)
        row = lax.broadcasted_iota(jnp.int32, (sections, width), 0)
        out = jnp.zeros((sections, width), jnp.float32)
        for k in range(sections):
            out = jnp.where(row == paired[k], rows[k : k + 1], out)
        ordered_ref[v] = out.astype(jnp.bfloat16)


def add_kernel(mine_ref, far_ref, after_ref, out_ref):
    out_ref[...] = mine_ref[...] + far_ref[...]


def stats_kernel(own_ref, lo_a, lo_b, hi_a, hi_b, teacher_ref, logits_ref, stats_ref):
    half = lo_a.shape[0]
    logits_ref[:half] = own_ref[:half] + lo_a[...] + lo_b[...]
    logits_ref[half:] = own_ref[half:] + hi_a[...] + hi_b[...]
    logits = logits_ref[...]
    teacher = teacher_ref[...].astype(jnp.float32)
    top_s = jnp.max(logits, axis=1, keepdims=True)
    top_t = jnp.max(teacher, axis=1, keepdims=True)
    sum_s = jnp.sum(jnp.exp(logits - top_s), axis=1, keepdims=True)
    exp_t = jnp.exp(teacher - top_t)
    sum_t = jnp.sum(exp_t, axis=1, keepdims=True)
    cross = jnp.sum(exp_t * (teacher - logits), axis=1, keepdims=True)
    own = logits.shape[0]
    lane = lax.broadcasted_iota(jnp.int32, (own, 128), 1)
    packed = jnp.zeros((own, 128), jnp.float32)
    for place, column in enumerate((top_s, top_t, sum_s, sum_t, cross)):
        packed = jnp.where(lane == place, column, packed)
    rows = packed.T[:8]
    for k in range(stats_ref.shape[0]):
        stats_ref[k] = rows


def grads_kernel(logits_ref, teacher_ref, stats_ref, low_ref, high_ref, div_ref):
    stats = stats_ref[...]
    top = jnp.max(stats, axis=0)
    scale = jnp.exp(stats[:, :2] - top[None, :2])
    top_s, top_t = top[0:1], top[1:2]
    total_s = jnp.sum(stats[:, 2] * scale[:, 0], axis=0, keepdims=True)
    total_t = jnp.sum(stats[:, 3] * scale[:, 1], axis=0, keepdims=True)
    cross = jnp.sum(stats[:, 4] * scale[:, 1], axis=0, keepdims=True)
    div_ref[...] = cross / total_t - top_t - jnp.log(total_t) + top_s + jnp.log(total_s)
    own = logits_ref.shape[0]
    half = own // 2
    row = lax.broadcasted_iota(jnp.int32, (128, own), 0)
    packed = jnp.zeros((128, own), jnp.float32)
    for place, values in enumerate((top_s, top_t, loss_scale / total_s, loss_scale / total_t)):
        packed = jnp.where(row == place, values, packed)
    columns = packed.T
    grad = (
        jnp.exp(logits_ref[...] - columns[:, 0:1]) * columns[:, 2:3]
        - jnp.exp(teacher_ref[...].astype(jnp.float32) - columns[:, 1:2]) * columns[:, 3:4]
    ).astype(jnp.bfloat16)
    low_ref[...] = grad[:half]
    high_ref[...] = grad[half:]


def hidden_kernel(earlier, place_ref, w_ref, *refs):
    *pieces, keep_ref, send_ref, window = refs
    pieces = pieces[: len(pieces) - earlier]

    @pl.when(pl.program_id(0) == 0)
    def _():
        start = 0
        for piece in pieces:
            window[start : start + piece.shape[0]] = piece[...]
            start += piece.shape[0]

    pairs, feats, rows = keep_ref.shape
    result = lax.dot_general(
        w_ref[...], window[...], (((1,), (1,)), ((), ())), preferred_element_type=jnp.float32
    ).reshape(pairs, 2, feats, rows)
    core = remainder(place_ref[2], 2)

    @pl.when(core == 0)
    def _():
        keep_ref[...] = result[:, 0]
        send_ref[...] = result[:, 1]

    @pl.when(core != 0)
    def _():
        keep_ref[...] = result[:, 1]
        send_ref[...] = result[:, 0]


def hidden_grads(place, head_weight, pieces, pairs, total, earlier=()):
    feats, width = head_weight.shape
    rows = sum(piece.shape[0] for piece in pieces)
    index = (total - rows) // rows if earlier else 0
    steps = 2
    shape = jax.ShapeDtypeStruct((pairs, feats // (2 * pairs), total), jnp.float32)
    block = pl.BlockSpec((pairs // steps, shape.shape[1], rows), lambda i: (i, 0, index))
    inputs = 2 + len(pieces)
    return pl.pallas_call(
        functools.partial(hidden_kernel, len(earlier)),
        grid=(steps,),
        in_specs=[SMEM, pl.BlockSpec((feats // steps, width), lambda i: (i, 0))]
        + [VMEM] * len(pieces)
        + [ANYWHERE] * len(earlier),
        out_specs=[block, block],
        out_shape=[shape, shape],
        scratch_shapes=[pltpu.VMEM((rows, width), jnp.bfloat16)],
        input_output_aliases={inputs + k: k for k in range(len(earlier))},
        compiler_params=params(),
        cost_estimate=cost(
            2 * rows * feats * width, feats * width * 2 + rows * width * 2 + rows * feats * 4
        ),
    )(place, head_weight, *pieces, *earlier)


def regroup_kernel(place_ref, parts_ref, div_ref, out_ref):
    sections, height, own = out_ref.shape
    _, feats, _ = parts_ref.shape
    unit = own // 4
    summed = jnp.sum(parts_ref[...], axis=0)
    lane = lax.broadcasted_iota(jnp.int32, (feats, own), 1)
    order = window_order(sections)
    order = order[sections:] + order[:sections]
    for s in range(sections):
        out = jnp.zeros((feats, own), jnp.float32)
        for piece in range(4):
            start = order.index((piece, s)) * unit
            whole = start // own * own
            turned = pltpu.roll(
                summed[:, whole : whole + own], (piece * unit - start + whole) % own, 1
            )
            out = jnp.where((lane >= piece * unit) & (lane < (piece + 1) * unit), turned, out)
        out_ref[s, :feats] = out
    section = place_ref[0]
    values = jnp.broadcast_to(div_ref[...], (height - feats, own))
    small = lane[: height - feats]
    for s in range(sections):
        out = jnp.zeros_like(values)
        for mine in range(sections):
            turned = pltpu.roll(values, (mine - s) * unit % own, 1)
            inside = (small >= mine * unit) & (small < (mine + 1) * unit)
            out = jnp.where(inside & (section == mine), turned, out)
        out_ref[s, feats:] = out


def return_kernel(place_ref, got_ref, grads_ref, div_ref, *, toks):
    sections, _, own = got_ref.shape
    unit = own // 4
    feats, rows = grads_ref.shape
    lane = lax.broadcasted_iota(jnp.int32, (feats, own), 1)
    outs = [jnp.zeros((feats, own), jnp.float32) for _ in range(rows // own)]
    for sender in range(sections):
        values = got_ref[sender, :feats]
        for piece in range(4):
            block = window_block(
                jnp.int32(sender), place_ref[1], place_ref[0], piece, sections, toks
            )
            begin = remainder(block, 4) * unit
            turned = pltpu.roll(values, remainder(begin - piece * unit + own, own), 1)
            first = lane - quotient(block, 4) * own - begin
            for index in range(len(outs)):
                inside = (first >= -index * own) & (first < unit - index * own)
                outs[index] = jnp.where(inside, turned, outs[index])
    for index, out in enumerate(outs):
        grads_ref[:, index * own : (index + 1) * own] = out
    div_ref[...] = jnp.sum(got_ref[:, feats : feats + 1, :], axis=0)


def shards(hidden, head_weight, teacher_logits, pairing):
    sections = lax.axis_size("sect")
    toks = lax.axis_size("tok")
    vocabs = lax.axis_size("vocab")
    planes = sections * toks
    width = head_weight.shape[1]
    rows, feats = hidden.shape
    own = rows // toks
    half = own // 2
    place = jnp.stack([lax.axis_index(name) for name in ("sect", "tok", "vocab")])

    picked = pl.pallas_call(
        functools.partial(pick_kernel, toks=toks),
        in_specs=[SMEM, VMEM],
        out_specs=VMEM,
        out_shape=jax.ShapeDtypeStruct((sections, feats, own), jnp.bfloat16),
        compiler_params=params(),
    )(place, hidden.T)
    spread = pl.pallas_call(
        arrange_kernel,
        in_specs=[VMEM],
        out_specs=VMEM,
        out_shape=jax.ShapeDtypeStruct((vocabs // 2, feats, rows), jnp.bfloat16),
        compiler_params=params(),
        cost_estimate=cost(20 * 10**9, 64 * 10**6),
    )(exchange(picked, "sect"))
    groups = [list(range(core, vocabs, 2)) for core in range(2)]
    other_core = [(i, i ^ 1) for i in range(vocabs)]
    mine = exchange(spread, "vocab", axis_index_groups=groups)
    other = lax.ppermute(mine, "vocab", other_core)

    edge_down, edge_up = partial_logits(
        place, mine, other, head_weight, 0, [half, half]
    )
    far_down = along_z(edge_down, -1, planes)
    far_up = along_z(edge_up, 1, planes)
    near_down, near_up, next_down, next_up, kept = partial_logits(
        place, mine, other, head_weight, own, [half, half, half, half, own]
    )
    down_b = along_z(near_down, -1, planes)
    up_a = along_z(near_up, 1, planes)

    ordered = pl.pallas_call(
        order_kernel,
        in_specs=[SMEM, SMEM, VMEM, ANYWHERE],
        out_specs=VMEM,
        out_shape=jax.ShapeDtypeStruct((vocabs, sections, width), jnp.bfloat16),
        compiler_params=params(),
    )(place, pairing, teacher_logits, kept)

    add = pl.pallas_call(
        add_kernel,
        in_specs=[VMEM, VMEM, ANYWHERE],
        out_specs=VMEM,
        out_shape=jax.ShapeDtypeStruct(next_down.shape, jnp.float32),
        compiler_params=params(),
    )
    down_a = along_z(add(next_down, far_down, ordered), -1, planes)
    up_b = along_z(add(next_up, far_up, ordered), 1, planes)
    teacher = exchange(ordered, "vocab").transpose(1, 0, 2).reshape(own, width)

    logits, stats = pl.pallas_call(
        stats_kernel,
        out_shape=[
            jax.ShapeDtypeStruct((own, width), jnp.float32),
            jax.ShapeDtypeStruct((vocabs, 8, own), jnp.float32),
        ],
        compiler_params=params(),
    )(kept, down_a, up_a, down_b, up_b, teacher)
    low, high, diverge = pl.pallas_call(
        grads_kernel,
        out_shape=[
            jax.ShapeDtypeStruct((half, width), jnp.bfloat16),
            jax.ShapeDtypeStruct((half, width), jnp.bfloat16),
            jax.ShapeDtypeStruct((1, own), jnp.float32),
        ],
        compiler_params=params(),
    )(logits, teacher, exchange(stats, "vocab"))

    below_low = along_z(low, 1, planes)
    above_high = along_z(high, -1, planes)
    below_high = along_z(high, 1, planes)
    above_low = along_z(low, -1, planes)
    far_below = along_z(below_low, 1, planes)
    far_above = along_z(above_high, -1, planes)
    near_pieces = [below_high, above_low, below_low, above_high, low, high]
    near = hidden_grads(place, head_weight, near_pieces, vocabs // 2, rows)
    keep, send = hidden_grads(
        place, head_weight, [far_below, far_above], vocabs // 2, rows, near
    )
    other = lax.ppermute(send, "vocab", other_core)
    parts = exchange(keep + other, "vocab", axis_index_groups=groups)

    regrouped = pl.pallas_call(
        regroup_kernel,
        in_specs=[SMEM, VMEM, VMEM],
        out_specs=VMEM,
        out_shape=jax.ShapeDtypeStruct((sections, feats + 8, own), jnp.float32),
        compiler_params=params(),
    )(place, parts, diverge)
    grads, div = pl.pallas_call(
        functools.partial(return_kernel, toks=toks),
        in_specs=[SMEM, VMEM],
        out_specs=[VMEM, VMEM],
        out_shape=[
            jax.ShapeDtypeStruct((feats, rows), jnp.float32),
            jax.ShapeDtypeStruct((1, own), jnp.float32),
        ],
        compiler_params=params(),
    )(place, exchange(regrouped, "sect"))
    return grads.T, div.reshape(own)


def solution(mesh):
    placed = (
        P("sect", ("tok", "vocab")),
        P("tok", "vocab"),
        P(("sect", "tok", "vocab"), None),
        P(),
    )
    return jax.shard_map(
        shards,
        mesh=mesh,
        in_specs=placed,
        out_specs=(P("sect", ("tok", "vocab")), P(("sect", "tok"))),
        check_vma=False,
    )
```

```python
import functools

import jax
import jax.numpy as jnp
from jax import lax
from jax.experimental import pallas as pl
from jax.experimental.pallas import tpu as pltpu
from jax.sharding import PartitionSpec as P

loss_scale = 16.0
VMEM_BYTES = 24 * 1024 * 1024
SMEM = pl.BlockSpec(memory_space=pltpu.SMEM)
VMEM = pl.BlockSpec(memory_space=pltpu.VMEM)
ANYWHERE = pl.BlockSpec(memory_space=pl.ANY)


def along_z(value, steps, planes, vocabs):
    pairs = []
    for plane in range(planes):
        for device in range(vocabs):
            there = (plane + (-steps if device % 2 else steps)) % planes
            pairs.append((plane * vocabs + device, there * vocabs + device))
    return lax.ppermute(value, ("sect", "tok", "vocab"), pairs)


def halves(core, half, start=0):
    first = pl.multiple_of(start + core * half, half)
    second = pl.multiple_of(start + (1 - core) * half, half)
    return pl.ds(first, half), pl.ds(second, half)


def exchange(value, axis, **groups):
    return lax.all_to_all(value, axis, split_axis=0, concat_axis=0, tiled=True, **groups)


def params():
    return pltpu.CompilerParams(vmem_limit_bytes=VMEM_BYTES)


def cost(flops, bytes_accessed):
    return pl.CostEstimate(flops=flops, bytes_accessed=bytes_accessed, transcendentals=0)


def remainder(value, count):
    return value & (count - 1) if count & (count - 1) == 0 else lax.rem(value, count)


def quotient(value, count):
    if count & (count - 1) == 0:
        return lax.shift_right_logical(value, jnp.int32(count.bit_length() - 1))
    return lax.div(value, count)


def window_block(section, tok, token_section, piece, sections, toks):
    planes = sections * toks
    near = jnp.int32(piece - 2)
    far = jnp.where(token_section < sections // 2, -2, 2)
    plane = remainder(section * toks + tok + (far if piece == 0 else near) + planes, planes)
    return remainder(plane, toks) * sections + quotient(plane, toks)


def window_order(sections):
    low = list(range(sections // 2))
    high = list(range(sections // 2, sections))
    order = [(0, s) for s in low + high]
    order += [(1, s) for s in high] + [(3, s) for s in low]
    order += [(1, s) for s in low] + [(3, s) for s in high]
    return order + [(2, s) for s in low + high]


def pick_kernel(place_ref, hidden_ref, picked_ref, *, toks):
    sections, _, own = picked_ref.shape
    rows = hidden_ref.shape[1]
    unit = own // 4
    section, tok = place_ref[0], place_ref[1]
    lane = lax.broadcasted_iota(jnp.int32, (rows, own), 1)
    row = lax.broadcasted_iota(jnp.int32, (rows, own), 0)
    for k in range(sections):
        source = lane
        for piece in range(4):
            block = window_block(jnp.int32(k), tok, section, piece, sections, toks)
            source = jnp.where(
                (lane >= piece * unit) & (lane < (piece + 1) * unit),
                (block - piece) * unit + lane,
                source,
            )
        pick = jnp.where(row == source, 1.0, 0.0).astype(jnp.bfloat16)
        picked_ref[k] = jnp.dot(
            hidden_ref[...], pick, preferred_element_type=jnp.float32
        ).astype(jnp.bfloat16)


def arrange_kernel(got_ref, spread_ref):
    sections, _, own = got_ref.shape
    rows = spread_ref.shape[2]
    unit = own // 4
    lane = lax.broadcasted_iota(jnp.int32, (own, rows), 1)
    row = lax.broadcasted_iota(jnp.int32, (own, rows), 0)
    total = None
    for s in range(sections):
        source = jnp.full((own, rows), -1, jnp.int32)
        for place, (piece, token_section) in enumerate(window_order(sections)):
            if token_section == s:
                source = jnp.where(
                    (lane >= place * unit) & (lane < (place + 1) * unit),
                    lane + (piece - place) * unit,
                    source,
                )
        move = jnp.where(row == source, 1.0, 0.0).astype(jnp.bfloat16)
        part = jnp.dot(got_ref[s], move, preferred_element_type=jnp.float32)
        total = part if total is None else total + part
    window = total.astype(jnp.bfloat16)
    for k in range(spread_ref.shape[0]):
        spread_ref[k] = window


def logits_kernel(first, place_ref, mine_ref, other_ref, w_ref, *refs):
    *outs, both, flipped = refs

    @pl.when(pl.program_id(0) == 0)
    def _():
        core = remainder(place_ref[2], 2)

        @pl.when(core == 0)
        def _():
            both[:, 0] = mine_ref[:, :, first : first + both.shape[3]]
            both[:, 1] = other_ref[:, :, first : first + both.shape[3]]

        @pl.when(core != 0)
        def _():
            both[:, 0] = other_ref[:, :, first : first + both.shape[3]]
            both[:, 1] = mine_ref[:, :, first : first + both.shape[3]]

        turned = both[...].reshape(w_ref.shape[0], flipped.shape[0]).T
        start = 0
        for one in outs[0 : len(outs) // 2 * 2 : 2]:
            half = one.shape[0]
            low, high = halves(core, half, start)
            flipped[low] = turned[start : start + half]
            flipped[high] = turned[start + half : start + 2 * half]
            start += 2 * half
        if len(outs) % 2:
            flipped[start:] = turned[start:]

    result = jnp.dot(flipped[...], w_ref[...], preferred_element_type=jnp.float32)
    start = 0
    for out in outs:
        out[...] = result[start : start + out.shape[0]]
        start += out.shape[0]


def partial_logits(place, mine, other, head_weight, first, sizes):
    feats, width = head_weight.shape
    tile = 512
    count = sum(sizes)
    pairs, unit, _ = mine.shape
    return pl.pallas_call(
        functools.partial(logits_kernel, first),
        grid=(width // tile,),
        in_specs=[SMEM, VMEM, VMEM, pl.BlockSpec((feats, tile), lambda i: (0, i))],
        out_specs=[pl.BlockSpec((size, tile), lambda i: (0, i)) for size in sizes],
        out_shape=[jax.ShapeDtypeStruct((size, width), jnp.float32) for size in sizes],
        scratch_shapes=[
            pltpu.VMEM((pairs, 2, unit, count), jnp.bfloat16),
            pltpu.VMEM((count, feats), jnp.bfloat16),
        ],
        compiler_params=params(),
        cost_estimate=cost(
            2 * count * feats * width, feats * width * 2 + count * (feats * 2 + width * 4)
        ),
    )(place, mine, other, head_weight)


def add_kernel(mine_ref, far_ref, out_ref):
    out_ref[...] = mine_ref[...] + far_ref[...]


def stats_kernel(
    place_ref,
    pairing_ref,
    own_ref,
    next_first,
    near_second,
    near_first,
    next_second,
    teacher_ref,
    logits_ref,
    sorted_ref,
    stats_ref,
):
    half = next_first.shape[0]
    one, two = halves(remainder(place_ref[2], 2), half)
    logits_ref[one] = own_ref[one] + next_first[...] + near_second[...]
    logits_ref[two] = own_ref[two] + near_first[...] + next_second[...]
    sections = pairing_ref.shape[0]
    unit = own_ref.shape[0] // sections
    for k in range(sections):
        begin = pl.multiple_of(pairing_ref[place_ref[0], k] * unit, unit)
        sorted_ref[pl.ds(begin, unit)] = teacher_ref[k * unit : (k + 1) * unit]
    logits = logits_ref[...]
    teacher = sorted_ref[...].astype(jnp.float32)
    top_s = jnp.max(logits, axis=1, keepdims=True)
    top_t = jnp.max(teacher, axis=1, keepdims=True)
    sum_s = jnp.sum(jnp.exp(logits - top_s), axis=1, keepdims=True)
    exp_t = jnp.exp(teacher - top_t)
    sum_t = jnp.sum(exp_t, axis=1, keepdims=True)
    cross = jnp.sum(exp_t * (teacher - logits), axis=1, keepdims=True)
    own = logits.shape[0]
    lane = lax.broadcasted_iota(jnp.int32, (own, 128), 1)
    packed = jnp.zeros((own, 128), jnp.float32)
    for place, column in enumerate((top_s, top_t, sum_s, sum_t, cross)):
        packed = jnp.where(lane == place, column, packed)
    rows = packed.T[:8]
    for k in range(stats_ref.shape[0]):
        stats_ref[k] = rows


def grads_kernel(
    place_ref, logits_ref, teacher_ref, stats_ref, first_ref, second_ref, div_ref, columns
):
    stats = stats_ref[...]
    top = jnp.max(stats, axis=0)
    scale = jnp.exp(stats[:, :2] - top[None, :2])
    top_s, top_t = top[0:1], top[1:2]
    total_s = jnp.sum(stats[:, 2] * scale[:, 0], axis=0, keepdims=True)
    total_t = jnp.sum(stats[:, 3] * scale[:, 1], axis=0, keepdims=True)
    cross = jnp.sum(stats[:, 4] * scale[:, 1], axis=0, keepdims=True)
    div_ref[...] = cross / total_t - top_t - jnp.log(total_t) + top_s + jnp.log(total_s)
    own = logits_ref.shape[0]
    half = own // 2
    row = lax.broadcasted_iota(jnp.int32, (128, own), 0)
    packed = jnp.zeros((128, own), jnp.float32)
    for place, values in enumerate((top_s, top_t, loss_scale / total_s, loss_scale / total_t)):
        packed = jnp.where(row == place, values, packed)
    columns[...] = packed.T
    places = halves(remainder(place_ref[2], 2), half)
    for place, out_ref in zip(places, (first_ref, second_ref)):
        values = columns[place]
        out_ref[...] = (
            jnp.exp(logits_ref[place] - values[:, 0:1]) * values[:, 2:3]
            - jnp.exp(teacher_ref[place].astype(jnp.float32) - values[:, 1:2]) * values[:, 3:4]
        ).astype(jnp.bfloat16)


def hidden_kernel(earlier, place_ref, w_ref, *refs):
    *pieces, keep_ref, send_ref, window = refs
    pieces = pieces[: len(pieces) - earlier]

    @pl.when(pl.program_id(0) == 0)
    def _():
        start = 0
        for one, two in zip(pieces[0::2], pieces[1::2]):
            half = one.shape[0]
            low, high = halves(remainder(place_ref[2], 2), half, start)
            window[low] = one[...]
            window[high] = two[...]
            start += 2 * half

    pairs, feats, rows = keep_ref.shape
    result = lax.dot_general(
        w_ref[...], window[...], (((1,), (1,)), ((), ())), preferred_element_type=jnp.float32
    ).reshape(pairs, 2, feats, rows)
    core = remainder(place_ref[2], 2)

    @pl.when(core == 0)
    def _():
        keep_ref[...] = result[:, 0]
        send_ref[...] = result[:, 1]

    @pl.when(core != 0)
    def _():
        keep_ref[...] = result[:, 1]
        send_ref[...] = result[:, 0]


def hidden_grads(place, head_weight, pieces, pairs, total, earlier=()):
    feats, width = head_weight.shape
    rows = sum(piece.shape[0] for piece in pieces)
    index = (total - rows) // rows if earlier else 0
    steps = 2
    shape = jax.ShapeDtypeStruct((pairs, feats // (2 * pairs), total), jnp.float32)
    block = pl.BlockSpec((pairs // steps, shape.shape[1], rows), lambda i: (i, 0, index))
    inputs = 2 + len(pieces)
    return pl.pallas_call(
        functools.partial(hidden_kernel, len(earlier)),
        grid=(steps,),
        in_specs=[SMEM, pl.BlockSpec((feats // steps, width), lambda i: (i, 0))]
        + [VMEM] * len(pieces)
        + [ANYWHERE] * len(earlier),
        out_specs=[block, block],
        out_shape=[shape, shape],
        scratch_shapes=[pltpu.VMEM((rows, width), jnp.bfloat16)],
        input_output_aliases={inputs + k: k for k in range(len(earlier))},
        compiler_params=params(),
        cost_estimate=cost(
            2 * rows * feats * width, feats * width * 2 + rows * width * 2 + rows * feats * 4
        ),
    )(place, head_weight, *pieces, *earlier)


def regroup_kernel(place_ref, parts_ref, div_ref, out_ref):
    sections, height, own = out_ref.shape
    _, feats, _ = parts_ref.shape
    unit = own // 4
    summed = jnp.sum(parts_ref[...], axis=0)
    lane = lax.broadcasted_iota(jnp.int32, (feats, own), 1)
    order = window_order(sections)
    order = order[sections:] + order[:sections]
    for s in range(sections):
        out = jnp.zeros((feats, own), jnp.float32)
        for piece in range(4):
            start = order.index((piece, s)) * unit
            whole = start // own * own
            turned = pltpu.roll(
                summed[:, whole : whole + own], (piece * unit - start + whole) % own, 1
            )
            out = jnp.where((lane >= piece * unit) & (lane < (piece + 1) * unit), turned, out)
        out_ref[s, :feats] = out
    section = place_ref[0]
    values = jnp.broadcast_to(div_ref[...], (height - feats, own))
    small = lane[: height - feats]
    for s in range(sections):
        out = jnp.zeros_like(values)
        for mine in range(sections):
            turned = pltpu.roll(values, (mine - s) * unit % own, 1)
            inside = (small >= mine * unit) & (small < (mine + 1) * unit)
            out = jnp.where(inside & (section == mine), turned, out)
        out_ref[s, feats:] = out


def return_kernel(place_ref, got_ref, grads_ref, div_ref, *, toks):
    sections, _, own = got_ref.shape
    unit = own // 4
    feats, rows = grads_ref.shape
    lane = lax.broadcasted_iota(jnp.int32, (feats, own), 1)
    outs = [jnp.zeros((feats, own), jnp.float32) for _ in range(rows // own)]
    for sender in range(sections):
        values = got_ref[sender, :feats]
        for piece in range(4):
            block = window_block(
                jnp.int32(sender), place_ref[1], place_ref[0], piece, sections, toks
            )
            begin = remainder(block, 4) * unit
            turned = pltpu.roll(values, remainder(begin - piece * unit + own, own), 1)
            first = lane - quotient(block, 4) * own - begin
            for index in range(len(outs)):
                inside = (first >= -index * own) & (first < unit - index * own)
                outs[index] = jnp.where(inside, turned, outs[index])
    for index, out in enumerate(outs):
        grads_ref[:, index * own : (index + 1) * own] = out
    div_ref[...] = jnp.sum(got_ref[:, feats : feats + 1, :], axis=0)


def shards(hidden, head_weight, teacher_logits, pairing):
    sections = lax.axis_size("sect")
    toks = lax.axis_size("tok")
    vocabs = lax.axis_size("vocab")
    planes = sections * toks
    width = head_weight.shape[1]
    rows, feats = hidden.shape
    own = rows // toks
    half = own // 2
    place = jnp.stack([lax.axis_index(name) for name in ("sect", "tok", "vocab")])

    picked = pl.pallas_call(
        functools.partial(pick_kernel, toks=toks),
        in_specs=[SMEM, VMEM],
        out_specs=VMEM,
        out_shape=jax.ShapeDtypeStruct((sections, feats, own), jnp.bfloat16),
        compiler_params=params(),
    )(place, hidden.T)
    spread = pl.pallas_call(
        arrange_kernel,
        in_specs=[VMEM],
        out_specs=VMEM,
        out_shape=jax.ShapeDtypeStruct((vocabs // 2, feats, rows), jnp.bfloat16),
        compiler_params=params(),
        cost_estimate=cost(20 * 10**9, 64 * 10**6),
    )(exchange(picked, "sect"))
    groups = [list(range(core, vocabs, 2)) for core in range(2)]
    other_core = [(i, i ^ 1) for i in range(vocabs)]
    mine = exchange(spread, "vocab", axis_index_groups=groups)
    other = lax.ppermute(mine, "vocab", other_core)

    shift = functools.partial(along_z, planes=planes, vocabs=vocabs)
    edge_first, edge_second = partial_logits(place, mine, other, head_weight, 0, [half, half])
    far_first = shift(edge_first, -1)
    far_second = shift(edge_second, 1)
    near_first, near_second, next_first, next_second, kept = partial_logits(
        place, mine, other, head_weight, own, [half, half, half, half, own]
    )
    near_first = shift(near_first, -1)
    near_second = shift(near_second, 1)

    add = pl.pallas_call(
        add_kernel,
        in_specs=[VMEM, VMEM],
        out_specs=VMEM,
        out_shape=jax.ShapeDtypeStruct(next_first.shape, jnp.float32),
        compiler_params=params(),
    )
    next_first = shift(add(next_first, far_first), -1)
    next_second = shift(add(next_second, far_second), 1)

    teacher_logits, _ = lax.optimization_barrier((teacher_logits, kept))
    teacher = teacher_logits.reshape(sections, vocabs, width).transpose(1, 0, 2)
    teacher = exchange(teacher, "vocab").transpose(1, 0, 2).reshape(own, width)

    logits, teacher, stats = pl.pallas_call(
        stats_kernel,
        in_specs=[SMEM, SMEM] + [VMEM] * 6,
        out_specs=[VMEM] * 3,
        out_shape=[
            jax.ShapeDtypeStruct((own, width), jnp.float32),
            jax.ShapeDtypeStruct((own, width), jnp.bfloat16),
            jax.ShapeDtypeStruct((vocabs, 8, own), jnp.float32),
        ],
        compiler_params=params(),
    )(place, pairing, kept, next_first, near_second, near_first, next_second, teacher)
    first, second, diverge = pl.pallas_call(
        grads_kernel,
        in_specs=[SMEM] + [VMEM] * 3,
        out_specs=[VMEM] * 3,
        out_shape=[
            jax.ShapeDtypeStruct((half, width), jnp.bfloat16),
            jax.ShapeDtypeStruct((half, width), jnp.bfloat16),
            jax.ShapeDtypeStruct((1, own), jnp.float32),
        ],
        scratch_shapes=[pltpu.VMEM((own, 128), jnp.float32)],
        compiler_params=params(),
    )(place, logits, teacher, exchange(stats, "vocab"))

    one = shift(first, 1)
    two = shift(second, -1)
    three = shift(second, 1)
    four = shift(first, -1)
    far_one = shift(one, 1)
    far_two = shift(two, -1)
    near_pieces = [three, four, one, two, first, second]
    near = hidden_grads(place, head_weight, near_pieces, vocabs // 2, rows)
    keep, send = hidden_grads(
        place, head_weight, [far_one, far_two], vocabs // 2, rows, near
    )
    other = lax.ppermute(send, "vocab", other_core)
    parts = exchange(keep + other, "vocab", axis_index_groups=groups)

    regrouped = pl.pallas_call(
        regroup_kernel,
        in_specs=[SMEM, VMEM, VMEM],
        out_specs=VMEM,
        out_shape=jax.ShapeDtypeStruct((sections, feats + 8, own), jnp.float32),
        compiler_params=params(),
    )(place, parts, diverge)
    grads, div = pl.pallas_call(
        functools.partial(return_kernel, toks=toks),
        in_specs=[SMEM, VMEM],
        out_specs=[VMEM, VMEM],
        out_shape=[
            jax.ShapeDtypeStruct((feats, rows), jnp.float32),
            jax.ShapeDtypeStruct((1, own), jnp.float32),
        ],
        compiler_params=params(),
    )(place, exchange(regrouped, "sect"))
    return grads.T, div.reshape(own)


def solution(mesh):
    placed = (
        P("sect", ("tok", "vocab")),
        P("tok", "vocab"),
        P(("sect", "tok", "vocab"), None),
        P(),
    )
    return jax.shard_map(
        shards,
        mesh=mesh,
        in_specs=placed,
        out_specs=(P("sect", ("tok", "vocab")), P(("sect", "tok"))),
        check_vma=False,
    )
```

```python
import functools

import jax
import jax.numpy as jnp
from jax import lax
from jax.experimental import pallas as pl
from jax.experimental.pallas import tpu as pltpu
from jax.sharding import PartitionSpec as P

loss_scale = 16.0
VMEM_BYTES = 24 * 1024 * 1024
VMEM = pl.BlockSpec(memory_space=pltpu.VMEM)
ANYWHERE = pl.BlockSpec(memory_space=pl.ANY)


def along_z(value, steps, planes, vocabs):
    pairs = []
    for plane in range(planes):
        for device in range(vocabs):
            there = (plane + (-steps if device % 2 else steps)) % planes
            pairs.append((plane * vocabs + device, there * vocabs + device))
    return lax.ppermute(value, ("sect", "tok", "vocab"), pairs)


def halves(core, half, start=0):
    first = pl.multiple_of(start + core * half, half)
    second = pl.multiple_of(start + (1 - core) * half, half)
    return pl.ds(first, half), pl.ds(second, half)


def exchange(value, axis, **groups):
    return lax.all_to_all(value, axis, split_axis=0, concat_axis=0, tiled=True, **groups)


def params():
    return pltpu.CompilerParams(vmem_limit_bytes=VMEM_BYTES)


def cost(flops, bytes_accessed):
    return pl.CostEstimate(flops=flops, bytes_accessed=bytes_accessed, transcendentals=0)


def remainder(value, count):
    return value & (count - 1) if count & (count - 1) == 0 else lax.rem(value, count)


def quotient(value, count):
    if count & (count - 1) == 0:
        return lax.shift_right_logical(value, jnp.int32(count.bit_length() - 1))
    return lax.div(value, count)


def window_block(section, tok, token_section, piece, sections, toks):
    planes = sections * toks
    near = jnp.int32(piece - 2)
    far = jnp.where(token_section < sections // 2, -2, 2)
    plane = remainder(section * toks + tok + (far if piece == 0 else near) + planes, planes)
    return remainder(plane, toks) * sections + quotient(plane, toks)


def window_order(sections):
    low = list(range(sections // 2))
    high = list(range(sections // 2, sections))
    order = [(0, s) for s in low + high]
    order += [(1, s) for s in high] + [(3, s) for s in low]
    order += [(1, s) for s in low] + [(3, s) for s in high]
    return order + [(2, s) for s in low + high]


def pick_kernel(hidden_ref, picked_ref, *, toks):
    sections, _, own = picked_ref.shape
    rows = hidden_ref.shape[1]
    unit = own // 4
    section, tok = lax.axis_index("sect"), lax.axis_index("tok")
    lane = lax.broadcasted_iota(jnp.int32, (rows, own), 1)
    row = lax.broadcasted_iota(jnp.int32, (rows, own), 0)
    for k in range(sections):
        source = lane
        for piece in range(4):
            block = window_block(jnp.int32(k), tok, section, piece, sections, toks)
            source = jnp.where(
                (lane >= piece * unit) & (lane < (piece + 1) * unit),
                (block - piece) * unit + lane,
                source,
            )
        pick = jnp.where(row == source, 1.0, 0.0).astype(jnp.bfloat16)
        picked_ref[k] = jnp.dot(
            hidden_ref[...], pick, preferred_element_type=jnp.float32
        ).astype(jnp.bfloat16)


def arrange_kernel(got_ref, spread_ref):
    sections, _, own = got_ref.shape
    rows = spread_ref.shape[2]
    unit = own // 4
    lane = lax.broadcasted_iota(jnp.int32, (own, rows), 1)
    row = lax.broadcasted_iota(jnp.int32, (own, rows), 0)
    total = None
    for s in range(sections):
        source = jnp.full((own, rows), -1, jnp.int32)
        for place, (piece, token_section) in enumerate(window_order(sections)):
            if token_section == s:
                source = jnp.where(
                    (lane >= place * unit) & (lane < (place + 1) * unit),
                    lane + (piece - place) * unit,
                    source,
                )
        move = jnp.where(row == source, 1.0, 0.0).astype(jnp.bfloat16)
        part = jnp.dot(got_ref[s], move, preferred_element_type=jnp.float32)
        total = part if total is None else total + part
    window = total.astype(jnp.bfloat16)
    for k in range(spread_ref.shape[0]):
        spread_ref[k] = window


def logits_kernel(first, mine_ref, other_ref, w_ref, *refs):
    *outs, both, flipped = refs

    @pl.when(pl.program_id(0) == 0)
    def _():
        core = remainder(lax.axis_index("vocab"), 2)

        @pl.when(core == 0)
        def _():
            both[:, 0] = mine_ref[:, :, first : first + both.shape[3]]
            both[:, 1] = other_ref[:, :, first : first + both.shape[3]]

        @pl.when(core != 0)
        def _():
            both[:, 0] = other_ref[:, :, first : first + both.shape[3]]
            both[:, 1] = mine_ref[:, :, first : first + both.shape[3]]

        turned = both[...].reshape(w_ref.shape[0], flipped.shape[0]).T
        start = 0
        for one in outs[0 : len(outs) // 2 * 2 : 2]:
            half = one.shape[0]
            low, high = halves(core, half, start)
            flipped[low] = turned[start : start + half]
            flipped[high] = turned[start + half : start + 2 * half]
            start += 2 * half
        if len(outs) % 2:
            flipped[start:] = turned[start:]

    result = jnp.dot(flipped[...], w_ref[...], preferred_element_type=jnp.float32)
    start = 0
    for out in outs:
        out[...] = result[start : start + out.shape[0]]
        start += out.shape[0]


def partial_logits(mine, other, head_weight, first, sizes):
    feats, width = head_weight.shape
    tile = 512
    count = sum(sizes)
    pairs, unit, _ = mine.shape
    return pl.pallas_call(
        functools.partial(logits_kernel, first),
        grid=(width // tile,),
        in_specs=[VMEM, VMEM, pl.BlockSpec((feats, tile), lambda i: (0, i))],
        out_specs=[pl.BlockSpec((size, tile), lambda i: (0, i)) for size in sizes],
        out_shape=[jax.ShapeDtypeStruct((size, width), jnp.float32) for size in sizes],
        scratch_shapes=[
            pltpu.VMEM((pairs, 2, unit, count), jnp.bfloat16),
            pltpu.VMEM((count, feats), jnp.bfloat16),
        ],
        compiler_params=params(),
        cost_estimate=cost(
            2 * count * feats * width, feats * width * 2 + count * (feats * 2 + width * 4)
        ),
    )(mine, other, head_weight)


def add_kernel(mine_ref, far_ref, out_ref):
    out_ref[...] = mine_ref[...] + far_ref[...]


def stats_kernel(
    pairing_ref,
    own_ref,
    next_first,
    near_second,
    near_first,
    next_second,
    teacher_ref,
    logits_ref,
    sorted_ref,
    stats_ref,
):
    half = next_first.shape[0]
    one, two = halves(remainder(lax.axis_index("vocab"), 2), half)
    logits_ref[one] = own_ref[one] + next_first[...] + near_second[...]
    logits_ref[two] = own_ref[two] + near_first[...] + next_second[...]
    sections = pairing_ref.shape[0]
    unit = own_ref.shape[0] // sections
    row = lax.broadcasted_iota(jnp.int32, pairing_ref.shape, 0)
    lane = lax.broadcasted_iota(jnp.int32, pairing_ref.shape, 1)
    here = jnp.where(row == lax.axis_index("sect"), pairing_ref[...], 0)
    paired = [
        jnp.sum(jnp.where(lane == k, here, 0), axis=(0, 1), keepdims=True) for k in range(sections)
    ]
    blocks = [
        teacher_ref[k * unit : (k + 1) * unit].astype(jnp.float32) for k in range(sections)
    ]
    for s in range(sections):
        block = blocks[0]
        for k in range(1, sections):
            block = jnp.where(paired[k] == s, blocks[k], block)
        sorted_ref[s * unit : (s + 1) * unit] = block.astype(jnp.bfloat16)
    logits = logits_ref[...]
    teacher = sorted_ref[...].astype(jnp.float32)
    top_s = jnp.max(logits, axis=1, keepdims=True)
    top_t = jnp.max(teacher, axis=1, keepdims=True)
    sum_s = jnp.sum(jnp.exp(logits - top_s), axis=1, keepdims=True)
    exp_t = jnp.exp(teacher - top_t)
    sum_t = jnp.sum(exp_t, axis=1, keepdims=True)
    cross = jnp.sum(exp_t * (teacher - logits), axis=1, keepdims=True)
    own = logits.shape[0]
    lane = lax.broadcasted_iota(jnp.int32, (own, 128), 1)
    packed = jnp.zeros((own, 128), jnp.float32)
    for place, column in enumerate((top_s, top_t, sum_s, sum_t, cross)):
        packed = jnp.where(lane == place, column, packed)
    rows = packed.T[:8]
    for k in range(stats_ref.shape[0]):
        stats_ref[k] = rows


def grads_kernel(
    logits_ref, teacher_ref, stats_ref, first_ref, second_ref, div_ref, columns
):
    stats = stats_ref[...]
    top = jnp.max(stats, axis=0)
    scale = jnp.exp(stats[:, :2] - top[None, :2])
    top_s, top_t = top[0:1], top[1:2]
    total_s = jnp.sum(stats[:, 2] * scale[:, 0], axis=0, keepdims=True)
    total_t = jnp.sum(stats[:, 3] * scale[:, 1], axis=0, keepdims=True)
    cross = jnp.sum(stats[:, 4] * scale[:, 1], axis=0, keepdims=True)
    div_ref[...] = cross / total_t - top_t - jnp.log(total_t) + top_s + jnp.log(total_s)
    own = logits_ref.shape[0]
    half = own // 2
    row = lax.broadcasted_iota(jnp.int32, (128, own), 0)
    packed = jnp.zeros((128, own), jnp.float32)
    for place, values in enumerate((top_s, top_t, loss_scale / total_s, loss_scale / total_t)):
        packed = jnp.where(row == place, values, packed)
    columns[...] = packed.T
    places = halves(remainder(lax.axis_index("vocab"), 2), half)
    for place, out_ref in zip(places, (first_ref, second_ref)):
        values = columns[place]
        out_ref[...] = (
            jnp.exp(logits_ref[place] - values[:, 0:1]) * values[:, 2:3]
            - jnp.exp(teacher_ref[place].astype(jnp.float32) - values[:, 1:2]) * values[:, 3:4]
        ).astype(jnp.bfloat16)


def hidden_kernel(earlier, w_ref, *refs):
    *pieces, keep_ref, send_ref, window = refs
    pieces = pieces[: len(pieces) - earlier]

    @pl.when(pl.program_id(0) == 0)
    def _():
        start = 0
        for one, two in zip(pieces[0::2], pieces[1::2]):
            half = one.shape[0]
            low, high = halves(remainder(lax.axis_index("vocab"), 2), half, start)
            window[low] = one[...]
            window[high] = two[...]
            start += 2 * half

    pairs, feats, rows = keep_ref.shape
    result = lax.dot_general(
        w_ref[...], window[...], (((1,), (1,)), ((), ())), preferred_element_type=jnp.float32
    ).reshape(pairs, 2, feats, rows)
    core = remainder(lax.axis_index("vocab"), 2)

    @pl.when(core == 0)
    def _():
        keep_ref[...] = result[:, 0]
        send_ref[...] = result[:, 1]

    @pl.when(core != 0)
    def _():
        keep_ref[...] = result[:, 1]
        send_ref[...] = result[:, 0]


def hidden_grads(head_weight, pieces, pairs, total, earlier=()):
    feats, width = head_weight.shape
    rows = sum(piece.shape[0] for piece in pieces)
    index = (total - rows) // rows if earlier else 0
    steps = 2
    shape = jax.ShapeDtypeStruct((pairs, feats // (2 * pairs), total), jnp.float32)
    block = pl.BlockSpec((pairs // steps, shape.shape[1], rows), lambda i: (i, 0, index))
    inputs = 1 + len(pieces)
    return pl.pallas_call(
        functools.partial(hidden_kernel, len(earlier)),
        grid=(steps,),
        in_specs=[pl.BlockSpec((feats // steps, width), lambda i: (i, 0))]
        + [VMEM] * len(pieces)
        + [ANYWHERE] * len(earlier),
        out_specs=[block, block],
        out_shape=[shape, shape],
        scratch_shapes=[pltpu.VMEM((rows, width), jnp.bfloat16)],
        input_output_aliases={inputs + k: k for k in range(len(earlier))},
        compiler_params=params(),
        cost_estimate=cost(
            2 * rows * feats * width, feats * width * 2 + rows * width * 2 + rows * feats * 4
        ),
    )(head_weight, *pieces, *earlier)


def regroup_kernel(parts_ref, div_ref, out_ref):
    sections, height, own = out_ref.shape
    _, feats, _ = parts_ref.shape
    unit = own // 4
    summed = jnp.sum(parts_ref[...], axis=0)
    lane = lax.broadcasted_iota(jnp.int32, (feats, own), 1)
    order = window_order(sections)
    order = order[sections:] + order[:sections]
    for s in range(sections):
        out = jnp.zeros((feats, own), jnp.float32)
        for piece in range(4):
            start = order.index((piece, s)) * unit
            whole = start // own * own
            turned = pltpu.roll(
                summed[:, whole : whole + own], (piece * unit - start + whole) % own, 1
            )
            out = jnp.where((lane >= piece * unit) & (lane < (piece + 1) * unit), turned, out)
        out_ref[s, :feats] = out
    section = lax.axis_index("sect")
    values = jnp.broadcast_to(div_ref[...], (height - feats, own))
    small = lane[: height - feats]
    for s in range(sections):
        out = jnp.zeros_like(values)
        for mine in range(sections):
            turned = pltpu.roll(values, (mine - s) * unit % own, 1)
            inside = (small >= mine * unit) & (small < (mine + 1) * unit)
            out = jnp.where(inside & (section == mine), turned, out)
        out_ref[s, feats:] = out


def return_kernel(got_ref, grads_ref, div_ref, *, toks):
    sections, _, own = got_ref.shape
    unit = own // 4
    feats, rows = grads_ref.shape
    lane = lax.broadcasted_iota(jnp.int32, (feats, own), 1)
    outs = [jnp.zeros((feats, own), jnp.float32) for _ in range(rows // own)]
    for sender in range(sections):
        values = got_ref[sender, :feats]
        for piece in range(4):
            block = window_block(
                jnp.int32(sender), lax.axis_index("tok"), lax.axis_index("sect"), piece, sections, toks
            )
            begin = remainder(block, 4) * unit
            turned = pltpu.roll(values, remainder(begin - piece * unit + own, own), 1)
            first = lane - quotient(block, 4) * own - begin
            for index in range(len(outs)):
                inside = (first >= -index * own) & (first < unit - index * own)
                outs[index] = jnp.where(inside, turned, outs[index])
    for index, out in enumerate(outs):
        grads_ref[:, index * own : (index + 1) * own] = out
    div_ref[...] = jnp.sum(got_ref[:, feats : feats + 1, :], axis=0)


def shards(hidden, head_weight, teacher_logits, pairing):
    sections = lax.axis_size("sect")
    toks = lax.axis_size("tok")
    vocabs = lax.axis_size("vocab")
    planes = sections * toks
    width = head_weight.shape[1]
    rows, feats = hidden.shape
    own = rows // toks
    half = own // 2

    picked = pl.pallas_call(
        functools.partial(pick_kernel, toks=toks),
        in_specs=[VMEM],
        out_specs=VMEM,
        out_shape=jax.ShapeDtypeStruct((sections, feats, own), jnp.bfloat16),
        compiler_params=params(),
    )(hidden.T)
    spread = pl.pallas_call(
        arrange_kernel,
        in_specs=[VMEM],
        out_specs=VMEM,
        out_shape=jax.ShapeDtypeStruct((vocabs // 2, feats, rows), jnp.bfloat16),
        compiler_params=params(),
        cost_estimate=cost(20 * 10**9, 64 * 10**6),
    )(exchange(picked, "sect"))
    groups = [list(range(core, vocabs, 2)) for core in range(2)]
    other_core = [(i, i ^ 1) for i in range(vocabs)]
    mine = exchange(spread, "vocab", axis_index_groups=groups)
    other = lax.ppermute(mine, "vocab", other_core)

    shift = functools.partial(along_z, planes=planes, vocabs=vocabs)
    edge_first, edge_second = partial_logits(mine, other, head_weight, 0, [half, half])
    far_first = shift(edge_first, -1)
    far_second = shift(edge_second, 1)
    near_first, near_second, next_first, next_second, kept = partial_logits(
        mine, other, head_weight, own, [half, half, half, half, own]
    )
    near_first = shift(near_first, -1)
    near_second = shift(near_second, 1)

    add = pl.pallas_call(
        add_kernel,
        in_specs=[VMEM, VMEM],
        out_specs=VMEM,
        out_shape=jax.ShapeDtypeStruct(next_first.shape, jnp.float32),
        compiler_params=params(),
    )
    next_first = shift(add(next_first, far_first), -1)
    next_second = shift(add(next_second, far_second), 1)

    teacher_logits, _ = lax.optimization_barrier((teacher_logits, kept))
    teacher = teacher_logits.reshape(sections, vocabs, width).transpose(1, 0, 2)
    teacher = exchange(teacher, "vocab").transpose(1, 0, 2).reshape(own, width)

    logits, teacher, stats = pl.pallas_call(
        stats_kernel,
        in_specs=[VMEM] * 7,
        out_specs=[VMEM] * 3,
        out_shape=[
            jax.ShapeDtypeStruct((own, width), jnp.float32),
            jax.ShapeDtypeStruct((own, width), jnp.bfloat16),
            jax.ShapeDtypeStruct((vocabs, 8, own), jnp.float32),
        ],
        compiler_params=params(),
    )(pairing, kept, next_first, near_second, near_first, next_second, teacher)
    first, second, diverge = pl.pallas_call(
        grads_kernel,
        in_specs=[VMEM] * 3,
        out_specs=[VMEM] * 3,
        out_shape=[
            jax.ShapeDtypeStruct((half, width), jnp.bfloat16),
            jax.ShapeDtypeStruct((half, width), jnp.bfloat16),
            jax.ShapeDtypeStruct((1, own), jnp.float32),
        ],
        scratch_shapes=[pltpu.VMEM((own, 128), jnp.float32)],
        compiler_params=params(),
    )(logits, teacher, exchange(stats, "vocab"))

    one = shift(first, 1)
    two = shift(second, -1)
    three = shift(second, 1)
    four = shift(first, -1)
    far_one = shift(one, 1)
    far_two = shift(two, -1)
    near_pieces = [three, four, one, two, first, second]
    near = hidden_grads(head_weight, near_pieces, vocabs // 2, rows)
    keep, send = hidden_grads(
        head_weight, [far_one, far_two], vocabs // 2, rows, near
    )
    other = lax.ppermute(send, "vocab", other_core)
    parts = exchange(keep + other, "vocab", axis_index_groups=groups)

    regrouped = pl.pallas_call(
        regroup_kernel,
        in_specs=[VMEM, VMEM],
        out_specs=VMEM,
        out_shape=jax.ShapeDtypeStruct((sections, feats + 8, own), jnp.float32),
        compiler_params=params(),
    )(parts, diverge)
    grads, div = pl.pallas_call(
        functools.partial(return_kernel, toks=toks),
        in_specs=[VMEM],
        out_specs=[VMEM, VMEM],
        out_shape=[
            jax.ShapeDtypeStruct((feats, rows), jnp.float32),
            jax.ShapeDtypeStruct((1, own), jnp.float32),
        ],
        compiler_params=params(),
    )(exchange(regrouped, "sect"))
    return grads.T, div.reshape(own)


def solution(mesh):
    placed = (
        P("sect", ("tok", "vocab")),
        P("tok", "vocab"),
        P(("sect", "tok", "vocab"), None),
        P(),
    )
    return jax.shard_map(
        shards,
        mesh=mesh,
        in_specs=placed,
        out_specs=(P("sect", ("tok", "vocab")), P(("sect", "tok"))),
        check_vma=False,
    )
```

```python
import functools

import jax
import jax.numpy as jnp
from jax import lax
from jax.experimental import pallas as pl
from jax.experimental.pallas import tpu as pltpu
from jax.sharding import PartitionSpec as P

loss_scale = 16.0
VMEM_BYTES = 24 * 1024 * 1024
VMEM = pl.BlockSpec(memory_space=pltpu.VMEM)
ANYWHERE = pl.BlockSpec(memory_space=pl.ANY)


def along_z(value, steps, planes, vocabs):
    pairs = []
    for plane in range(planes):
        for device in range(vocabs):
            there = (plane + (-steps if device % 2 else steps)) % planes
            pairs.append((plane * vocabs + device, there * vocabs + device))
    return lax.ppermute(value, ("sect", "tok", "vocab"), pairs)


def halves(core, half, start=0):
    first = pl.multiple_of(start + core * half, half)
    second = pl.multiple_of(start + (1 - core) * half, half)
    return pl.ds(first, half), pl.ds(second, half)


def exchange(value, axis, **groups):
    return lax.all_to_all(value, axis, split_axis=0, concat_axis=0, tiled=True, **groups)


def params():
    return pltpu.CompilerParams(vmem_limit_bytes=VMEM_BYTES)


def cost(flops, bytes_accessed):
    return pl.CostEstimate(flops=flops, bytes_accessed=bytes_accessed, transcendentals=0)


def remainder(value, count):
    return value & (count - 1) if count & (count - 1) == 0 else lax.rem(value, count)


def quotient(value, count):
    if count & (count - 1) == 0:
        return lax.shift_right_logical(value, jnp.int32(count.bit_length() - 1))
    return lax.div(value, count)


def window_block(section, tok, token_section, piece, sections, toks):
    planes = sections * toks
    near = jnp.int32(piece - 2)
    far = jnp.where(token_section < sections // 2, -2, 2)
    plane = remainder(section * toks + tok + (far if piece == 0 else near) + planes, planes)
    return remainder(plane, toks) * sections + quotient(plane, toks)


def window_order(sections):
    low = list(range(sections // 2))
    high = list(range(sections // 2, sections))
    order = [(0, s) for s in low + high]
    order += [(1, s) for s in high] + [(3, s) for s in low]
    order += [(1, s) for s in low] + [(3, s) for s in high]
    return order + [(2, s) for s in low + high]


def pick_kernel(hidden_ref, picked_ref, *, toks):
    sections, _, own = picked_ref.shape
    rows = hidden_ref.shape[1]
    unit = own // 4
    section, tok = lax.axis_index("sect"), lax.axis_index("tok")
    lane = lax.broadcasted_iota(jnp.int32, (rows, own), 1)
    row = lax.broadcasted_iota(jnp.int32, (rows, own), 0)
    for k in range(sections):
        source = lane
        for piece in range(4):
            block = window_block(jnp.int32(k), tok, section, piece, sections, toks)
            source = jnp.where(
                (lane >= piece * unit) & (lane < (piece + 1) * unit),
                (block - piece) * unit + lane,
                source,
            )
        pick = jnp.where(row == source, 1.0, 0.0).astype(jnp.bfloat16)
        picked_ref[k] = jnp.dot(
            hidden_ref[...], pick, preferred_element_type=jnp.float32
        ).astype(jnp.bfloat16)


def arrange_kernel(got_ref, spread_ref):
    sections, _, own = got_ref.shape
    rows = spread_ref.shape[2]
    unit = own // 4
    lane = lax.broadcasted_iota(jnp.int32, (own, rows), 1)
    row = lax.broadcasted_iota(jnp.int32, (own, rows), 0)
    total = None
    for s in range(sections):
        source = jnp.full((own, rows), -1, jnp.int32)
        for place, (piece, token_section) in enumerate(window_order(sections)):
            if token_section == s:
                source = jnp.where(
                    (lane >= place * unit) & (lane < (place + 1) * unit),
                    lane + (piece - place) * unit,
                    source,
                )
        move = jnp.where(row == source, 1.0, 0.0).astype(jnp.bfloat16)
        part = jnp.dot(got_ref[s], move, preferred_element_type=jnp.float32)
        total = part if total is None else total + part
    window = total.astype(jnp.bfloat16)
    for k in range(spread_ref.shape[0]):
        spread_ref[k] = window


def logits_kernel(first, mine_ref, other_ref, w_ref, *refs):
    *outs, both, flipped = refs

    @pl.when(pl.program_id(0) == 0)
    def _():
        core = remainder(lax.axis_index("vocab"), 2)

        @pl.when(core == 0)
        def _():
            both[:, 0] = mine_ref[:, :, first : first + both.shape[3]]
            both[:, 1] = other_ref[:, :, first : first + both.shape[3]]

        @pl.when(core != 0)
        def _():
            both[:, 0] = other_ref[:, :, first : first + both.shape[3]]
            both[:, 1] = mine_ref[:, :, first : first + both.shape[3]]

        turned = both[...].reshape(w_ref.shape[0], flipped.shape[0]).T
        start = 0
        for one in outs[0 : len(outs) // 2 * 2 : 2]:
            half = one.shape[0]
            low, high = halves(core, half, start)
            flipped[low] = turned[start : start + half]
            flipped[high] = turned[start + half : start + 2 * half]
            start += 2 * half
        if len(outs) % 2:
            flipped[start:] = turned[start:]

    result = jnp.dot(flipped[...], w_ref[...], preferred_element_type=jnp.float32)
    start = 0
    for out in outs:
        out[...] = result[start : start + out.shape[0]]
        start += out.shape[0]


def partial_logits(mine, other, head_weight, first, sizes):
    feats, width = head_weight.shape
    tile = 512
    count = sum(sizes)
    pairs, unit, _ = mine.shape
    return pl.pallas_call(
        functools.partial(logits_kernel, first),
        grid=(width // tile,),
        in_specs=[VMEM, VMEM, pl.BlockSpec((feats, tile), lambda i: (0, i))],
        out_specs=[pl.BlockSpec((size, tile), lambda i: (0, i)) for size in sizes],
        out_shape=[jax.ShapeDtypeStruct((size, width), jnp.float32) for size in sizes],
        scratch_shapes=[
            pltpu.VMEM((pairs, 2, unit, count), jnp.bfloat16),
            pltpu.VMEM((count, feats), jnp.bfloat16),
        ],
        compiler_params=params(),
        cost_estimate=cost(
            2 * count * feats * width, feats * width * 2 + count * (feats * 2 + width * 4)
        ),
    )(mine, other, head_weight)


def edge_kernel(swapped, x_ref, w_ref, *refs):
    *earlier, first_ref, second_ref, flipped = refs
    half, width = first_ref.shape
    pairs, unit, _ = x_ref.shape
    core = remainder(lax.axis_index("vocab"), 2)
    turned = x_ref[:, :, : 2 * half].reshape(pairs * unit, 2 * half).T
    low, high = halves(core, half)
    flipped[low] = turned[:half]
    flipped[high] = turned[half:]
    chosen = remainder(core + swapped, 2)
    tile = 512

    @pl.loop(0, width // tile)
    def _(step):
        place = pl.ds(pl.multiple_of(step * tile, tile), tile)
        weights = w_ref[:, chosen, :, place].reshape(pairs * unit, tile)
        result = jnp.dot(flipped[...], weights, preferred_element_type=jnp.float32)
        first, second = result[:half], result[half:]
        if earlier:
            first, second = first + earlier[0][:, place], second + earlier[1][:, place]
        first_ref[:, place] = first
        second_ref[:, place] = second


def edge_logits(hidden, head, own, earlier=()):
    pairs, _, unit, width = head.shape
    shape = jax.ShapeDtypeStruct((own // 2, width), jnp.float32)
    return pl.pallas_call(
        functools.partial(edge_kernel, 1 if earlier else 0),
        in_specs=[VMEM] * (2 + len(earlier)),
        out_specs=[VMEM, VMEM],
        out_shape=[shape, shape],
        scratch_shapes=[pltpu.VMEM((own, pairs * unit), jnp.bfloat16)],
        compiler_params=params(),
        cost_estimate=cost(
            2 * own * pairs * unit * width, pairs * unit * width * 2 + own * width * 4
        ),
    )(hidden, head, *earlier)


def add_kernel(mine_ref, far_ref, out_ref):
    out_ref[...] = mine_ref[...] + far_ref[...]


def stats_kernel(
    pairing_ref,
    own_ref,
    next_first,
    near_second,
    near_first,
    next_second,
    teacher_ref,
    logits_ref,
    sorted_ref,
    stats_ref,
):
    half = next_first.shape[0]
    one, two = halves(remainder(lax.axis_index("vocab"), 2), half)
    logits_ref[one] = own_ref[one] + next_first[...] + near_second[...]
    logits_ref[two] = own_ref[two] + near_first[...] + next_second[...]
    sections = pairing_ref.shape[0]
    unit = own_ref.shape[0] // sections
    row = lax.broadcasted_iota(jnp.int32, pairing_ref.shape, 0)
    lane = lax.broadcasted_iota(jnp.int32, pairing_ref.shape, 1)
    here = jnp.where(row == lax.axis_index("sect"), pairing_ref[...], 0)
    paired = [
        jnp.sum(jnp.where(lane == k, here, 0), axis=(0, 1), keepdims=True) for k in range(sections)
    ]
    blocks = [
        teacher_ref[k * unit : (k + 1) * unit].astype(jnp.float32) for k in range(sections)
    ]
    for s in range(sections):
        block = blocks[0]
        for k in range(1, sections):
            block = jnp.where(paired[k] == s, blocks[k], block)
        sorted_ref[s * unit : (s + 1) * unit] = block.astype(jnp.bfloat16)
    logits = logits_ref[...]
    teacher = sorted_ref[...].astype(jnp.float32)
    top_s = jnp.max(logits, axis=1, keepdims=True)
    top_t = jnp.max(teacher, axis=1, keepdims=True)
    sum_s = jnp.sum(jnp.exp(logits - top_s), axis=1, keepdims=True)
    exp_t = jnp.exp(teacher - top_t)
    sum_t = jnp.sum(exp_t, axis=1, keepdims=True)
    cross = jnp.sum(exp_t * (teacher - logits), axis=1, keepdims=True)
    own = logits.shape[0]
    lane = lax.broadcasted_iota(jnp.int32, (own, 128), 1)
    packed = jnp.zeros((own, 128), jnp.float32)
    for place, column in enumerate((top_s, top_t, sum_s, sum_t, cross)):
        packed = jnp.where(lane == place, column, packed)
    rows = packed.T[:8]
    for k in range(stats_ref.shape[0]):
        stats_ref[k] = rows


def grads_kernel(
    logits_ref, teacher_ref, stats_ref, first_ref, second_ref, div_ref, columns
):
    stats = stats_ref[...]
    top = jnp.max(stats, axis=0)
    scale = jnp.exp(stats[:, :2] - top[None, :2])
    top_s, top_t = top[0:1], top[1:2]
    total_s = jnp.sum(stats[:, 2] * scale[:, 0], axis=0, keepdims=True)
    total_t = jnp.sum(stats[:, 3] * scale[:, 1], axis=0, keepdims=True)
    cross = jnp.sum(stats[:, 4] * scale[:, 1], axis=0, keepdims=True)
    div_ref[...] = cross / total_t - top_t - jnp.log(total_t) + top_s + jnp.log(total_s)
    own = logits_ref.shape[0]
    half = own // 2
    row = lax.broadcasted_iota(jnp.int32, (128, own), 0)
    packed = jnp.zeros((128, own), jnp.float32)
    for place, values in enumerate((top_s, top_t, loss_scale / total_s, loss_scale / total_t)):
        packed = jnp.where(row == place, values, packed)
    columns[...] = packed.T
    places = halves(remainder(lax.axis_index("vocab"), 2), half)
    for place, out_ref in zip(places, (first_ref, second_ref)):
        values = columns[place]
        out_ref[...] = (
            jnp.exp(logits_ref[place] - values[:, 0:1]) * values[:, 2:3]
            - jnp.exp(teacher_ref[place].astype(jnp.float32) - values[:, 1:2]) * values[:, 3:4]
        ).astype(jnp.bfloat16)


def hidden_kernel(earlier, w_ref, *refs):
    *pieces, keep_ref, send_ref, window = refs
    pieces = pieces[: len(pieces) - earlier]

    @pl.when(pl.program_id(0) == 0)
    def _():
        start = 0
        for one, two in zip(pieces[0::2], pieces[1::2]):
            half = one.shape[0]
            low, high = halves(remainder(lax.axis_index("vocab"), 2), half, start)
            window[low] = one[...]
            window[high] = two[...]
            start += 2 * half

    pairs, feats, rows = keep_ref.shape
    result = lax.dot_general(
        w_ref[...], window[...], (((1,), (1,)), ((), ())), preferred_element_type=jnp.float32
    ).reshape(pairs, 2, feats, rows)
    core = remainder(lax.axis_index("vocab"), 2)

    @pl.when(core == 0)
    def _():
        keep_ref[...] = result[:, 0]
        send_ref[...] = result[:, 1]

    @pl.when(core != 0)
    def _():
        keep_ref[...] = result[:, 1]
        send_ref[...] = result[:, 0]


def hidden_grads(head_weight, pieces, pairs, total, earlier=()):
    feats, width = head_weight.shape
    rows = sum(piece.shape[0] for piece in pieces)
    index = (total - rows) // rows if earlier else 0
    steps = 2
    shape = jax.ShapeDtypeStruct((pairs, feats // (2 * pairs), total), jnp.float32)
    block = pl.BlockSpec((pairs // steps, shape.shape[1], rows), lambda i: (i, 0, index))
    inputs = 1 + len(pieces)
    return pl.pallas_call(
        functools.partial(hidden_kernel, len(earlier)),
        grid=(steps,),
        in_specs=[pl.BlockSpec((feats // steps, width), lambda i: (i, 0))]
        + [VMEM] * len(pieces)
        + [ANYWHERE] * len(earlier),
        out_specs=[block, block],
        out_shape=[shape, shape],
        scratch_shapes=[pltpu.VMEM((rows, width), jnp.bfloat16)],
        input_output_aliases={inputs + k: k for k in range(len(earlier))},
        compiler_params=params(),
        cost_estimate=cost(
            2 * rows * feats * width, feats * width * 2 + rows * width * 2 + rows * feats * 4
        ),
    )(head_weight, *pieces, *earlier)


def regroup_kernel(parts_ref, div_ref, out_ref):
    sections, height, own = out_ref.shape
    _, feats, _ = parts_ref.shape
    unit = own // 4
    summed = jnp.sum(parts_ref[...], axis=0)
    lane = lax.broadcasted_iota(jnp.int32, (feats, own), 1)
    order = window_order(sections)
    order = order[sections:] + order[:sections]
    for s in range(sections):
        out = jnp.zeros((feats, own), jnp.float32)
        for piece in range(4):
            start = order.index((piece, s)) * unit
            whole = start // own * own
            turned = pltpu.roll(
                summed[:, whole : whole + own], (piece * unit - start + whole) % own, 1
            )
            out = jnp.where((lane >= piece * unit) & (lane < (piece + 1) * unit), turned, out)
        out_ref[s, :feats] = out
    section = lax.axis_index("sect")
    values = jnp.broadcast_to(div_ref[...], (height - feats, own))
    small = lane[: height - feats]
    for s in range(sections):
        out = jnp.zeros_like(values)
        for mine in range(sections):
            turned = pltpu.roll(values, (mine - s) * unit % own, 1)
            inside = (small >= mine * unit) & (small < (mine + 1) * unit)
            out = jnp.where(inside & (section == mine), turned, out)
        out_ref[s, feats:] = out


def return_kernel(got_ref, grads_ref, div_ref, *, toks):
    sections, _, own = got_ref.shape
    unit = own // 4
    feats, rows = grads_ref.shape
    lane = lax.broadcasted_iota(jnp.int32, (feats, own), 1)
    outs = [jnp.zeros((feats, own), jnp.float32) for _ in range(rows // own)]
    for sender in range(sections):
        values = got_ref[sender, :feats]
        for piece in range(4):
            block = window_block(
                jnp.int32(sender), lax.axis_index("tok"), lax.axis_index("sect"), piece, sections, toks
            )
            begin = remainder(block, 4) * unit
            turned = pltpu.roll(values, remainder(begin - piece * unit + own, own), 1)
            first = lane - quotient(block, 4) * own - begin
            for index in range(len(outs)):
                inside = (first >= -index * own) & (first < unit - index * own)
                outs[index] = jnp.where(inside, turned, outs[index])
    for index, out in enumerate(outs):
        grads_ref[:, index * own : (index + 1) * own] = out
    div_ref[...] = jnp.sum(got_ref[:, feats : feats + 1, :], axis=0)


def shards(hidden, head_weight, teacher_logits, pairing):
    sections = lax.axis_size("sect")
    toks = lax.axis_size("tok")
    vocabs = lax.axis_size("vocab")
    planes = sections * toks
    width = head_weight.shape[1]
    rows, feats = hidden.shape
    own = rows // toks
    half = own // 2

    picked = pl.pallas_call(
        functools.partial(pick_kernel, toks=toks),
        in_specs=[VMEM],
        out_specs=VMEM,
        out_shape=jax.ShapeDtypeStruct((sections, feats, own), jnp.bfloat16),
        compiler_params=params(),
    )(hidden.T)
    spread = pl.pallas_call(
        arrange_kernel,
        in_specs=[VMEM],
        out_specs=VMEM,
        out_shape=jax.ShapeDtypeStruct((vocabs // 2, feats, rows), jnp.bfloat16),
        compiler_params=params(),
        cost_estimate=cost(20 * 10**9, 64 * 10**6),
    )(exchange(picked, "sect"))
    groups = [list(range(core, vocabs, 2)) for core in range(2)]
    other_core = [(i, i ^ 1) for i in range(vocabs)]
    mine = exchange(spread, "vocab", axis_index_groups=groups)
    other = lax.ppermute(mine, "vocab", other_core)

    shift = functools.partial(along_z, planes=planes, vocabs=vocabs)
    paired_head = head_weight.reshape(vocabs // 2, 2, feats, width)
    edges = edge_logits(mine, paired_head, own)
    edge_first, edge_second = edge_logits(other, paired_head, own, edges)
    far_first = shift(edge_first, -1)
    far_second = shift(edge_second, 1)
    near_first, near_second, next_first, next_second, kept = partial_logits(
        mine, other, head_weight, own, [half, half, half, half, own]
    )
    near_first = shift(near_first, -1)
    near_second = shift(near_second, 1)

    add = pl.pallas_call(
        add_kernel,
        in_specs=[VMEM, VMEM],
        out_specs=VMEM,
        out_shape=jax.ShapeDtypeStruct(next_first.shape, jnp.float32),
        compiler_params=params(),
    )
    next_first = shift(add(next_first, far_first), -1)
    next_second = shift(add(next_second, far_second), 1)

    teacher_logits, _ = lax.optimization_barrier((teacher_logits, kept))
    teacher = teacher_logits.reshape(sections, vocabs, width).transpose(1, 0, 2)
    teacher = exchange(teacher, "vocab").transpose(1, 0, 2).reshape(own, width)

    logits, teacher, stats = pl.pallas_call(
        stats_kernel,
        in_specs=[VMEM] * 7,
        out_specs=[VMEM] * 3,
        out_shape=[
            jax.ShapeDtypeStruct((own, width), jnp.float32),
            jax.ShapeDtypeStruct((own, width), jnp.bfloat16),
            jax.ShapeDtypeStruct((vocabs, 8, own), jnp.float32),
        ],
        compiler_params=params(),
    )(pairing, kept, next_first, near_second, near_first, next_second, teacher)
    first, second, diverge = pl.pallas_call(
        grads_kernel,
        in_specs=[VMEM] * 3,
        out_specs=[VMEM] * 3,
        out_shape=[
            jax.ShapeDtypeStruct((half, width), jnp.bfloat16),
            jax.ShapeDtypeStruct((half, width), jnp.bfloat16),
            jax.ShapeDtypeStruct((1, own), jnp.float32),
        ],
        scratch_shapes=[pltpu.VMEM((own, 128), jnp.float32)],
        compiler_params=params(),
    )(logits, teacher, exchange(stats, "vocab"))

    one = shift(first, 1)
    two = shift(second, -1)
    three = shift(second, 1)
    four = shift(first, -1)
    far_one = shift(one, 1)
    far_two = shift(two, -1)
    near_pieces = [three, four, one, two, first, second]
    near = hidden_grads(head_weight, near_pieces, vocabs // 2, rows)
    keep, send = hidden_grads(
        head_weight, [far_one, far_two], vocabs // 2, rows, near
    )
    other = lax.ppermute(send, "vocab", other_core)
    parts = exchange(keep + other, "vocab", axis_index_groups=groups)

    regrouped = pl.pallas_call(
        regroup_kernel,
        in_specs=[VMEM, VMEM],
        out_specs=VMEM,
        out_shape=jax.ShapeDtypeStruct((sections, feats + 8, own), jnp.float32),
        compiler_params=params(),
    )(parts, diverge)
    grads, div = pl.pallas_call(
        functools.partial(return_kernel, toks=toks),
        in_specs=[VMEM],
        out_specs=[VMEM, VMEM],
        out_shape=[
            jax.ShapeDtypeStruct((feats, rows), jnp.float32),
            jax.ShapeDtypeStruct((1, own), jnp.float32),
        ],
        compiler_params=params(),
    )(exchange(regrouped, "sect"))
    return grads.T, div.reshape(own)


def solution(mesh):
    placed = (
        P("sect", ("tok", "vocab")),
        P("tok", "vocab"),
        P(("sect", "tok", "vocab"), None),
        P(),
    )
    return jax.shard_map(
        shards,
        mesh=mesh,
        in_specs=placed,
        out_specs=(P("sect", ("tok", "vocab")), P(("sect", "tok"))),
        check_vma=False,
    )
```

```python
import functools

import jax
import jax.numpy as jnp
from jax import lax
from jax.experimental import pallas as pl
from jax.experimental.pallas import tpu as pltpu
from jax.sharding import PartitionSpec as P

loss_scale = 16.0
VMEM_BYTES = 24 * 1024 * 1024
VMEM = pl.BlockSpec(memory_space=pltpu.VMEM)
ANYWHERE = pl.BlockSpec(memory_space=pl.ANY)


def along_z(value, steps, planes, vocabs):
    pairs = []
    for plane in range(planes):
        for device in range(vocabs):
            there = (plane + (-steps if device % 2 else steps)) % planes
            pairs.append((plane * vocabs + device, there * vocabs + device))
    return lax.ppermute(value, ("sect", "tok", "vocab"), pairs)


def halves(core, half, start=0):
    first = pl.multiple_of(start + core * half, half)
    second = pl.multiple_of(start + (1 - core) * half, half)
    return pl.ds(first, half), pl.ds(second, half)


def exchange(value, axis, **groups):
    return lax.all_to_all(value, axis, split_axis=0, concat_axis=0, tiled=True, **groups)


def params():
    return pltpu.CompilerParams(vmem_limit_bytes=VMEM_BYTES)


def cost(flops, bytes_accessed):
    return pl.CostEstimate(flops=flops, bytes_accessed=bytes_accessed, transcendentals=0)


def remainder(value, count):
    return value & (count - 1) if count & (count - 1) == 0 else lax.rem(value, count)


def quotient(value, count):
    if count & (count - 1) == 0:
        return lax.shift_right_logical(value, jnp.int32(count.bit_length() - 1))
    return lax.div(value, count)


def window_block(section, tok, token_section, piece, sections, toks):
    planes = sections * toks
    near = jnp.int32(piece - 2)
    far = jnp.where(token_section < sections // 2, -2, 2)
    plane = remainder(section * toks + tok + (far if piece == 0 else near) + planes, planes)
    return remainder(plane, toks) * sections + quotient(plane, toks)


def window_order(sections):
    low = list(range(sections // 2))
    high = list(range(sections // 2, sections))
    order = [(0, s) for s in low + high]
    order += [(1, s) for s in high] + [(3, s) for s in low]
    order += [(1, s) for s in low] + [(3, s) for s in high]
    return order + [(2, s) for s in low + high]


def pick_kernel(hidden_ref, picked_ref, *, toks):
    sections, _, own = picked_ref.shape
    rows = hidden_ref.shape[1]
    unit = own // 4
    section, tok = lax.axis_index("sect"), lax.axis_index("tok")
    lane = lax.broadcasted_iota(jnp.int32, (rows, own), 1)
    row = lax.broadcasted_iota(jnp.int32, (rows, own), 0)
    for k in range(sections):
        source = lane
        for piece in range(4):
            block = window_block(jnp.int32(k), tok, section, piece, sections, toks)
            source = jnp.where(
                (lane >= piece * unit) & (lane < (piece + 1) * unit),
                (block - piece) * unit + lane,
                source,
            )
        pick = jnp.where(row == source, 1.0, 0.0).astype(jnp.bfloat16)
        picked_ref[k] = jnp.dot(
            hidden_ref[...], pick, preferred_element_type=jnp.float32
        ).astype(jnp.bfloat16)


def arrange_kernel(got_ref, spread_ref):
    sections, _, own = got_ref.shape
    rows = spread_ref.shape[2]
    unit = own // 4
    lane = lax.broadcasted_iota(jnp.int32, (own, rows), 1)
    row = lax.broadcasted_iota(jnp.int32, (own, rows), 0)
    total = None
    for s in range(sections):
        source = jnp.full((own, rows), -1, jnp.int32)
        for place, (piece, token_section) in enumerate(window_order(sections)):
            if token_section == s:
                source = jnp.where(
                    (lane >= place * unit) & (lane < (place + 1) * unit),
                    lane + (piece - place) * unit,
                    source,
                )
        move = jnp.where(row == source, 1.0, 0.0).astype(jnp.bfloat16)
        part = jnp.dot(got_ref[s], move, preferred_element_type=jnp.float32)
        total = part if total is None else total + part
    window = total.astype(jnp.bfloat16)
    for k in range(spread_ref.shape[0]):
        spread_ref[k] = window


def logits_kernel(first, mine_ref, other_ref, w_ref, *refs):
    *outs, both, flipped = refs

    @pl.when(pl.program_id(0) == 0)
    def _():
        core = remainder(lax.axis_index("vocab"), 2)

        @pl.when(core == 0)
        def _():
            both[:, 0] = mine_ref[:, :, first : first + both.shape[3]]
            both[:, 1] = other_ref[:, :, first : first + both.shape[3]]

        @pl.when(core != 0)
        def _():
            both[:, 0] = other_ref[:, :, first : first + both.shape[3]]
            both[:, 1] = mine_ref[:, :, first : first + both.shape[3]]

        turned = both[...].reshape(w_ref.shape[0], flipped.shape[0]).T
        start = 0
        for one in outs[0 : len(outs) // 2 * 2 : 2]:
            half = one.shape[0]
            low, high = halves(core, half, start)
            flipped[low] = turned[start : start + half]
            flipped[high] = turned[start + half : start + 2 * half]
            start += 2 * half
        if len(outs) % 2:
            flipped[start:] = turned[start:]

    result = jnp.dot(flipped[...], w_ref[...], preferred_element_type=jnp.float32)
    start = 0
    for out in outs:
        out[...] = result[start : start + out.shape[0]]
        start += out.shape[0]


def partial_logits(mine, other, head_weight, first, sizes):
    feats, width = head_weight.shape
    tile = 1024
    count = sum(sizes)
    pairs, unit, _ = mine.shape
    return pl.pallas_call(
        functools.partial(logits_kernel, first),
        grid=(width // tile,),
        in_specs=[VMEM, VMEM, pl.BlockSpec((feats, tile), lambda i: (0, i))],
        out_specs=[pl.BlockSpec((size, tile), lambda i: (0, i)) for size in sizes],
        out_shape=[jax.ShapeDtypeStruct((size, width), jnp.float32) for size in sizes],
        scratch_shapes=[
            pltpu.VMEM((pairs, 2, unit, count), jnp.bfloat16),
            pltpu.VMEM((count, feats), jnp.bfloat16),
        ],
        compiler_params=params(),
        cost_estimate=cost(
            2 * count * feats * width, feats * width * 2 + count * (feats * 2 + width * 4)
        ),
    )(mine, other, head_weight)


def edge_kernel(swapped, x_ref, w_ref, *refs):
    *earlier, first_ref, second_ref, flipped = refs
    half, width = first_ref.shape
    pairs, unit, _ = x_ref.shape
    core = remainder(lax.axis_index("vocab"), 2)
    turned = x_ref[:, :, : 2 * half].reshape(pairs * unit, 2 * half).T
    low, high = halves(core, half)
    flipped[low] = turned[:half]
    flipped[high] = turned[half:]
    chosen = remainder(core + swapped, 2)
    tile = 512

    @pl.loop(0, width // tile)
    def _(step):
        place = pl.ds(pl.multiple_of(step * tile, tile), tile)
        weights = w_ref[:, chosen, :, place].reshape(pairs * unit, tile)
        result = jnp.dot(flipped[...], weights, preferred_element_type=jnp.float32)
        first, second = result[:half], result[half:]
        if earlier:
            first, second = first + earlier[0][:, place], second + earlier[1][:, place]
        first_ref[:, place] = first
        second_ref[:, place] = second


def edge_logits(hidden, head, own, earlier=()):
    pairs, _, unit, width = head.shape
    shape = jax.ShapeDtypeStruct((own // 2, width), jnp.float32)
    return pl.pallas_call(
        functools.partial(edge_kernel, 1 if earlier else 0),
        in_specs=[VMEM] * (2 + len(earlier)),
        out_specs=[VMEM, VMEM],
        out_shape=[shape, shape],
        scratch_shapes=[pltpu.VMEM((own, pairs * unit), jnp.bfloat16)],
        compiler_params=params(),
        cost_estimate=cost(
            2 * own * pairs * unit * width, pairs * unit * width * 2 + own * width * 4
        ),
    )(hidden, head, *earlier)


def add_kernel(mine_ref, far_ref, out_ref):
    out_ref[...] = mine_ref[...] + far_ref[...]


def stats_kernel(
    pairing_ref,
    own_ref,
    next_first,
    near_second,
    near_first,
    next_second,
    teacher_ref,
    logits_ref,
    sorted_ref,
    stats_ref,
):
    half = next_first.shape[0]
    one, two = halves(remainder(lax.axis_index("vocab"), 2), half)
    logits_ref[one] = own_ref[one] + next_first[...] + near_second[...]
    logits_ref[two] = own_ref[two] + near_first[...] + next_second[...]
    sections = pairing_ref.shape[0]
    unit = own_ref.shape[0] // sections
    row = lax.broadcasted_iota(jnp.int32, pairing_ref.shape, 0)
    lane = lax.broadcasted_iota(jnp.int32, pairing_ref.shape, 1)
    here = jnp.where(row == lax.axis_index("sect"), pairing_ref[...], 0)
    paired = [
        jnp.sum(jnp.where(lane == k, here, 0), axis=(0, 1), keepdims=True) for k in range(sections)
    ]
    blocks = [
        teacher_ref[k * unit : (k + 1) * unit].astype(jnp.float32) for k in range(sections)
    ]
    for s in range(sections):
        block = blocks[0]
        for k in range(1, sections):
            block = jnp.where(paired[k] == s, blocks[k], block)
        sorted_ref[s * unit : (s + 1) * unit] = block.astype(jnp.bfloat16)
    logits = logits_ref[...]
    teacher = sorted_ref[...].astype(jnp.float32)
    top_s = jnp.max(logits, axis=1, keepdims=True)
    top_t = jnp.max(teacher, axis=1, keepdims=True)
    sum_s = jnp.sum(jnp.exp(logits - top_s), axis=1, keepdims=True)
    exp_t = jnp.exp(teacher - top_t)
    sum_t = jnp.sum(exp_t, axis=1, keepdims=True)
    cross = jnp.sum(exp_t * (teacher - logits), axis=1, keepdims=True)
    own = logits.shape[0]
    lane = lax.broadcasted_iota(jnp.int32, (own, 128), 1)
    packed = jnp.zeros((own, 128), jnp.float32)
    for place, column in enumerate((top_s, top_t, sum_s, sum_t, cross)):
        packed = jnp.where(lane == place, column, packed)
    rows = packed.T[:8]
    for k in range(stats_ref.shape[0]):
        stats_ref[k] = rows


def grads_kernel(
    logits_ref, teacher_ref, stats_ref, first_ref, second_ref, div_ref, columns
):
    stats = stats_ref[...]
    top = jnp.max(stats, axis=0)
    scale = jnp.exp(stats[:, :2] - top[None, :2])
    top_s, top_t = top[0:1], top[1:2]
    total_s = jnp.sum(stats[:, 2] * scale[:, 0], axis=0, keepdims=True)
    total_t = jnp.sum(stats[:, 3] * scale[:, 1], axis=0, keepdims=True)
    cross = jnp.sum(stats[:, 4] * scale[:, 1], axis=0, keepdims=True)
    div_ref[...] = cross / total_t - top_t - jnp.log(total_t) + top_s + jnp.log(total_s)
    own = logits_ref.shape[0]
    half = own // 2
    row = lax.broadcasted_iota(jnp.int32, (128, own), 0)
    packed = jnp.zeros((128, own), jnp.float32)
    for place, values in enumerate((top_s, top_t, loss_scale / total_s, loss_scale / total_t)):
        packed = jnp.where(row == place, values, packed)
    columns[...] = packed.T
    places = halves(remainder(lax.axis_index("vocab"), 2), half)
    for place, out_ref in zip(places, (first_ref, second_ref)):
        values = columns[place]
        out_ref[...] = (
            jnp.exp(logits_ref[place] - values[:, 0:1]) * values[:, 2:3]
            - jnp.exp(teacher_ref[place].astype(jnp.float32) - values[:, 1:2]) * values[:, 3:4]
        ).astype(jnp.bfloat16)


def hidden_kernel(earlier, w_ref, *refs):
    *pieces, keep_ref, send_ref, window = refs
    pieces = pieces[: len(pieces) - earlier]

    @pl.when(pl.program_id(0) == 0)
    def _():
        start = 0
        for one, two in zip(pieces[0::2], pieces[1::2]):
            half = one.shape[0]
            low, high = halves(remainder(lax.axis_index("vocab"), 2), half, start)
            window[low] = one[...]
            window[high] = two[...]
            start += 2 * half

    pairs, feats, rows = keep_ref.shape
    result = lax.dot_general(
        w_ref[...], window[...], (((1,), (1,)), ((), ())), preferred_element_type=jnp.float32
    ).reshape(pairs, 2, feats, rows)
    core = remainder(lax.axis_index("vocab"), 2)

    @pl.when(core == 0)
    def _():
        keep_ref[...] = result[:, 0]
        send_ref[...] = result[:, 1]

    @pl.when(core != 0)
    def _():
        keep_ref[...] = result[:, 1]
        send_ref[...] = result[:, 0]


def hidden_grads(head_weight, pieces, pairs, total, earlier=()):
    feats, width = head_weight.shape
    rows = sum(piece.shape[0] for piece in pieces)
    index = (total - rows) // rows if earlier else 0
    steps = 1
    shape = jax.ShapeDtypeStruct((pairs, feats // (2 * pairs), total), jnp.float32)
    block = pl.BlockSpec((pairs // steps, shape.shape[1], rows), lambda i: (i, 0, index))
    inputs = 1 + len(pieces)
    return pl.pallas_call(
        functools.partial(hidden_kernel, len(earlier)),
        grid=(steps,),
        in_specs=[pl.BlockSpec((feats // steps, width), lambda i: (i, 0))]
        + [VMEM] * len(pieces)
        + [ANYWHERE] * len(earlier),
        out_specs=[block, block],
        out_shape=[shape, shape],
        scratch_shapes=[pltpu.VMEM((rows, width), jnp.bfloat16)],
        input_output_aliases={inputs + k: k for k in range(len(earlier))},
        compiler_params=params(),
        cost_estimate=cost(
            2 * rows * feats * width, feats * width * 2 + rows * width * 2 + rows * feats * 4
        ),
    )(head_weight, *pieces, *earlier)


def regroup_kernel(parts_ref, div_ref, out_ref):
    sections, height, own = out_ref.shape
    _, feats, _ = parts_ref.shape
    unit = own // 4
    summed = jnp.sum(parts_ref[...], axis=0)
    lane = lax.broadcasted_iota(jnp.int32, (feats, own), 1)
    order = window_order(sections)
    order = order[sections:] + order[:sections]
    for s in range(sections):
        out = jnp.zeros((feats, own), jnp.float32)
        for piece in range(4):
            start = order.index((piece, s)) * unit
            whole = start // own * own
            turned = pltpu.roll(
                summed[:, whole : whole + own], (piece * unit - start + whole) % own, 1
            )
            out = jnp.where((lane >= piece * unit) & (lane < (piece + 1) * unit), turned, out)
        out_ref[s, :feats] = out
    section = lax.axis_index("sect")
    values = jnp.broadcast_to(div_ref[...], (height - feats, own))
    small = lane[: height - feats]
    for s in range(sections):
        out = jnp.zeros_like(values)
        for mine in range(sections):
            turned = pltpu.roll(values, (mine - s) * unit % own, 1)
            inside = (small >= mine * unit) & (small < (mine + 1) * unit)
            out = jnp.where(inside & (section == mine), turned, out)
        out_ref[s, feats:] = out


def return_kernel(got_ref, grads_ref, div_ref, *, toks):
    sections, _, own = got_ref.shape
    unit = own // 4
    feats, rows = grads_ref.shape
    lane = lax.broadcasted_iota(jnp.int32, (feats, own), 1)
    outs = [jnp.zeros((feats, own), jnp.float32) for _ in range(rows // own)]
    for sender in range(sections):
        values = got_ref[sender, :feats]
        for piece in range(4):
            block = window_block(
                jnp.int32(sender), lax.axis_index("tok"), lax.axis_index("sect"), piece, sections, toks
            )
            begin = remainder(block, 4) * unit
            turned = pltpu.roll(values, remainder(begin - piece * unit + own, own), 1)
            first = lane - quotient(block, 4) * own - begin
            for index in range(len(outs)):
                inside = (first >= -index * own) & (first < unit - index * own)
                outs[index] = jnp.where(inside, turned, outs[index])
    for index, out in enumerate(outs):
        grads_ref[:, index * own : (index + 1) * own] = out
    div_ref[...] = jnp.sum(got_ref[:, feats : feats + 1, :], axis=0)


def shards(hidden, head_weight, teacher_logits, pairing):
    sections = lax.axis_size("sect")
    toks = lax.axis_size("tok")
    vocabs = lax.axis_size("vocab")
    planes = sections * toks
    width = head_weight.shape[1]
    rows, feats = hidden.shape
    own = rows // toks
    half = own // 2

    picked = pl.pallas_call(
        functools.partial(pick_kernel, toks=toks),
        in_specs=[VMEM],
        out_specs=VMEM,
        out_shape=jax.ShapeDtypeStruct((sections, feats, own), jnp.bfloat16),
        compiler_params=params(),
    )(hidden.T)
    spread = pl.pallas_call(
        arrange_kernel,
        in_specs=[VMEM],
        out_specs=VMEM,
        out_shape=jax.ShapeDtypeStruct((vocabs // 2, feats, rows), jnp.bfloat16),
        compiler_params=params(),
        cost_estimate=cost(20 * 10**9, 64 * 10**6),
    )(exchange(picked, "sect"))
    groups = [list(range(core, vocabs, 2)) for core in range(2)]
    other_core = [(i, i ^ 1) for i in range(vocabs)]
    mine = exchange(spread, "vocab", axis_index_groups=groups)
    other = lax.ppermute(mine, "vocab", other_core)

    shift = functools.partial(along_z, planes=planes, vocabs=vocabs)
    paired_head = head_weight.reshape(vocabs // 2, 2, feats, width)
    edges = edge_logits(mine, paired_head, own)
    edge_first, edge_second = edge_logits(other, paired_head, own, edges)
    far_first = shift(edge_first, -1)
    far_second = shift(edge_second, 1)
    near_first, near_second, next_first, next_second, kept = partial_logits(
        mine, other, head_weight, own, [half, half, half, half, own]
    )
    near_first = shift(near_first, -1)
    near_second = shift(near_second, 1)

    add = pl.pallas_call(
        add_kernel,
        in_specs=[VMEM, VMEM],
        out_specs=VMEM,
        out_shape=jax.ShapeDtypeStruct(next_first.shape, jnp.float32),
        compiler_params=params(),
    )
    next_first = shift(add(next_first, far_first), -1)
    next_second = shift(add(next_second, far_second), 1)

    teacher_logits, _ = lax.optimization_barrier((teacher_logits, kept))
    teacher = teacher_logits.reshape(sections, vocabs, width).transpose(1, 0, 2)
    teacher = exchange(teacher, "vocab").transpose(1, 0, 2).reshape(own, width)

    logits, teacher, stats = pl.pallas_call(
        stats_kernel,
        in_specs=[VMEM] * 7,
        out_specs=[VMEM] * 3,
        out_shape=[
            jax.ShapeDtypeStruct((own, width), jnp.float32),
            jax.ShapeDtypeStruct((own, width), jnp.bfloat16),
            jax.ShapeDtypeStruct((vocabs, 8, own), jnp.float32),
        ],
        compiler_params=params(),
    )(pairing, kept, next_first, near_second, near_first, next_second, teacher)
    first, second, diverge = pl.pallas_call(
        grads_kernel,
        in_specs=[VMEM] * 3,
        out_specs=[VMEM] * 3,
        out_shape=[
            jax.ShapeDtypeStruct((half, width), jnp.bfloat16),
            jax.ShapeDtypeStruct((half, width), jnp.bfloat16),
            jax.ShapeDtypeStruct((1, own), jnp.float32),
        ],
        scratch_shapes=[pltpu.VMEM((own, 128), jnp.float32)],
        compiler_params=params(),
    )(logits, teacher, exchange(stats, "vocab"))

    one = shift(first, 1)
    two = shift(second, -1)
    three = shift(second, 1)
    four = shift(first, -1)
    far_one = shift(one, 1)
    far_two = shift(two, -1)
    near_pieces = [three, four, one, two, first, second]
    near = hidden_grads(head_weight, near_pieces, vocabs // 2, rows)
    keep, send = hidden_grads(
        head_weight, [far_one, far_two], vocabs // 2, rows, near
    )
    other = lax.ppermute(send, "vocab", other_core)
    parts = exchange(keep + other, "vocab", axis_index_groups=groups)

    regrouped = pl.pallas_call(
        regroup_kernel,
        in_specs=[VMEM, VMEM],
        out_specs=VMEM,
        out_shape=jax.ShapeDtypeStruct((sections, feats + 8, own), jnp.float32),
        compiler_params=params(),
    )(parts, diverge)
    grads, div = pl.pallas_call(
        functools.partial(return_kernel, toks=toks),
        in_specs=[VMEM],
        out_specs=[VMEM, VMEM],
        out_shape=[
            jax.ShapeDtypeStruct((feats, rows), jnp.float32),
            jax.ShapeDtypeStruct((1, own), jnp.float32),
        ],
        compiler_params=params(),
    )(exchange(regrouped, "sect"))
    return grads.T, div.reshape(own)


def solution(mesh):
    placed = (
        P("sect", ("tok", "vocab")),
        P("tok", "vocab"),
        P(("sect", "tok", "vocab"), None),
        P(),
    )
    return jax.shard_map(
        shards,
        mesh=mesh,
        in_specs=placed,
        out_specs=(P("sect", ("tok", "vocab")), P(("sect", "tok"))),
        check_vma=False,
    )
```

```python
import functools

import jax
import jax.numpy as jnp
from jax import lax
from jax.experimental import pallas as pl
from jax.experimental.pallas import tpu as pltpu
from jax.sharding import PartitionSpec as P

loss_scale = 16.0
VMEM_BYTES = 24 * 1024 * 1024
VMEM = pl.BlockSpec(memory_space=pltpu.VMEM)
ANYWHERE = pl.BlockSpec(memory_space=pl.ANY)


def along_z(value, steps, planes, vocabs):
    pairs = []
    for plane in range(planes):
        for device in range(vocabs):
            there = (plane + (-steps if device % 2 else steps)) % planes
            pairs.append((plane * vocabs + device, there * vocabs + device))
    return lax.ppermute(value, ("sect", "tok", "vocab"), pairs)


def halves(core, half, start=0):
    first = pl.multiple_of(start + core * half, half)
    second = pl.multiple_of(start + (1 - core) * half, half)
    return pl.ds(first, half), pl.ds(second, half)


def exchange(value, axis, **groups):
    return lax.all_to_all(value, axis, split_axis=0, concat_axis=0, tiled=True, **groups)


def params():
    return pltpu.CompilerParams(vmem_limit_bytes=VMEM_BYTES)


def cost(flops, bytes_accessed):
    return pl.CostEstimate(flops=flops, bytes_accessed=bytes_accessed, transcendentals=0)


def remainder(value, count):
    return value & (count - 1) if count & (count - 1) == 0 else lax.rem(value, count)


def quotient(value, count):
    if count & (count - 1) == 0:
        return lax.shift_right_logical(value, jnp.int32(count.bit_length() - 1))
    return lax.div(value, count)


def window_block(section, tok, token_section, piece, sections, toks):
    planes = sections * toks
    near = jnp.int32(piece - 2)
    far = jnp.where(token_section < sections // 2, -2, 2)
    plane = remainder(section * toks + tok + (far if piece == 0 else near) + planes, planes)
    return remainder(plane, toks) * sections + quotient(plane, toks)


def window_order(sections):
    low = list(range(sections // 2))
    high = list(range(sections // 2, sections))
    order = [(0, s) for s in low + high]
    order += [(1, s) for s in high] + [(3, s) for s in low]
    order += [(1, s) for s in low] + [(3, s) for s in high]
    return order + [(2, s) for s in low + high]


def pick_kernel(hidden_ref, picked_ref, *, toks):
    sections, _, own = picked_ref.shape
    rows = hidden_ref.shape[1]
    unit = own // 4
    section, tok = lax.axis_index("sect"), lax.axis_index("tok")
    lane = lax.broadcasted_iota(jnp.int32, (rows, own), 1)
    row = lax.broadcasted_iota(jnp.int32, (rows, own), 0)
    for k in range(sections):
        source = lane
        for piece in range(4):
            block = window_block(jnp.int32(k), tok, section, piece, sections, toks)
            source = jnp.where(
                (lane >= piece * unit) & (lane < (piece + 1) * unit),
                (block - piece) * unit + lane,
                source,
            )
        pick = jnp.where(row == source, 1.0, 0.0).astype(jnp.bfloat16)
        picked_ref[k] = jnp.dot(
            hidden_ref[...], pick, preferred_element_type=jnp.float32
        ).astype(jnp.bfloat16)


def arrange_kernel(got_ref, spread_ref):
    sections, _, own = got_ref.shape
    rows = spread_ref.shape[2]
    unit = own // 4
    lane = lax.broadcasted_iota(jnp.int32, (own, rows), 1)
    row = lax.broadcasted_iota(jnp.int32, (own, rows), 0)
    total = None
    for s in range(sections):
        source = jnp.full((own, rows), -1, jnp.int32)
        for place, (piece, token_section) in enumerate(window_order(sections)):
            if token_section == s:
                source = jnp.where(
                    (lane >= place * unit) & (lane < (place + 1) * unit),
                    lane + (piece - place) * unit,
                    source,
                )
        move = jnp.where(row == source, 1.0, 0.0).astype(jnp.bfloat16)
        part = jnp.dot(got_ref[s], move, preferred_element_type=jnp.float32)
        total = part if total is None else total + part
    window = total.astype(jnp.bfloat16)
    for k in range(spread_ref.shape[0]):
        spread_ref[k] = window


def logits_kernel(first, mine_ref, other_ref, w_ref, *refs):
    *outs, both, flipped = refs

    @pl.when(pl.program_id(0) == 0)
    def _():
        core = remainder(lax.axis_index("vocab"), 2)

        @pl.when(core == 0)
        def _():
            both[:, 0] = mine_ref[:, :, first : first + both.shape[3]]
            both[:, 1] = other_ref[:, :, first : first + both.shape[3]]

        @pl.when(core != 0)
        def _():
            both[:, 0] = other_ref[:, :, first : first + both.shape[3]]
            both[:, 1] = mine_ref[:, :, first : first + both.shape[3]]

        turned = both[...].reshape(w_ref.shape[0], flipped.shape[0]).T
        start = 0
        for one in outs[0 : len(outs) // 2 * 2 : 2]:
            half = one.shape[0]
            low, high = halves(core, half, start)
            flipped[low] = turned[start : start + half]
            flipped[high] = turned[start + half : start + 2 * half]
            start += 2 * half
        if len(outs) % 2:
            flipped[start:] = turned[start:]

    result = jnp.dot(flipped[...], w_ref[...], preferred_element_type=jnp.float32)
    start = 0
    for out in outs:
        out[...] = result[start : start + out.shape[0]]
        start += out.shape[0]


def partial_logits(mine, other, head_weight, first, sizes):
    feats, width = head_weight.shape
    tile = 1024
    count = sum(sizes)
    pairs, unit, _ = mine.shape
    return pl.pallas_call(
        functools.partial(logits_kernel, first),
        grid=(width // tile,),
        in_specs=[VMEM, VMEM, pl.BlockSpec((feats, tile), lambda i: (0, i))],
        out_specs=[pl.BlockSpec((size, tile), lambda i: (0, i)) for size in sizes],
        out_shape=[jax.ShapeDtypeStruct((size, width), jnp.float32) for size in sizes],
        scratch_shapes=[
            pltpu.VMEM((pairs, 2, unit, count), jnp.bfloat16),
            pltpu.VMEM((count, feats), jnp.bfloat16),
        ],
        compiler_params=params(),
        cost_estimate=cost(
            2 * count * feats * width, feats * width * 2 + count * (feats * 2 + width * 4)
        ),
    )(mine, other, head_weight)


def edge_kernel(swapped, x_ref, w_ref, *refs):
    *earlier, first_ref, second_ref, flipped = refs
    half, width = first_ref.shape
    pairs, unit, _ = x_ref.shape
    core = remainder(lax.axis_index("vocab"), 2)
    turned = x_ref[:, :, : 2 * half].reshape(pairs * unit, 2 * half).T
    low, high = halves(core, half)
    flipped[low] = turned[:half]
    flipped[high] = turned[half:]
    chosen = remainder(core + swapped, 2)
    tile = 1024

    @pl.loop(0, width // tile)
    def _(step):
        place = pl.ds(pl.multiple_of(step * tile, tile), tile)
        weights = w_ref[:, chosen, :, place].reshape(pairs * unit, tile)
        result = jnp.dot(flipped[...], weights, preferred_element_type=jnp.float32)
        first, second = result[:half], result[half:]
        if earlier:
            first, second = first + earlier[0][:, place], second + earlier[1][:, place]
        first_ref[:, place] = first
        second_ref[:, place] = second


def edge_logits(hidden, head, own, earlier=()):
    pairs, _, unit, width = head.shape
    shape = jax.ShapeDtypeStruct((own // 2, width), jnp.float32)
    return pl.pallas_call(
        functools.partial(edge_kernel, 1 if earlier else 0),
        in_specs=[VMEM] * (2 + len(earlier)),
        out_specs=[VMEM, VMEM],
        out_shape=[shape, shape],
        scratch_shapes=[pltpu.VMEM((own, pairs * unit), jnp.bfloat16)],
        compiler_params=params(),
        cost_estimate=cost(
            2 * own * pairs * unit * width, pairs * unit * width * 2 + own * width * 4
        ),
    )(hidden, head, *earlier)


def add_kernel(mine_ref, far_ref, out_ref):
    out_ref[...] = mine_ref[...] + far_ref[...]


def stats_kernel(
    pairing_ref,
    own_ref,
    next_first,
    near_second,
    near_first,
    next_second,
    teacher_ref,
    logits_ref,
    sorted_ref,
    stats_ref,
):
    half = next_first.shape[0]
    one, two = halves(remainder(lax.axis_index("vocab"), 2), half)
    logits_ref[one] = own_ref[one] + next_first[...] + near_second[...]
    logits_ref[two] = own_ref[two] + near_first[...] + next_second[...]
    sections = pairing_ref.shape[0]
    unit = own_ref.shape[0] // sections
    row = lax.broadcasted_iota(jnp.int32, pairing_ref.shape, 0)
    lane = lax.broadcasted_iota(jnp.int32, pairing_ref.shape, 1)
    here = jnp.where(row == lax.axis_index("sect"), pairing_ref[...], 0)
    paired = [
        jnp.sum(jnp.where(lane == k, here, 0), axis=(0, 1), keepdims=True) for k in range(sections)
    ]
    blocks = [
        teacher_ref[k * unit : (k + 1) * unit].astype(jnp.float32) for k in range(sections)
    ]
    for s in range(sections):
        block = blocks[0]
        for k in range(1, sections):
            block = jnp.where(paired[k] == s, blocks[k], block)
        sorted_ref[s * unit : (s + 1) * unit] = block.astype(jnp.bfloat16)
    logits = logits_ref[...]
    teacher = sorted_ref[...].astype(jnp.float32)
    top_s = jnp.max(logits, axis=1, keepdims=True)
    top_t = jnp.max(teacher, axis=1, keepdims=True)
    sum_s = jnp.sum(jnp.exp(logits - top_s), axis=1, keepdims=True)
    exp_t = jnp.exp(teacher - top_t)
    sum_t = jnp.sum(exp_t, axis=1, keepdims=True)
    cross = jnp.sum(exp_t * (teacher - logits), axis=1, keepdims=True)
    own = logits.shape[0]
    lane = lax.broadcasted_iota(jnp.int32, (own, 128), 1)
    packed = jnp.zeros((own, 128), jnp.float32)
    for place, column in enumerate((top_s, top_t, sum_s, sum_t, cross)):
        packed = jnp.where(lane == place, column, packed)
    rows = packed.T[:8]
    for k in range(stats_ref.shape[0]):
        stats_ref[k] = rows


def grads_kernel(
    logits_ref, teacher_ref, stats_ref, first_ref, second_ref, div_ref, columns
):
    stats = stats_ref[...]
    top = jnp.max(stats, axis=0)
    scale = jnp.exp(stats[:, :2] - top[None, :2])
    top_s, top_t = top[0:1], top[1:2]
    total_s = jnp.sum(stats[:, 2] * scale[:, 0], axis=0, keepdims=True)
    total_t = jnp.sum(stats[:, 3] * scale[:, 1], axis=0, keepdims=True)
    cross = jnp.sum(stats[:, 4] * scale[:, 1], axis=0, keepdims=True)
    div_ref[...] = cross / total_t - top_t - jnp.log(total_t) + top_s + jnp.log(total_s)
    own = logits_ref.shape[0]
    half = own // 2
    row = lax.broadcasted_iota(jnp.int32, (128, own), 0)
    packed = jnp.zeros((128, own), jnp.float32)
    for place, values in enumerate((top_s, top_t, loss_scale / total_s, loss_scale / total_t)):
        packed = jnp.where(row == place, values, packed)
    columns[...] = packed.T
    places = halves(remainder(lax.axis_index("vocab"), 2), half)
    for place, out_ref in zip(places, (first_ref, second_ref)):
        values = columns[place]
        out_ref[...] = (
            jnp.exp(logits_ref[place] - values[:, 0:1]) * values[:, 2:3]
            - jnp.exp(teacher_ref[place].astype(jnp.float32) - values[:, 1:2]) * values[:, 3:4]
        ).astype(jnp.bfloat16)


def hidden_kernel(earlier, w_ref, *refs):
    *pieces, keep_ref, send_ref, window = refs
    pieces = pieces[: len(pieces) - earlier]

    @pl.when(pl.program_id(0) == 0)
    def _():
        start = 0
        for one, two in zip(pieces[0::2], pieces[1::2]):
            half = one.shape[0]
            low, high = halves(remainder(lax.axis_index("vocab"), 2), half, start)
            window[low] = one[...]
            window[high] = two[...]
            start += 2 * half

    pairs, feats, rows = keep_ref.shape
    result = lax.dot_general(
        w_ref[...], window[...], (((1,), (1,)), ((), ())), preferred_element_type=jnp.float32
    ).reshape(pairs, 2, feats, rows)
    core = remainder(lax.axis_index("vocab"), 2)

    @pl.when(core == 0)
    def _():
        keep_ref[...] = result[:, 0]
        send_ref[...] = result[:, 1]

    @pl.when(core != 0)
    def _():
        keep_ref[...] = result[:, 1]
        send_ref[...] = result[:, 0]


def hidden_grads(head_weight, pieces, pairs, total, earlier=()):
    feats, width = head_weight.shape
    rows = sum(piece.shape[0] for piece in pieces)
    index = (total - rows) // rows if earlier else 0
    steps = 1
    shape = jax.ShapeDtypeStruct((pairs, feats // (2 * pairs), total), jnp.float32)
    block = pl.BlockSpec((pairs // steps, shape.shape[1], rows), lambda i: (i, 0, index))
    inputs = 1 + len(pieces)
    return pl.pallas_call(
        functools.partial(hidden_kernel, len(earlier)),
        grid=(steps,),
        in_specs=[pl.BlockSpec((feats // steps, width), lambda i: (i, 0))]
        + [VMEM] * len(pieces)
        + [ANYWHERE] * len(earlier),
        out_specs=[block, block],
        out_shape=[shape, shape],
        scratch_shapes=[pltpu.VMEM((rows, width), jnp.bfloat16)],
        input_output_aliases={inputs + k: k for k in range(len(earlier))},
        compiler_params=params(),
        cost_estimate=cost(
            2 * rows * feats * width, feats * width * 2 + rows * width * 2 + rows * feats * 4
        ),
    )(head_weight, *pieces, *earlier)


def regroup_kernel(parts_ref, div_ref, out_ref):
    sections, height, own = out_ref.shape
    _, feats, _ = parts_ref.shape
    unit = own // 4
    summed = jnp.sum(parts_ref[...], axis=0)
    lane = lax.broadcasted_iota(jnp.int32, (feats, own), 1)
    order = window_order(sections)
    order = order[sections:] + order[:sections]
    for s in range(sections):
        out = jnp.zeros((feats, own), jnp.float32)
        for piece in range(4):
            start = order.index((piece, s)) * unit
            whole = start // own * own
            turned = pltpu.roll(
                summed[:, whole : whole + own], (piece * unit - start + whole) % own, 1
            )
            out = jnp.where((lane >= piece * unit) & (lane < (piece + 1) * unit), turned, out)
        out_ref[s, :feats] = out
    section = lax.axis_index("sect")
    values = jnp.broadcast_to(div_ref[...], (height - feats, own))
    small = lane[: height - feats]
    for s in range(sections):
        out = jnp.zeros_like(values)
        for mine in range(sections):
            turned = pltpu.roll(values, (mine - s) * unit % own, 1)
            inside = (small >= mine * unit) & (small < (mine + 1) * unit)
            out = jnp.where(inside & (section == mine), turned, out)
        out_ref[s, feats:] = out


def return_kernel(got_ref, grads_ref, div_ref, *, toks):
    sections, _, own = got_ref.shape
    unit = own // 4
    feats, rows = grads_ref.shape
    lane = lax.broadcasted_iota(jnp.int32, (feats, own), 1)
    outs = [jnp.zeros((feats, own), jnp.float32) for _ in range(rows // own)]
    for sender in range(sections):
        values = got_ref[sender, :feats]
        for piece in range(4):
            block = window_block(
                jnp.int32(sender), lax.axis_index("tok"), lax.axis_index("sect"), piece, sections, toks
            )
            begin = remainder(block, 4) * unit
            turned = pltpu.roll(values, remainder(begin - piece * unit + own, own), 1)
            first = lane - quotient(block, 4) * own - begin
            for index in range(len(outs)):
                inside = (first >= -index * own) & (first < unit - index * own)
                outs[index] = jnp.where(inside, turned, outs[index])
    for index, out in enumerate(outs):
        grads_ref[:, index * own : (index + 1) * own] = out
    div_ref[...] = jnp.sum(got_ref[:, feats : feats + 1, :], axis=0)


def shards(hidden, head_weight, teacher_logits, pairing):
    sections = lax.axis_size("sect")
    toks = lax.axis_size("tok")
    vocabs = lax.axis_size("vocab")
    planes = sections * toks
    width = head_weight.shape[1]
    rows, feats = hidden.shape
    own = rows // toks
    half = own // 2

    picked = pl.pallas_call(
        functools.partial(pick_kernel, toks=toks),
        in_specs=[VMEM],
        out_specs=VMEM,
        out_shape=jax.ShapeDtypeStruct((sections, feats, own), jnp.bfloat16),
        compiler_params=params(),
    )(hidden.T)
    spread = pl.pallas_call(
        arrange_kernel,
        in_specs=[VMEM],
        out_specs=VMEM,
        out_shape=jax.ShapeDtypeStruct((vocabs // 2, feats, rows), jnp.bfloat16),
        compiler_params=params(),
        cost_estimate=cost(20 * 10**9, 64 * 10**6),
    )(exchange(picked, "sect"))
    groups = [list(range(core, vocabs, 2)) for core in range(2)]
    other_core = [(i, i ^ 1) for i in range(vocabs)]
    mine = exchange(spread, "vocab", axis_index_groups=groups)
    other = lax.ppermute(mine, "vocab", other_core)

    shift = functools.partial(along_z, planes=planes, vocabs=vocabs)
    paired_head = head_weight.reshape(vocabs // 2, 2, feats, width)
    edges = edge_logits(mine, paired_head, own)
    edge_first, edge_second = edge_logits(other, paired_head, own, edges)
    far_first = shift(edge_first, -1)
    far_second = shift(edge_second, 1)
    near_first, near_second, next_first, next_second, kept = partial_logits(
        mine, other, head_weight, own, [half, half, half, half, own]
    )
    near_first = shift(near_first, -1)
    near_second = shift(near_second, 1)

    add = pl.pallas_call(
        add_kernel,
        in_specs=[VMEM, VMEM],
        out_specs=VMEM,
        out_shape=jax.ShapeDtypeStruct(next_first.shape, jnp.float32),
        compiler_params=params(),
    )
    next_first = shift(add(next_first, far_first), -1)
    next_second = shift(add(next_second, far_second), 1)

    teacher_logits, _ = lax.optimization_barrier((teacher_logits, kept))
    teacher = teacher_logits.reshape(sections, vocabs, width).transpose(1, 0, 2)
    teacher = exchange(teacher, "vocab").transpose(1, 0, 2).reshape(own, width)

    logits, teacher, stats = pl.pallas_call(
        stats_kernel,
        in_specs=[VMEM] * 7,
        out_specs=[VMEM] * 3,
        out_shape=[
            jax.ShapeDtypeStruct((own, width), jnp.float32),
            jax.ShapeDtypeStruct((own, width), jnp.bfloat16),
            jax.ShapeDtypeStruct((vocabs, 8, own), jnp.float32),
        ],
        compiler_params=params(),
    )(pairing, kept, next_first, near_second, near_first, next_second, teacher)
    first, second, diverge = pl.pallas_call(
        grads_kernel,
        in_specs=[VMEM] * 3,
        out_specs=[VMEM] * 3,
        out_shape=[
            jax.ShapeDtypeStruct((half, width), jnp.bfloat16),
            jax.ShapeDtypeStruct((half, width), jnp.bfloat16),
            jax.ShapeDtypeStruct((1, own), jnp.float32),
        ],
        scratch_shapes=[pltpu.VMEM((own, 128), jnp.float32)],
        compiler_params=params(),
    )(logits, teacher, exchange(stats, "vocab"))

    one = shift(first, 1)
    two = shift(second, -1)
    three = shift(second, 1)
    four = shift(first, -1)
    far_one = shift(one, 1)
    far_two = shift(two, -1)
    near_pieces = [three, four, one, two, first, second]
    near = hidden_grads(head_weight, near_pieces, vocabs // 2, rows)
    keep, send = hidden_grads(
        head_weight, [far_one, far_two], vocabs // 2, rows, near
    )
    other = lax.ppermute(send, "vocab", other_core)
    parts = exchange(keep + other, "vocab", axis_index_groups=groups)

    regrouped = pl.pallas_call(
        regroup_kernel,
        in_specs=[VMEM, VMEM],
        out_specs=VMEM,
        out_shape=jax.ShapeDtypeStruct((sections, feats + 8, own), jnp.float32),
        compiler_params=params(),
    )(parts, diverge)
    grads, div = pl.pallas_call(
        functools.partial(return_kernel, toks=toks),
        in_specs=[VMEM],
        out_specs=[VMEM, VMEM],
        out_shape=[
            jax.ShapeDtypeStruct((feats, rows), jnp.float32),
            jax.ShapeDtypeStruct((1, own), jnp.float32),
        ],
        compiler_params=params(),
    )(exchange(regrouped, "sect"))
    return grads.T, div.reshape(own)


def solution(mesh):
    placed = (
        P("sect", ("tok", "vocab")),
        P("tok", "vocab"),
        P(("sect", "tok", "vocab"), None),
        P(),
    )
    return jax.shard_map(
        shards,
        mesh=mesh,
        in_specs=placed,
        out_specs=(P("sect", ("tok", "vocab")), P(("sect", "tok"))),
        check_vma=False,
    )
```

```python
import functools

import jax
import jax.numpy as jnp
from jax import lax
from jax.experimental import pallas as pl
from jax.experimental.pallas import tpu as pltpu
from jax.sharding import PartitionSpec as P

loss_scale = 16.0
VMEM_BYTES = 24 * 1024 * 1024
VMEM = pl.BlockSpec(memory_space=pltpu.VMEM)
ANYWHERE = pl.BlockSpec(memory_space=pl.ANY)


def along_z(value, steps, planes, vocabs):
    pairs = []
    for plane in range(planes):
        for device in range(vocabs):
            there = (plane + (-steps if device % 2 else steps)) % planes
            pairs.append((plane * vocabs + device, there * vocabs + device))
    return lax.ppermute(value, ("sect", "tok", "vocab"), pairs)


def halves(core, half, start=0):
    first = pl.multiple_of(start + core * half, half)
    second = pl.multiple_of(start + (1 - core) * half, half)
    return pl.ds(first, half), pl.ds(second, half)


def exchange(value, axis, **groups):
    return lax.all_to_all(value, axis, split_axis=0, concat_axis=0, tiled=True, **groups)


def params():
    return pltpu.CompilerParams(vmem_limit_bytes=VMEM_BYTES)


def cost(flops, bytes_accessed):
    return pl.CostEstimate(flops=flops, bytes_accessed=bytes_accessed, transcendentals=0)


def remainder(value, count):
    return value & (count - 1) if count & (count - 1) == 0 else lax.rem(value, count)


def quotient(value, count):
    if count & (count - 1) == 0:
        return lax.shift_right_logical(value, jnp.int32(count.bit_length() - 1))
    return lax.div(value, count)


def window_block(section, tok, token_section, piece, sections, toks):
    planes = sections * toks
    near = jnp.int32(piece - 2)
    far = jnp.where(token_section < sections // 2, -2, 2)
    plane = remainder(section * toks + tok + (far if piece == 0 else near) + planes, planes)
    return remainder(plane, toks) * sections + quotient(plane, toks)


def window_order(sections):
    low = list(range(sections // 2))
    high = list(range(sections // 2, sections))
    order = [(0, s) for s in low + high]
    order += [(1, s) for s in high] + [(3, s) for s in low]
    order += [(1, s) for s in low] + [(3, s) for s in high]
    return order + [(2, s) for s in low + high]


def pick_kernel(hidden_ref, picked_ref, *, toks):
    sections, _, own = picked_ref.shape
    rows = hidden_ref.shape[1]
    unit = own // 4
    section, tok = lax.axis_index("sect"), lax.axis_index("tok")
    lane = lax.broadcasted_iota(jnp.int32, (rows, own), 1)
    row = lax.broadcasted_iota(jnp.int32, (rows, own), 0)
    for k in range(sections):
        source = lane
        for piece in range(4):
            block = window_block(jnp.int32(k), tok, section, piece, sections, toks)
            source = jnp.where(
                (lane >= piece * unit) & (lane < (piece + 1) * unit),
                (block - piece) * unit + lane,
                source,
            )
        pick = jnp.where(row == source, 1.0, 0.0).astype(jnp.bfloat16)
        picked_ref[k] = jnp.dot(
            hidden_ref[...], pick, preferred_element_type=jnp.float32
        ).astype(jnp.bfloat16)


def arrange_kernel(got_ref, spread_ref):
    sections, _, own = got_ref.shape
    rows = spread_ref.shape[2]
    unit = own // 4
    lane = lax.broadcasted_iota(jnp.int32, (own, rows), 1)
    row = lax.broadcasted_iota(jnp.int32, (own, rows), 0)
    total = None
    for s in range(sections):
        source = jnp.full((own, rows), -1, jnp.int32)
        for place, (piece, token_section) in enumerate(window_order(sections)):
            if token_section == s:
                source = jnp.where(
                    (lane >= place * unit) & (lane < (place + 1) * unit),
                    lane + (piece - place) * unit,
                    source,
                )
        move = jnp.where(row == source, 1.0, 0.0).astype(jnp.bfloat16)
        part = jnp.dot(got_ref[s], move, preferred_element_type=jnp.float32)
        total = part if total is None else total + part
    window = total.astype(jnp.bfloat16)
    for k in range(spread_ref.shape[0]):
        spread_ref[k] = window


def logits_kernel(first, mine_ref, other_ref, w_ref, *refs):
    *outs, both, flipped = refs

    @pl.when(pl.program_id(0) == 0)
    def _():
        core = remainder(lax.axis_index("vocab"), 2)

        @pl.when(core == 0)
        def _():
            both[:, 0] = mine_ref[:, :, first : first + both.shape[3]]
            both[:, 1] = other_ref[:, :, first : first + both.shape[3]]

        @pl.when(core != 0)
        def _():
            both[:, 0] = other_ref[:, :, first : first + both.shape[3]]
            both[:, 1] = mine_ref[:, :, first : first + both.shape[3]]

        turned = both[...].reshape(w_ref.shape[0], flipped.shape[0]).T
        start = 0
        for one in outs[0 : len(outs) // 2 * 2 : 2]:
            half = one.shape[0]
            low, high = halves(core, half, start)
            flipped[low] = turned[start : start + half]
            flipped[high] = turned[start + half : start + 2 * half]
            start += 2 * half
        if len(outs) % 2:
            flipped[start:] = turned[start:]

    result = jnp.dot(flipped[...], w_ref[...], preferred_element_type=jnp.float32)
    start = 0
    for out in outs:
        out[...] = result[start : start + out.shape[0]]
        start += out.shape[0]


def partial_logits(mine, other, head_weight, first, sizes):
    feats, width = head_weight.shape
    tile = 1024
    count = sum(sizes)
    pairs, unit, _ = mine.shape
    return pl.pallas_call(
        functools.partial(logits_kernel, first),
        grid=(width // tile,),
        in_specs=[VMEM, VMEM, pl.BlockSpec((feats, tile), lambda i: (0, i))],
        out_specs=[pl.BlockSpec((size, tile), lambda i: (0, i)) for size in sizes],
        out_shape=[jax.ShapeDtypeStruct((size, width), jnp.float32) for size in sizes],
        scratch_shapes=[
            pltpu.VMEM((pairs, 2, unit, count), jnp.bfloat16),
            pltpu.VMEM((count, feats), jnp.bfloat16),
        ],
        compiler_params=params(),
        cost_estimate=cost(
            2 * count * feats * width, feats * width * 2 + count * (feats * 2 + width * 4)
        ),
    )(mine, other, head_weight)


def edge_kernel(swapped, x_ref, w_ref, *refs):
    *earlier, first_ref, second_ref, flipped = refs
    half, width = first_ref.shape
    pairs, unit, _ = x_ref.shape
    core = remainder(lax.axis_index("vocab"), 2)
    turned = x_ref[:, :, : 2 * half].reshape(pairs * unit, 2 * half).T
    low, high = halves(core, half)
    flipped[low] = turned[:half]
    flipped[high] = turned[half:]
    chosen = remainder(core + swapped, 2)
    tile = 2048

    @pl.loop(0, width // tile)
    def _(step):
        place = pl.ds(pl.multiple_of(step * tile, tile), tile)
        weights = w_ref[:, chosen, :, place].reshape(pairs * unit, tile)
        result = jnp.dot(flipped[...], weights, preferred_element_type=jnp.float32)
        first, second = result[:half], result[half:]
        if earlier:
            first, second = first + earlier[0][:, place], second + earlier[1][:, place]
        first_ref[:, place] = first
        second_ref[:, place] = second


def edge_logits(hidden, head, own, earlier=()):
    pairs, _, unit, width = head.shape
    shape = jax.ShapeDtypeStruct((own // 2, width), jnp.float32)
    return pl.pallas_call(
        functools.partial(edge_kernel, 1 if earlier else 0),
        in_specs=[VMEM] * (2 + len(earlier)),
        out_specs=[VMEM, VMEM],
        out_shape=[shape, shape],
        scratch_shapes=[pltpu.VMEM((own, pairs * unit), jnp.bfloat16)],
        compiler_params=params(),
        cost_estimate=cost(
            2 * own * pairs * unit * width, pairs * unit * width * 2 + own * width * 4
        ),
    )(hidden, head, *earlier)


def add_kernel(mine_ref, far_ref, out_ref):
    out_ref[...] = mine_ref[...] + far_ref[...]


def stats_kernel(
    pairing_ref,
    own_ref,
    next_first,
    near_second,
    near_first,
    next_second,
    teacher_ref,
    logits_ref,
    sorted_ref,
    stats_ref,
):
    half = next_first.shape[0]
    one, two = halves(remainder(lax.axis_index("vocab"), 2), half)
    logits_ref[one] = own_ref[one] + next_first[...] + near_second[...]
    logits_ref[two] = own_ref[two] + near_first[...] + next_second[...]
    sections = pairing_ref.shape[0]
    unit = own_ref.shape[0] // sections
    row = lax.broadcasted_iota(jnp.int32, pairing_ref.shape, 0)
    lane = lax.broadcasted_iota(jnp.int32, pairing_ref.shape, 1)
    here = jnp.where(row == lax.axis_index("sect"), pairing_ref[...], 0)
    paired = [
        jnp.sum(jnp.where(lane == k, here, 0), axis=(0, 1), keepdims=True) for k in range(sections)
    ]
    blocks = [
        teacher_ref[k * unit : (k + 1) * unit].astype(jnp.float32) for k in range(sections)
    ]
    for s in range(sections):
        block = blocks[0]
        for k in range(1, sections):
            block = jnp.where(paired[k] == s, blocks[k], block)
        sorted_ref[s * unit : (s + 1) * unit] = block.astype(jnp.bfloat16)
    logits = logits_ref[...]
    teacher = sorted_ref[...].astype(jnp.float32)
    top_s = jnp.max(logits, axis=1, keepdims=True)
    top_t = jnp.max(teacher, axis=1, keepdims=True)
    sum_s = jnp.sum(jnp.exp(logits - top_s), axis=1, keepdims=True)
    exp_t = jnp.exp(teacher - top_t)
    sum_t = jnp.sum(exp_t, axis=1, keepdims=True)
    cross = jnp.sum(exp_t * (teacher - logits), axis=1, keepdims=True)
    own = logits.shape[0]
    lane = lax.broadcasted_iota(jnp.int32, (own, 128), 1)
    packed = jnp.zeros((own, 128), jnp.float32)
    for place, column in enumerate((top_s, top_t, sum_s, sum_t, cross)):
        packed = jnp.where(lane == place, column, packed)
    rows = packed.T[:8]
    for k in range(stats_ref.shape[0]):
        stats_ref[k] = rows


def grads_kernel(
    logits_ref, teacher_ref, stats_ref, first_ref, second_ref, div_ref, columns
):
    stats = stats_ref[...]
    top = jnp.max(stats, axis=0)
    scale = jnp.exp(stats[:, :2] - top[None, :2])
    top_s, top_t = top[0:1], top[1:2]
    total_s = jnp.sum(stats[:, 2] * scale[:, 0], axis=0, keepdims=True)
    total_t = jnp.sum(stats[:, 3] * scale[:, 1], axis=0, keepdims=True)
    cross = jnp.sum(stats[:, 4] * scale[:, 1], axis=0, keepdims=True)
    div_ref[...] = cross / total_t - top_t - jnp.log(total_t) + top_s + jnp.log(total_s)
    own = logits_ref.shape[0]
    half = own // 2
    row = lax.broadcasted_iota(jnp.int32, (128, own), 0)
    packed = jnp.zeros((128, own), jnp.float32)
    for place, values in enumerate((top_s, top_t, loss_scale / total_s, loss_scale / total_t)):
        packed = jnp.where(row == place, values, packed)
    columns[...] = packed.T
    places = halves(remainder(lax.axis_index("vocab"), 2), half)
    for place, out_ref in zip(places, (first_ref, second_ref)):
        values = columns[place]
        out_ref[...] = (
            jnp.exp(logits_ref[place] - values[:, 0:1]) * values[:, 2:3]
            - jnp.exp(teacher_ref[place].astype(jnp.float32) - values[:, 1:2]) * values[:, 3:4]
        ).astype(jnp.bfloat16)


def hidden_kernel(earlier, w_ref, *refs):
    *pieces, keep_ref, send_ref, window = refs
    pieces = pieces[: len(pieces) - earlier]

    @pl.when(pl.program_id(0) == 0)
    def _():
        start = 0
        for one, two in zip(pieces[0::2], pieces[1::2]):
            half = one.shape[0]
            low, high = halves(remainder(lax.axis_index("vocab"), 2), half, start)
            window[low] = one[...]
            window[high] = two[...]
            start += 2 * half

    pairs, feats, rows = keep_ref.shape
    result = lax.dot_general(
        w_ref[...], window[...], (((1,), (1,)), ((), ())), preferred_element_type=jnp.float32
    ).reshape(pairs, 2, feats, rows)
    core = remainder(lax.axis_index("vocab"), 2)

    @pl.when(core == 0)
    def _():
        keep_ref[...] = result[:, 0]
        send_ref[...] = result[:, 1]

    @pl.when(core != 0)
    def _():
        keep_ref[...] = result[:, 1]
        send_ref[...] = result[:, 0]


def hidden_grads(head_weight, pieces, pairs, total, earlier=()):
    feats, width = head_weight.shape
    rows = sum(piece.shape[0] for piece in pieces)
    index = (total - rows) // rows if earlier else 0
    steps = 1
    shape = jax.ShapeDtypeStruct((pairs, feats // (2 * pairs), total), jnp.float32)
    block = pl.BlockSpec((pairs // steps, shape.shape[1], rows), lambda i: (i, 0, index))
    inputs = 1 + len(pieces)
    return pl.pallas_call(
        functools.partial(hidden_kernel, len(earlier)),
        grid=(steps,),
        in_specs=[pl.BlockSpec((feats // steps, width), lambda i: (i, 0))]
        + [VMEM] * len(pieces)
        + [ANYWHERE] * len(earlier),
        out_specs=[block, block],
        out_shape=[shape, shape],
        scratch_shapes=[pltpu.VMEM((rows, width), jnp.bfloat16)],
        input_output_aliases={inputs + k: k for k in range(len(earlier))},
        compiler_params=params(),
        cost_estimate=cost(
            2 * rows * feats * width, feats * width * 2 + rows * width * 2 + rows * feats * 4
        ),
    )(head_weight, *pieces, *earlier)


def regroup_kernel(parts_ref, div_ref, out_ref):
    sections, height, own = out_ref.shape
    _, feats, _ = parts_ref.shape
    unit = own // 4
    summed = jnp.sum(parts_ref[...], axis=0)
    lane = lax.broadcasted_iota(jnp.int32, (feats, own), 1)
    order = window_order(sections)
    order = order[sections:] + order[:sections]
    for s in range(sections):
        out = jnp.zeros((feats, own), jnp.float32)
        for piece in range(4):
            start = order.index((piece, s)) * unit
            whole = start // own * own
            turned = pltpu.roll(
                summed[:, whole : whole + own], (piece * unit - start + whole) % own, 1
            )
            out = jnp.where((lane >= piece * unit) & (lane < (piece + 1) * unit), turned, out)
        out_ref[s, :feats] = out
    section = lax.axis_index("sect")
    values = jnp.broadcast_to(div_ref[...], (height - feats, own))
    small = lane[: height - feats]
    for s in range(sections):
        out = jnp.zeros_like(values)
        for mine in range(sections):
            turned = pltpu.roll(values, (mine - s) * unit % own, 1)
            inside = (small >= mine * unit) & (small < (mine + 1) * unit)
            out = jnp.where(inside & (section == mine), turned, out)
        out_ref[s, feats:] = out


def return_kernel(got_ref, grads_ref, div_ref, *, toks):
    sections, _, own = got_ref.shape
    unit = own // 4
    feats, rows = grads_ref.shape
    lane = lax.broadcasted_iota(jnp.int32, (feats, own), 1)
    outs = [jnp.zeros((feats, own), jnp.float32) for _ in range(rows // own)]
    for sender in range(sections):
        values = got_ref[sender, :feats]
        for piece in range(4):
            block = window_block(
                jnp.int32(sender), lax.axis_index("tok"), lax.axis_index("sect"), piece, sections, toks
            )
            begin = remainder(block, 4) * unit
            turned = pltpu.roll(values, remainder(begin - piece * unit + own, own), 1)
            first = lane - quotient(block, 4) * own - begin
            for index in range(len(outs)):
                inside = (first >= -index * own) & (first < unit - index * own)
                outs[index] = jnp.where(inside, turned, outs[index])
    for index, out in enumerate(outs):
        grads_ref[:, index * own : (index + 1) * own] = out
    div_ref[...] = jnp.sum(got_ref[:, feats : feats + 1, :], axis=0)


def shards(hidden, head_weight, teacher_logits, pairing):
    sections = lax.axis_size("sect")
    toks = lax.axis_size("tok")
    vocabs = lax.axis_size("vocab")
    planes = sections * toks
    width = head_weight.shape[1]
    rows, feats = hidden.shape
    own = rows // toks
    half = own // 2

    picked = pl.pallas_call(
        functools.partial(pick_kernel, toks=toks),
        in_specs=[VMEM],
        out_specs=VMEM,
        out_shape=jax.ShapeDtypeStruct((sections, feats, own), jnp.bfloat16),
        compiler_params=params(),
    )(hidden.T)
    spread = pl.pallas_call(
        arrange_kernel,
        in_specs=[VMEM],
        out_specs=VMEM,
        out_shape=jax.ShapeDtypeStruct((vocabs // 2, feats, rows), jnp.bfloat16),
        compiler_params=params(),
        cost_estimate=cost(20 * 10**9, 64 * 10**6),
    )(exchange(picked, "sect"))
    groups = [list(range(core, vocabs, 2)) for core in range(2)]
    other_core = [(i, i ^ 1) for i in range(vocabs)]
    mine = exchange(spread, "vocab", axis_index_groups=groups)
    other = lax.ppermute(mine, "vocab", other_core)

    shift = functools.partial(along_z, planes=planes, vocabs=vocabs)
    paired_head = head_weight.reshape(vocabs // 2, 2, feats, width)
    edges = edge_logits(mine, paired_head, own)
    edge_first, edge_second = edge_logits(other, paired_head, own, edges)
    far_first = shift(edge_first, -1)
    far_second = shift(edge_second, 1)
    near_first, near_second, next_first, next_second, kept = partial_logits(
        mine, other, head_weight, own, [half, half, half, half, own]
    )
    near_first = shift(near_first, -1)
    near_second = shift(near_second, 1)

    add = pl.pallas_call(
        add_kernel,
        in_specs=[VMEM, VMEM],
        out_specs=VMEM,
        out_shape=jax.ShapeDtypeStruct(next_first.shape, jnp.float32),
        compiler_params=params(),
    )
    next_first = shift(add(next_first, far_first), -1)
    next_second = shift(add(next_second, far_second), 1)

    teacher_logits, _ = lax.optimization_barrier((teacher_logits, kept))
    teacher = teacher_logits.reshape(sections, vocabs, width).transpose(1, 0, 2)
    teacher = exchange(teacher, "vocab").transpose(1, 0, 2).reshape(own, width)

    logits, teacher, stats = pl.pallas_call(
        stats_kernel,
        in_specs=[VMEM] * 7,
        out_specs=[VMEM] * 3,
        out_shape=[
            jax.ShapeDtypeStruct((own, width), jnp.float32),
            jax.ShapeDtypeStruct((own, width), jnp.bfloat16),
            jax.ShapeDtypeStruct((vocabs, 8, own), jnp.float32),
        ],
        compiler_params=params(),
    )(pairing, kept, next_first, near_second, near_first, next_second, teacher)
    first, second, diverge = pl.pallas_call(
        grads_kernel,
        in_specs=[VMEM] * 3,
        out_specs=[VMEM] * 3,
        out_shape=[
            jax.ShapeDtypeStruct((half, width), jnp.bfloat16),
            jax.ShapeDtypeStruct((half, width), jnp.bfloat16),
            jax.ShapeDtypeStruct((1, own), jnp.float32),
        ],
        scratch_shapes=[pltpu.VMEM((own, 128), jnp.float32)],
        compiler_params=params(),
    )(logits, teacher, exchange(stats, "vocab"))

    one = shift(first, 1)
    two = shift(second, -1)
    three = shift(second, 1)
    four = shift(first, -1)
    far_one = shift(one, 1)
    far_two = shift(two, -1)
    near_pieces = [three, four, one, two, first, second]
    near = hidden_grads(head_weight, near_pieces, vocabs // 2, rows)
    keep, send = hidden_grads(
        head_weight, [far_one, far_two], vocabs // 2, rows, near
    )
    other = lax.ppermute(send, "vocab", other_core)
    parts = exchange(keep + other, "vocab", axis_index_groups=groups)

    regrouped = pl.pallas_call(
        regroup_kernel,
        in_specs=[VMEM, VMEM],
        out_specs=VMEM,
        out_shape=jax.ShapeDtypeStruct((sections, feats + 8, own), jnp.float32),
        compiler_params=params(),
    )(parts, diverge)
    grads, div = pl.pallas_call(
        functools.partial(return_kernel, toks=toks),
        in_specs=[VMEM],
        out_specs=[VMEM, VMEM],
        out_shape=[
            jax.ShapeDtypeStruct((feats, rows), jnp.float32),
            jax.ShapeDtypeStruct((1, own), jnp.float32),
        ],
        compiler_params=params(),
    )(exchange(regrouped, "sect"))
    return grads.T, div.reshape(own)


def solution(mesh):
    placed = (
        P("sect", ("tok", "vocab")),
        P("tok", "vocab"),
        P(("sect", "tok", "vocab"), None),
        P(),
    )
    return jax.shard_map(
        shards,
        mesh=mesh,
        in_specs=placed,
        out_specs=(P("sect", ("tok", "vocab")), P(("sect", "tok"))),
        check_vma=False,
    )
```
